128 devices in a mesh: grp: 4 (over y_hi, core), blk: 32 (over y_lo, x, z).
Axes of the slice: x: 4, y: 4 (y_hi: 2, y_lo: 2; y = y_hi * 2 + y_lo), z: 4, core: 2. Of those that a mesh axis runs over, the one named last changes fastest.
Arguments:
- queries: bfloat16 [5376, 2048], P('blk', 'grp'), may hold values from -512 to 512
- key_rows: bfloat16 [5376, 2048], P('blk', 'grp'), may hold values from -8 to 8
- value_rows: bfloat16 [5376, 2048], P('blk', 'grp'), may hold values from -6 to 6
- out_grad: bfloat16 [5376, 2048], P('blk', 'grp'), may hold values from -6 to 6
- enc_lengths: int32 [32], P('blk'), may hold values from 42 to 168, as said below
- dec_lengths: int32 [32], P('blk'), may hold values from 14 to 56, as said below
Outputs:
- query_grad: float32 [5376, 2048], P('blk', 'grp')
- key_grad: float32 [5376, 2048], P('blk', 'grp')
- value_grad: float32 [5376, 2048], P('blk', 'grp')
The draws below stay inside these ranges and needn't reach their ends.
Inputs may be any that keep to these rules, and one draw needn't show every extreme that they name: `enc_lengths`: some encoder block is full. `dec_lengths`: some decoder block is full.
All inputs are finite; a program needn't handle non-finite values.
Results may differ from the reference program's by a relative error of at most 0.0055.
Values may be sent and summed in bfloat16 or wider, within the bound.
No kernel may reach another device: no remote copies, remote signals or barrier semaphores. Data moves between devices by JAX's collectives and lax.ppermute only.
A program may use at most 128 MiB of HBM per device.

```python
import math
import jax
import jax.numpy as jnp
from jax import lax

H = 24
HD = 64
TOK = 168
HG = 8
DTOK = 56
S = 5376
DEC = 1792
N_GRP = 4
N_BLK = 32


def base_field(key):
    return jax.random.normal(jax.random.fold_in(key, 101), (S, N_GRP * (H // 3) * HD), jnp.float32)


def chosen_rows(key):
    return jax.random.randint(jax.random.fold_in(key, 102), (S,), 0, 40) == 0


def copied_field(key, spread):
    normal_rows = base_field(key)
    jitter = jax.random.normal(jax.random.fold_in(key, 103), normal_rows.shape, jnp.float32)
    copies = jnp.roll(chosen_rows(key), 3)
    return jnp.where(copies[:, None], jnp.roll(normal_rows, 3, axis=0) + spread * jitter, normal_rows)


def draw_key_rows(key, part):
    return base_field(key).astype(jnp.bfloat16)


def draw_queries(key, part):
    aligned = copied_field(key, 0.08)
    key = jax.random.fold_in(key, 7)
    return jax.random.normal(key, aligned.shape, jnp.float32).astype(jnp.bfloat16)


def draw_enc_lengths(key, part):
    key = jax.random.fold_in(key, 5)
    lengths = jax.random.randint(key, (N_BLK,), TOK // 4, TOK + 1)
    fullest = jax.random.randint(jax.random.fold_in(key, 1), (), 0, N_BLK)
    return jnp.where(jnp.arange(N_BLK) == fullest, TOK, lengths).astype(jnp.int32)


def draw_dec_lengths(key, part):
    key = jax.random.fold_in(key, 9)
    lengths = jax.random.randint(key, (N_BLK,), DTOK // 4, DTOK + 1)
    fullest = jax.random.randint(jax.random.fold_in(key, 1), (), 0, N_BLK)
    return jnp.where(jnp.arange(N_BLK) == fullest, DTOK, lengths).astype(jnp.int32)


def block_scale(stream_key, dims, shards, low, high):
    factor_of = 1.0
    for dim, shards_of in shards:
        draws = jax.random.uniform(jax.random.fold_in(jax.random.fold_in(stream_key, 6), dim), (shards_of,), jnp.float32, low / len(shards), high / len(shards))
        factor_of = factor_of * jnp.repeat(jnp.exp(draws), dims[dim] // shards_of).reshape((-1,) + (1,) * (len(dims) - 1 - dim))
    return factor_of


def noise(key, dims, width, reach, shards=(), held_as=jnp.bfloat16):
    level = block_scale(key, dims, shards, -0.22, 0.18) if shards else 1.0
    values = jax.random.normal(key, dims, jnp.float32) * width * level
    return jnp.minimum(jnp.maximum(values, -reach), reach).astype(held_as)


def setup_inputs(seed: int = 0) -> dict:
    seeds = jax.random.split(jax.random.key(seed), 7)
    return {
        "queries": draw_queries(jax.random.fold_in(seeds[6], 71), 0),
        "key_rows": draw_key_rows(jax.random.fold_in(seeds[6], 71), 0),
        "value_rows": noise(seeds[2], (S, N_GRP * HG * HD), 1.0, 6.0, ((0, 32), (1, 4))),
        "out_grad": noise(seeds[3], (S, N_GRP * HG * HD), 1.0, 6.0, ((0, 32), (1, 4))),
        "enc_lengths": draw_enc_lengths(jax.random.fold_in(seeds[6], 71), 0),
        "dec_lengths": draw_dec_lengths(jax.random.fold_in(seeds[6], 71), 0),
    }


NEG_FILL = -1e+30

def backward_pass(query_heads, grad_heads, key_heads, value_heads, visibility, block_rows, scaling):
    key_wide = key_heads.astype(jnp.float32)
    value_wide = value_heads.astype(jnp.float32)
    step_count = query_heads.shape[0] // block_rows

    def one_step(running, step_id):
        first_row = step_id * block_rows
        query_sub = lax.dynamic_slice_in_dim(query_heads, first_row, block_rows, 0).astype(jnp.float32)
        grad_sub = lax.dynamic_slice_in_dim(grad_heads, first_row, block_rows, 0).astype(jnp.float32)
        visible = visibility(first_row + jnp.arange(block_rows, dtype=jnp.int32))[None]
        scores = jnp.einsum('qhd,khd->hqk', query_sub, key_wide) * scaling
        dprob_rows = jnp.einsum('qhd,khd->hqk', grad_sub, value_wide)
        scores = jnp.where(visible, scores, NEG_FILL)
        row_peak = lax.optimization_barrier(jnp.max(scores, axis=2, keepdims=True))
        weights = jnp.where(visible, jnp.exp(scores - row_peak), 0.0)
        prob_full = weights / lax.optimization_barrier(jnp.sum(weights, axis=2, keepdims=True))
        row_delta = lax.optimization_barrier(jnp.sum(prob_full * dprob_rows, axis=2, keepdims=True))
        dscore = lax.optimization_barrier((prob_full * (dprob_rows - row_delta) * scaling).astype(jnp.bfloat16)).astype(jnp.float32)
        prob_low = lax.optimization_barrier(prob_full.astype(jnp.bfloat16)).astype(jnp.float32)
        query_part = jnp.einsum('hqk,khd->qhd', dscore, key_wide)
        key_part = jnp.einsum('hqk,qhd->khd', dscore, query_sub)
        value_part = jnp.einsum('hqk,qhd->khd', prob_low, grad_sub)
        return ((running[0] + key_part, running[1] + value_part), query_part)
    empty_grads = jnp.zeros(key_heads.shape, jnp.float32)
    (key_total, value_total), query_parts = lax.scan(one_step, (empty_grads, empty_grads), jnp.arange(step_count, dtype=jnp.int32))
    return (query_parts.reshape(query_heads.shape), key_total, value_total)

def reference(queries, key_rows, value_rows, out_grad, enc_lengths, dec_lengths):
    group_heads = H // 3
    slot_width = group_heads * HD
    scaling = 1.0 / math.sqrt(HD)

    def encoder_view(layout):
        return layout[:, :3 * slot_width].reshape(S, H, HD)

    def decoder_view(layout):
        return layout[:, 3 * slot_width:].reshape(DEC, H, HD)
    enc_index = jnp.arange(S, dtype=jnp.int32)
    enc_visible = enc_index % TOK < enc_lengths[enc_index // TOK]
    dec_index = jnp.arange(DEC, dtype=jnp.int32)
    dec_visible = dec_index % DTOK < dec_lengths[dec_index // DTOK]

    def enc_visibility(row_ids):
        return jnp.broadcast_to(enc_visible[None], (row_ids.shape[0], S))

    def dec_visibility(row_ids):
        self_part = dec_visible[None] & (dec_index[None] <= row_ids[:, None])
        return jnp.concatenate([jnp.broadcast_to(enc_visible[None], (row_ids.shape[0], S)), self_part], axis=1)
    enc_dq, enc_dk, enc_dv = backward_pass(encoder_view(queries), encoder_view(out_grad), encoder_view(key_rows), encoder_view(value_rows), enc_visibility, TOK, scaling)
    memory_keys = jnp.concatenate([encoder_view(key_rows), decoder_view(key_rows)], axis=0)
    memory_values = jnp.concatenate([encoder_view(value_rows), decoder_view(value_rows)], axis=0)
    dec_dq, dec_dk, dec_dv = backward_pass(decoder_view(queries), decoder_view(out_grad), memory_keys, memory_values, dec_visibility, DTOK, scaling)

    def to_layout(enc_part, dec_part):
        return jnp.concatenate([enc_part.reshape(S, 3 * slot_width), dec_part.reshape(S, slot_width)], axis=1).astype(jnp.float32)
    return (to_layout(enc_dq, dec_dq), to_layout(enc_dk + dec_dk[:S], dec_dk[S:]), to_layout(enc_dv + dec_dv[:S], dec_dv[S:]))
```

```python
import functools

import jax
import jax.numpy as jnp
from jax import lax
from jax.experimental import pallas as pl
from jax.experimental.pallas import tpu as pltpu
from jax.sharding import PartitionSpec as P

HD = 64
LANES = 128
NB = 32
TOK = 168
DTOK = 56
QTR = TOK // 4
DQTR = DTOK // 4
IN_ROWS = 216
DIN_ROWS = 72
OUT_ROWS = 192
DOUT_ROWS = 64
NQ_ENC = NB * QTR
NQ = NQ_ENC + NB * DQTR
TQ = 256
TK = 256
NK_ENC = -(-(NB * 176) // TK) * TK
NK_DEC = NB * 64
NK = NK_ENC + NK_DEC + TK
NT = NK // TK
NEG = -1e30
F32 = jnp.float32
BF16 = jnp.bfloat16
VMEM_BYTES = 56 * 1024 * 1024


def flip(head):
    return (head + 4) % 8


def lane_low(shape):
    return lax.broadcasted_iota(jnp.int32, shape, len(shape) - 1) < HD


def pair_up(first, second):
    low = lane_low(first.shape)
    even = jnp.where(low, first, pltpu.roll(second, HD, 1))
    odd = jnp.where(low, pltpu.roll(first, HD, 1), second)
    return even, odd


def pack_kernel(group_ref, lens_ref, q_ref, k_ref, v_ref, g_ref, x_ref, kv_s, qg_s):
    is_dec = group_ref[0] == 3
    enc_len = lens_ref[0].astype(F32)
    dec_len = lens_ref[1].astype(F32)
    for pair in range(4):
        cols = pl.ds(pair * LANES, LANES)
        even, odd = pair_up(k_ref[:, cols].astype(F32), v_ref[:, cols].astype(F32))
        kv_s[2 * pair], kv_s[2 * pair + 1] = even, odd
        even, odd = pair_up(q_ref[:, cols].astype(F32), g_ref[:, cols].astype(F32))
        qg_s[2 * pair], qg_s[2 * pair + 1] = even, odd
    row = lax.broadcasted_iota(jnp.int32, (8, LANES), 0)
    tail = jnp.where(row == 6, enc_len, jnp.where(row == 7, dec_len, 0.0))

    @pl.when(jnp.logical_not(is_dec))
    def _():
        for head in range(8):
            kv = kv_s[head]
            for part in range(4):
                qg = qg_s[head, pl.ds(part * QTR, QTR), :]
                x_ref[4 * head + part] = jnp.concatenate([kv, qg, tail[2:]], axis=0).astype(BF16)

    @pl.when(is_dec)
    def _():
        for head in range(8):
            for part in range(4):
                pieces = []
                for c in range(3):
                    src = flip(head) if c < 2 else head
                    pieces.append(kv_s[src, pl.ds(c, DTOK, stride=3), :])
                    pieces.append(qg_s[src, pl.ds(3 * part * DQTR + c, DQTR, stride=3), :])
                    pieces.append(tail[6:])
                x_ref[4 * head + part] = jnp.concatenate(pieces, axis=0).astype(BF16)


def unpack_kernel(group_ref, w_ref, qo_ref, ko_ref, vo_ref, dq_s, dk_s, dv_s, tmp_s):
    is_dec = group_ref[0] == 3

    @pl.when(jnp.logical_not(is_dec))
    def _():
        for pair in range(4):
            cols = pl.ds(pair * LANES, LANES)
            sums = []
            for head in (2 * pair, 2 * pair + 1):
                total = None
                for part in range(4):
                    chunk = w_ref[4 * head + part].astype(F32)
                    total = chunk[:TOK] if total is None else total + chunk[:TOK]
                    dq = chunk[TOK:]
                    turned = pltpu.roll(dq, HD, 1)
                    first, second = (dq, turned) if head % 2 == 0 else (turned, dq)
                    base = part * QTR
                    if head % 2 == 0:
                        dq_s[pl.ds(base, 21), :] = first[:21]
                        dq_s[pl.ds(base + 21, 21), :] = second[:21]
                    else:
                        low = lane_low((21, LANES))
                        for start, value in ((base, first), (base + 21, second)):
                            old = dq_s[pl.ds(start, 21), :]
                            dq_s[pl.ds(start, 21), :] = jnp.where(low, old, value[:21])
                sums.append(total)
            low = lane_low((TOK, LANES))
            ko_ref[:, cols] = jnp.where(low, sums[0], pltpu.roll(sums[1], HD, 1))
            vo_ref[:, cols] = jnp.where(low, pltpu.roll(sums[0], HD, 1), sums[1])
            qo_ref[:, cols] = dq_s[...]

    @pl.when(is_dec)
    def _():
        for pair in range(4):
            cols = pl.ds(pair * LANES, LANES)
            for c in range(3):
                sums, dqs = [], []
                for head in (2 * pair, 2 * pair + 1):
                    place = flip(head) if c < 2 else head
                    total, pieces = None, []
                    for part in range(4):
                        chunk = w_ref[4 * place + part].astype(F32)[DOUT_ROWS * c : DOUT_ROWS * (c + 1)]
                        kv = chunk[:DTOK]
                        total = kv if total is None else total + kv
                        dq = chunk[DTOK:]
                        turned = pltpu.roll(dq, HD, 1)
                        pieces.append((dq, turned) if head % 2 == 0 else (turned, dq))
                    sums.append(total)
                    dqs.append(pieces)
                low = lane_low((DTOK, LANES))
                rows = pl.ds(c, DTOK, stride=3)
                dk_s[rows, :] = jnp.where(low, sums[0], pltpu.roll(sums[1], HD, 1))
                dv_s[rows, :] = jnp.where(low, pltpu.roll(sums[0], HD, 1), sums[1])
                low = lane_low((8, LANES))
                for part in range(4):
                    for half in range(2):
                        value = jnp.where(low, dqs[0][part][half], dqs[1][part][half])
                        tmp_s[pl.ds(part * DQTR + half * 7, 7), :] = value[:7]
                dq_s[rows, :] = tmp_s[...]
            ko_ref[:, cols] = dk_s[...]
            vo_ref[:, cols] = dv_s[...]
            qo_ref[:, cols] = dq_s[...]


def fold(tile, op):
    rows = tile.shape[0]
    parts = [tile[8 * i : 8 * i + 8] for i in range(rows // 8)]
    while len(parts) > 1:
        parts = [op(parts[i], parts[i + 1]) if i + 1 < len(parts) else parts[i] for i in range(0, len(parts), 2)]
    return parts[0]


def attend_kernel(lens_ref, y_ref, z_ref, o_ref, zo_ref,
                  kv_s, ka_s, kt_s, pos_s, qg_s, dq_s, acc_s, s_s, dp_s, off_s):
    def place_block(block, offset, size, length, first_pos):
        row = lax.broadcasted_iota(jnp.int32, (size, LANES), 0)
        lane = lax.broadcasted_iota(jnp.int32, (size, LANES), 1)
        rows = pl.ds(pl.multiple_of(offset, 16), size)
        kv_s[rows, :] = block
        bias = jnp.where(row < length, 0.0, NEG)
        ka_s[rows, :] = jnp.where(lane == HD, bias, block.astype(F32)).astype(BF16)
        return rows, row

    lane_t = lax.broadcasted_iota(jnp.int32, (TK, LANES), 1)
    empty_kv = jnp.zeros((TK, LANES), BF16)
    empty_ka = jnp.where(lane_t == HD, NEG, 0.0).astype(BF16)

    def enc_block(b, offset):
        off_s[b] = offset
        length = lens_ref[b]
        place_block(y_ref[b, 0:176, :], offset, 176, length, 0)
        return offset + ((length + 15) // 16) * 16

    enc_end = lax.fori_loop(0, NB, enc_block, jnp.int32(0))
    rows = pl.ds(pl.multiple_of(enc_end, 16), TK)
    kv_s[rows, :] = empty_kv
    ka_s[rows, :] = empty_ka
    enc_tiles = (enc_end + TK - 1) // TK

    def dec_block(b, offset):
        off_s[NB + b] = offset
        length = lens_ref[NB + b]
        rows, row = place_block(z_ref[b, 0:64, :], offset, 64, length, b * DTOK)
        start = pl.multiple_of(offset - enc_tiles * TK, 16)
        pos_s[pl.ds(start, 64), :] = (row + b * DTOK).astype(F32)
        return offset + ((length + 15) // 16) * 16

    dec_end = lax.fori_loop(0, NB, dec_block, enc_tiles * TK)
    rows = pl.ds(pl.multiple_of(dec_end, 16), TK)
    kv_s[rows, :] = empty_kv
    ka_s[rows, :] = empty_ka
    pos_s[pl.ds(pl.multiple_of(dec_end - enc_tiles * TK, 16), TK), :] = jnp.zeros((TK, LANES), F32)
    all_tiles = (dec_end + TK - 1) // TK

    def tile_rows(kt):
        return pl.ds(pl.multiple_of(kt * TK, TK), TK)

    @pl.loop(0, all_tiles)
    def _(kt):
        kt_s[kt] = kv_s[tile_rows(kt), :].astype(F32).T[:HD].astype(BF16)
        acc_s[tile_rows(kt), :] = jnp.zeros((TK, LANES), F32)

    for b in range(NB):
        qg_s[pl.ds(QTR * b, 48), :] = y_ref[b].astype(F32)[TOK:]
    for b in range(NB):
        qg_s[pl.ds(NQ_ENC + DQTR * b, 16), :] = z_ref[b].astype(F32)[DTOK:]

    def q_tile(t, carry):
        q_rows = pl.ds(pl.multiple_of(t * TQ, TQ), TQ)
        qg = qg_s[q_rows, :]
        low = lane_low((TQ, LANES))
        q_nat = jnp.where(low, qg, 0.0).astype(BF16)
        d_nat = jnp.where(low, 0.0, qg).astype(BF16)
        turned = qg.T
        sub = lax.broadcasted_iota(jnp.int32, (LANES, TQ), 0)
        q_t = jnp.where(sub < HD, turned * 0.125, jnp.where(sub == HD, 1.0, 0.0)).astype(BF16)
        d_t = jnp.where(sub < HD, 0.0, turned).astype(BF16)
        q_id = t * TQ + lax.broadcasted_iota(jnp.int32, (1, TQ), 1) - NQ_ENC
        dec_id = jnp.maximum(q_id, 0)
        part = lens_ref[2 * NB]
        q_pos = (dec_id // DQTR) * DTOK + part * DQTR + dec_id % DQTR
        q_pos = jnp.where(q_id < 0, -1, q_pos).astype(F32)
        tiles = jnp.where(t * TQ + TQ > NQ_ENC, all_tiles, enc_tiles)

        def enc_scores(kt, peak):
            s = jnp.dot(ka_s[tile_rows(kt), :], q_t, preferred_element_type=F32)
            s_s[tile_rows(kt), :] = s
            return jnp.maximum(peak, fold(s, jnp.maximum))

        def dec_scores(kt, peak):
            s = jnp.dot(ka_s[tile_rows(kt), :], q_t, preferred_element_type=F32)
            k_pos = pos_s[tile_rows(kt - enc_tiles), :]
            k_pos = jnp.concatenate([k_pos, k_pos], axis=1)
            s = jnp.where(k_pos <= q_pos, s, NEG)
            s_s[tile_rows(kt), :] = s
            return jnp.maximum(peak, fold(s, jnp.maximum))

        peak = lax.fori_loop(0, enc_tiles, enc_scores, jnp.full((8, TQ), NEG, F32))
        peak = lax.fori_loop(enc_tiles, tiles, dec_scores, peak)
        peak = jnp.max(peak, axis=0, keepdims=True)

        def moments(kt, running):
            norm, inner = running
            prob = jnp.exp(s_s[tile_rows(kt), :] - peak)
            dprob = jnp.dot(kv_s[tile_rows(kt), :], d_t, preferred_element_type=F32)
            s_s[tile_rows(kt), :] = prob
            dp_s[tile_rows(kt), :] = dprob
            return norm + fold(prob, jnp.add), inner + fold(prob * dprob, jnp.add)

        zero = jnp.zeros((8, TQ), F32)
        norm, inner = lax.fori_loop(0, tiles, moments, (zero, zero))
        inverse = 1.0 / jnp.sum(norm, axis=0, keepdims=True)
        delta = jnp.sum(inner, axis=0, keepdims=True) * inverse

        def grads(kt, dq_t):
            prob = s_s[tile_rows(kt), :] * inverse
            dscore = (prob * (dp_s[tile_rows(kt), :] - delta)).astype(BF16)
            prob = prob.astype(BF16)
            acc_s[tile_rows(kt), :] += (
                jnp.dot(dscore, q_nat, preferred_element_type=F32)
                + jnp.dot(prob, d_nat, preferred_element_type=F32)
            )
            return dq_t + jnp.dot(kt_s[kt], dscore, preferred_element_type=F32)

        dq_t = lax.fori_loop(0, tiles, grads, jnp.zeros((HD, TQ), F32))
        dq_t = dq_t * 0.125
        dq_s[q_rows, :] = jnp.concatenate([dq_t, dq_t], axis=0).T
        return carry

    lax.fori_loop(0, NQ // TQ, q_tile, 0)

    def taken(offset, size, length):
        grad = acc_s[pl.ds(pl.multiple_of(offset, 16), size), :]
        row = lax.broadcasted_iota(jnp.int32, (size, LANES), 0)
        grad = jnp.where(lane_low((size, LANES)), grad * 0.125, grad)
        return jnp.where(row < length, grad, 0.0)

    dq_s[pl.ds(NQ, 32), :] = jnp.zeros((32, LANES), F32)
    for b in range(NB):
        base = QTR * b
        dq = jnp.where(lane_low((24, LANES)), dq_s[pl.ds(base, 24), :], dq_s[pl.ds(base + 21, 24), :])
        o_ref[b] = jnp.concatenate([taken(off_s[b], TOK, lens_ref[b]), dq], axis=0).astype(BF16)
        base = NQ_ENC + DQTR * b
        dq = jnp.where(lane_low((8, LANES)), dq_s[pl.ds(base, 8), :], dq_s[pl.ds(base + 7, 8), :])
        zo_ref[b] = jnp.concatenate([taken(off_s[NB + b], DTOK, lens_ref[NB + b]), dq], axis=0).astype(BF16)


SMEM = pl.BlockSpec(memory_space=pltpu.SMEM)
VMEM = pl.BlockSpec(memory_space=pltpu.VMEM)
PARAMS = pltpu.CompilerParams(vmem_limit_bytes=VMEM_BYTES)


def on_device(queries, key_rows, value_rows, out_grad, enc_lengths, dec_lengths):
    group = lax.axis_index("grp").astype(jnp.int32).reshape(1)
    own_lens = jnp.concatenate([enc_lengths, dec_lengths])
    chunks = pl.pallas_call(
        pack_kernel,
        out_shape=jax.ShapeDtypeStruct((NB, IN_ROWS, LANES), BF16),
        in_specs=[SMEM, SMEM, VMEM, VMEM, VMEM, VMEM],
        out_specs=VMEM,
        scratch_shapes=[pltpu.VMEM((8, TOK, LANES), F32), pltpu.VMEM((8, TOK, LANES), F32)],
        compiler_params=PARAMS,
    )(group, own_lens, queries, key_rows, value_rows, out_grad)
    held = lax.all_to_all(chunks, "blk", 0, 0, tiled=True)
    lens = held[:, 214:216, 0].T.reshape(2 * NB).astype(jnp.int32)
    part = (lax.axis_index("blk") % 4).astype(jnp.int32).reshape(1)
    lens = jnp.concatenate([lens, part])

    def partner(c, blk):
        return (blk + 16) % NB if c < 2 else blk

    to_enc = [[(3 * NB + s, c * NB + partner(c, s)) for s in range(NB)] for c in range(3)]
    got = [
        lax.ppermute(held[:, DIN_ROWS * c : DIN_ROWS * (c + 1)], ("grp", "blk"), to_enc[c])
        for c in range(3)
    ]
    dec_held = got[0] + got[1] + got[2]
    enc_out, dec_out = pl.pallas_call(
        attend_kernel,
        out_shape=[
            jax.ShapeDtypeStruct((NB, OUT_ROWS, LANES), BF16),
            jax.ShapeDtypeStruct((NB, DOUT_ROWS, LANES), BF16),
        ],
        in_specs=[SMEM, VMEM, VMEM],
        out_specs=[VMEM, VMEM],
        scratch_shapes=[
            pltpu.VMEM((NK, LANES), BF16),
            pltpu.VMEM((NK, LANES), BF16),
            pltpu.VMEM((NT, HD, TK), BF16),
            pltpu.VMEM((NK_DEC + TK, LANES), F32),
            pltpu.VMEM((NQ + 48, LANES), F32),
            pltpu.VMEM((NQ + 48, LANES), F32),
            pltpu.VMEM((NK, LANES), F32),
            pltpu.VMEM((NK, TQ), F32),
            pltpu.VMEM((NK, TQ), F32),
            pltpu.SMEM((2 * NB,), jnp.int32),
        ],
        compiler_params=PARAMS,
    )(lens, held, dec_held)
    back = [
        lax.ppermute(dec_out, ("grp", "blk"), [(d, s) for s, d in to_enc[c]]) for c in range(3)
    ]
    final = jnp.where(group[0] == 3, jnp.concatenate(back, axis=1), enc_out)
    final = lax.all_to_all(final, "blk", 0, 0, tiled=True)
    out = jax.ShapeDtypeStruct(queries.shape, F32)
    return pl.pallas_call(
        unpack_kernel,
        out_shape=[out, out, out],
        in_specs=[SMEM, VMEM],
        out_specs=[VMEM, VMEM, VMEM],
        scratch_shapes=[pltpu.VMEM((TOK, LANES), F32)] * 3 + [pltpu.VMEM((DTOK, LANES), F32)],
        compiler_params=PARAMS,
    )(group, final)


def solution(mesh):
    rows = P("blk", "grp")
    return jax.shard_map(
        on_device,
        mesh=mesh,
        in_specs=(rows, rows, rows, rows, P("blk"), P("blk")),
        out_specs=(rows, rows, rows),
        check_vma=False,
    )
```

```python
import functools

import jax
import jax.numpy as jnp
from jax import lax
from jax.experimental import pallas as pl
from jax.experimental.pallas import tpu as pltpu
from jax.sharding import PartitionSpec as P

HD = 64
LANES = 128
NB = 32
TOK = 168
DTOK = 56
QTR = TOK // 4
DQTR = DTOK // 4
IN_ROWS = 216
DIN_ROWS = 72
OUT_ROWS = 192
DOUT_ROWS = 64
NQ_ENC = NB * QTR
DQ = NB * DQTR
TQ = 256
TK = 1024
SUB = 256
TKD = 512
NK_ENC = -(-(NB * 176) // TK) * TK
NK_DEC = -(-(NB * 64) // TKD) * TKD
REST = 2 * TQ - DQ
FIRST_TILES = 3
LAST_TILES = (NQ_ENC - REST) // TQ - FIRST_TILES
THERE_ROWS = 2 * TQ + 48
BACK_ROWS = 2 * TQ + 32
NEG = -1e30
F32 = jnp.float32
BF16 = jnp.bfloat16
VMEM_BYTES = 60 * 1024 * 1024


def flip(head):
    return (head + 4) % 8


def lane_low(shape):
    return lax.broadcasted_iota(jnp.int32, shape, len(shape) - 1) < HD


def pair_up(first, second):
    low = lane_low(first.shape)
    even = jnp.where(low, first, pltpu.roll(second, HD, 1))
    odd = jnp.where(low, pltpu.roll(first, HD, 1), second)
    return even, odd


def pack_kernel(group_ref, enc_ref, dec_ref, q_ref, k_ref, v_ref, g_ref, x_ref, kv_s, qg_s):
    is_dec = group_ref[0] == 3
    enc_len = enc_ref[0].astype(F32)
    dec_len = dec_ref[0].astype(F32)
    for pair in range(4):
        cols = pl.ds(pair * LANES, LANES)
        even, odd = pair_up(k_ref[:, cols].astype(F32), v_ref[:, cols].astype(F32))
        kv_s[2 * pair], kv_s[2 * pair + 1] = even, odd
        even, odd = pair_up(q_ref[:, cols].astype(F32), g_ref[:, cols].astype(F32))
        qg_s[2 * pair], qg_s[2 * pair + 1] = even, odd
    row = lax.broadcasted_iota(jnp.int32, (8, LANES), 0)
    tail = jnp.where(row == 6, enc_len, jnp.where(row == 7, dec_len, 0.0))

    @pl.when(jnp.logical_not(is_dec))
    def _():
        for head in range(8):
            kv = kv_s[head]
            for part in range(4):
                qg = qg_s[head, pl.ds(part * QTR, QTR), :]
                x_ref[4 * head + part] = jnp.concatenate([kv, qg, tail[2:]], axis=0).astype(BF16)

    @pl.when(is_dec)
    def _():
        for head in range(8):
            for part in range(4):
                pieces = []
                for c in range(3):
                    src = flip(head) if c < 2 else head
                    pieces.append(kv_s[src, pl.ds(c, DTOK, stride=3), :])
                    pieces.append(qg_s[src, pl.ds(3 * part * DQTR + c, DQTR, stride=3), :])
                    pieces.append(tail[6:])
                x_ref[4 * head + part] = jnp.concatenate(pieces, axis=0).astype(BF16)


def unpack_kernel(group_ref, w_ref, qo_ref, ko_ref, vo_ref, dq_s, dk_s, dv_s, tmp_s):
    is_dec = group_ref[0] == 3

    @pl.when(jnp.logical_not(is_dec))
    def _():
        for pair in range(4):
            cols = pl.ds(pair * LANES, LANES)
            sums = []
            for head in (2 * pair, 2 * pair + 1):
                total = None
                for part in range(4):
                    chunk = w_ref[4 * head + part].astype(F32)
                    total = chunk[:TOK] if total is None else total + chunk[:TOK]
                    dq = chunk[TOK:]
                    turned = pltpu.roll(dq, HD, 1)
                    first, second = (dq, turned) if head % 2 == 0 else (turned, dq)
                    base = part * QTR
                    if head % 2 == 0:
                        dq_s[pl.ds(base, 21), :] = first[:21]
                        dq_s[pl.ds(base + 21, 21), :] = second[:21]
                    else:
                        low = lane_low((21, LANES))
                        for start, value in ((base, first), (base + 21, second)):
                            old = dq_s[pl.ds(start, 21), :]
                            dq_s[pl.ds(start, 21), :] = jnp.where(low, old, value[:21])
                sums.append(total)
            low = lane_low((TOK, LANES))
            ko_ref[:, cols] = jnp.where(low, sums[0], pltpu.roll(sums[1], HD, 1))
            vo_ref[:, cols] = jnp.where(low, pltpu.roll(sums[0], HD, 1), sums[1])
            qo_ref[:, cols] = dq_s[...]

    @pl.when(is_dec)
    def _():
        for pair in range(4):
            cols = pl.ds(pair * LANES, LANES)
            for c in range(3):
                sums, dqs = [], []
                for head in (2 * pair, 2 * pair + 1):
                    place = flip(head) if c < 2 else head
                    total, pieces = None, []
                    for part in range(4):
                        chunk = w_ref[4 * place + part].astype(F32)[DOUT_ROWS * c : DOUT_ROWS * (c + 1)]
                        kv = chunk[:DTOK]
                        total = kv if total is None else total + kv
                        dq = chunk[DTOK:]
                        turned = pltpu.roll(dq, HD, 1)
                        pieces.append((dq, turned) if head % 2 == 0 else (turned, dq))
                    sums.append(total)
                    dqs.append(pieces)
                low = lane_low((DTOK, LANES))
                rows = pl.ds(c, DTOK, stride=3)
                dk_s[rows, :] = jnp.where(low, sums[0], pltpu.roll(sums[1], HD, 1))
                dv_s[rows, :] = jnp.where(low, pltpu.roll(sums[0], HD, 1), sums[1])
                low = lane_low((8, LANES))
                for part in range(4):
                    for half in range(2):
                        value = jnp.where(low, dqs[0][part][half], dqs[1][part][half])
                        tmp_s[pl.ds(part * DQTR + half * 7, 7), :] = value[:7]
                dq_s[rows, :] = tmp_s[...]
            ko_ref[:, cols] = dk_s[...]
            vo_ref[:, cols] = dv_s[...]
            qo_ref[:, cols] = dq_s[...]


def fold(tile, op):
    parts = [tile[8 * i : 8 * i + 8] for i in range(tile.shape[0] // 8)]
    while len(parts) > 1:
        parts = [op(parts[i], parts[i + 1]) if i + 1 < len(parts) else parts[i] for i in range(0, len(parts), 2)]
    return parts[0]


def spread(stat, rows):
    return jnp.concatenate([stat] * (rows // 8), axis=0)


def tile_rows(kt, size):
    return pl.ds(pl.multiple_of(kt * size, size), size)


def place_block(kv_ref, ka_ref, block, offset, length):
    size = block.shape[0]
    row = lax.broadcasted_iota(jnp.int32, (size, LANES), 0)
    lane = lax.broadcasted_iota(jnp.int32, (size, LANES), 1)
    rows = pl.ds(pl.multiple_of(offset, 16), size)
    kv_ref[rows, :] = block
    bias = jnp.where(row < length, 0.0, NEG)
    ka_ref[rows, :] = jnp.where(lane == HD, bias, block.astype(F32)).astype(BF16)
    return rows, row


def place_padding(kv_ref, ka_ref, offset, size):
    lane = lax.broadcasted_iota(jnp.int32, (size, LANES), 1)
    rows = pl.ds(pl.multiple_of(offset, 16), size)
    kv_ref[rows, :] = jnp.zeros((size, LANES), BF16)
    ka_ref[rows, :] = jnp.where(lane == HD, NEG, 0.0).astype(BF16)
    return rows


def turn(keys):
    return keys.astype(F32).T[:HD].astype(BF16)


def read_lens(y_ref, wide_s, lens_s, sem):
    for b in range(NB):
        wide_s[pl.ds(8 * b, 8), :] = y_ref[b].astype(F32)[IN_ROWS - 8 :].astype(jnp.int32)
    copy = pltpu.make_async_copy(wide_s, lens_s, sem)
    copy.start()
    copy.wait()


def query_operands(qg):
    turned = qg.T
    sub = lax.broadcasted_iota(jnp.int32, (LANES, TQ), 0)
    q_t = jnp.where(sub < HD, turned * 0.125, jnp.where(sub == HD, 1.0, 0.0)).astype(BF16)
    d_t = jnp.where(sub < HD, 0.0, turned).astype(BF16)
    return q_t, d_t


def natural_operands(qg):
    low = lane_low((TQ, LANES))
    return jnp.where(low, qg, 0.0).astype(BF16), jnp.where(low, 0.0, qg).astype(BF16)


def score_sums(found, running):
    s, dprob = found
    peak, norm, inner = running
    new_peak = jnp.maximum(peak, fold(s, jnp.maximum))
    prob = jnp.exp(s - spread(new_peak, s.shape[0]))
    shrink = jnp.exp(peak - new_peak)
    norm = norm * shrink + fold(prob, jnp.add)
    inner = inner * shrink + fold(prob * dprob, jnp.add)
    return new_peak, norm, inner


def merged(running):
    peak8, norm8, inner8 = running
    peak = jnp.max(peak8, axis=0, keepdims=True)
    shrink = jnp.exp(peak8 - peak)
    norm = jnp.sum(norm8 * shrink, axis=0, keepdims=True)
    inner = jnp.sum(inner8 * shrink, axis=0, keepdims=True)
    return peak, norm, inner


def no_moments():
    zero = jnp.zeros((8, TQ), F32)
    return jnp.full((8, TQ), NEG, F32), zero, zero


def grad_parts(s, dprob, total, delta):
    prob = jnp.exp(s - total)
    dscore = (prob * (dprob - delta)).astype(BF16)
    return prob.astype(BF16), dscore


def key_grads(parts, naturals):
    prob, dscore = parts
    q_nat, d_nat = naturals
    return jnp.dot(dscore, q_nat, preferred_element_type=F32) + jnp.dot(
        prob, d_nat, preferred_element_type=F32
    )


def both_halves(dq_t):
    dq_t = dq_t * 0.125
    return jnp.concatenate([dq_t, dq_t], axis=0).T


def write_split(ref, first_row, value):
    for term in range(3):
        low = value.astype(BF16).astype(F32)
        value = value - low
        for half in range(2):
            ref[pl.ds(first_row + 4 * term + half, 1), :] = low[:, half * LANES : (half + 1) * LANES]


def read_split(rows, first_row):
    total = None
    for term in (2, 1, 0):
        at = first_row + 4 * term
        piece = jnp.concatenate([rows[at : at + 1], rows[at + 1 : at + 2]], axis=1)
        total = piece if total is None else total + piece
    return total


def sweep(count, tiles, refs, query, start, emit):
    kv_ref, ka_ref, kt_ref, acc_ref, s_pair, dp_pair = refs

    def tile_step(kt, slot, now, then, dq_t, running):
        found = None
        for j in range(TK // SUB):
            rows = pl.ds(pl.multiple_of(kt * TK + j * SUB, SUB), SUB)
            fresh = None
            if then is not None:
                q_t, d_t = then
                fresh = (
                    jnp.dot(ka_ref[rows, :], q_t, preferred_element_type=F32),
                    jnp.dot(kv_ref[rows, :], d_t, preferred_element_type=F32),
                )
                s_pair[1 - slot][rows, :], dp_pair[1 - slot][rows, :] = fresh
            if now is not None:
                naturals, total, delta = now
                parts = grad_parts(s_pair[slot][rows, :], dp_pair[slot][rows, :], total, delta)
            if found is not None:
                running = score_sums(found, running)
            if now is not None:
                acc_ref[rows, :] += key_grads(parts, naturals)
                keys = kt_ref[kt, :, j * SUB : (j + 1) * SUB]
                dq_t = dq_t + jnp.dot(keys, parts[1], preferred_element_type=F32)
            found = fresh
        if found is not None:
            running = score_sums(found, running)
        return dq_t, running

    def run(slot, now, then, running):
        def step(kt, carry):
            return tile_step(kt, slot, now, then, *carry)

        return lax.fori_loop(0, tiles, step, (jnp.zeros((HD, TQ), F32), running))

    _, running = run(1, None, query_operands(query(0)), start(0))
    for t in range(count):
        peak, norm, inner = merged(running)
        total, delta = peak + jnp.log(norm), inner / norm
        now = natural_operands(query(t)), total, delta
        if t == count - 1:
            dq_t, _ = run(t % 2, now, None, no_moments())
        else:
            dq_t, running = run(t % 2, now, query_operands(query(t + 1)), start(t + 1))
        emit(t, dq_t, total, delta)


def clear(acc_ref, tiles):
    @pl.loop(0, tiles)
    def _(kt):
        acc_ref[tile_rows(kt, TK), :] = jnp.zeros((TK, LANES), F32)


def enc_first_kernel(place_ref, y_ref, kv_ref, ka_ref, kt_ref, qg_ref, acc_ref, dq_ref, meta_ref,
                     s0_s, s1_s, dp0_s, dp1_s, wide_s, lens_s, sem):
    @pl.when(place_ref[0] < 3)
    def _():
        read_lens(y_ref, wide_s, lens_s, sem)

        def block(b, offset):
            length = lens_s[8 * b + 6, 0]
            meta_ref[b] = offset
            meta_ref[NB + b] = length
            place_block(kv_ref, ka_ref, y_ref[b, 0:176, :], offset, length)
            return offset + ((length + 15) // 16) * 16

        end = lax.fori_loop(0, NB, block, jnp.int32(0))
        place_padding(kv_ref, ka_ref, end, TK)
        tiles = (end + TK - 1) // TK
        meta_ref[2 * NB] = tiles

        @pl.loop(0, tiles)
        def _(kt):
            kt_ref[kt] = turn(kv_ref[tile_rows(kt, TK), :])

        clear(acc_ref, tiles)
        for b in range(NB):
            qg_ref[pl.ds(QTR * b, 48), :] = y_ref[b].astype(F32)[TOK:]

        def emit(t, dq_t, total, delta):
            dq_ref[pl.ds(t * TQ, TQ), :] = both_halves(dq_t)

        sweep(FIRST_TILES, tiles, (kv_ref, ka_ref, kt_ref, acc_ref, (s0_s, s1_s), (dp0_s, dp1_s)),
              lambda t: qg_ref[pl.ds(t * TQ, TQ), :], lambda t: no_moments(), emit)


def enc_dec_kernel(place_ref, meta_ref, kv_ref, ka_ref, kt_ref, qg_ref, m0_ref, m1_ref, m2_ref,
                   acc_ref, dq_ref, back_ref, s0_s, s1_s, dp0_s, dp1_s, own_s, stat_s):
    group = place_ref[0]

    @pl.when(group < 3)
    def _():
        got = jnp.where(group == 0, m0_ref[...], jnp.where(group == 1, m1_ref[...], m2_ref[...])).astype(F32)
        own_s[...] = got[: 2 * TQ]
        own_s[pl.ds(DQ, REST), :] = qg_ref[pl.ds(NQ_ENC - REST, REST), :]
        stats = got[2 * TQ :]
        tiles = meta_ref[2 * NB]
        clear(acc_ref, tiles)

        def start(t):
            row = lax.broadcasted_iota(jnp.int32, (8, TQ), 0)
            peak, norm, inner = (read_split(stats, 12 * k + 2 * t) for k in range(3))
            return (jnp.where(row == 0, peak, NEG), jnp.where(row == 0, norm, 0.0),
                    jnp.where(row == 0, inner, 0.0))

        stat_s[...] = jnp.zeros_like(stat_s)

        def emit(t, dq_t, total, delta):
            dq = both_halves(dq_t)
            back_ref[pl.ds(t * TQ, TQ), :] = dq.astype(BF16)
            write_split(stat_s, 2 * t, total)
            write_split(stat_s, 12 + 2 * t, delta)
            if t == 1:
                dq_ref[...] = dq[TQ - REST :]

        sweep(2, tiles, (kv_ref, ka_ref, kt_ref, acc_ref, (s0_s, s1_s), (dp0_s, dp1_s)),
              lambda t: own_s[pl.ds(t * TQ, TQ), :], start, emit)
        back_ref[pl.ds(2 * TQ, BACK_ROWS - 2 * TQ), :] = stat_s[...].astype(BF16)


def enc_last_kernel(place_ref, meta_ref, kv_ref, ka_ref, kt_ref, qg_ref, acc1_ref, acc2_ref, dq1_ref, dq2_ref,
                    o_ref, acc_s, dq_s, s0_s, s1_s, dp0_s, dp1_s):
    @pl.when(place_ref[0] < 3)
    def _():
        tiles = meta_ref[2 * NB]
        clear(acc_s, tiles)
        dq_s[pl.ds(0, FIRST_TILES * TQ), :] = dq1_ref[...]
        dq_s[pl.ds(NQ_ENC - REST, REST), :] = dq2_ref[...]
        dq_s[pl.ds(NQ_ENC, 8), :] = jnp.zeros((8, LANES), F32)

        def emit(t, dq_t, total, delta):
            dq_s[pl.ds((FIRST_TILES + t) * TQ, TQ), :] = both_halves(dq_t)

        sweep(LAST_TILES, tiles, (kv_ref, ka_ref, kt_ref, acc_s, (s0_s, s1_s), (dp0_s, dp1_s)),
              lambda t: qg_ref[pl.ds((FIRST_TILES + t) * TQ, TQ), :], lambda t: no_moments(), emit)
        row = lax.broadcasted_iota(jnp.int32, (TOK, LANES), 0)
        low = lane_low((TOK, LANES))
        for b in range(NB):
            rows = pl.ds(pl.multiple_of(meta_ref[b], 16), TOK)
            grad = acc1_ref[rows, :] + acc2_ref[rows, :] + acc_s[rows, :]
            grad = jnp.where(row < meta_ref[NB + b], jnp.where(low, grad * 0.125, grad), 0.0)
            base = QTR * b
            dq = jnp.where(lane_low((24, LANES)), dq_s[pl.ds(base, 24), :], dq_s[pl.ds(base + 21, 24), :])
            o_ref[b] = jnp.concatenate([grad, dq], axis=0).astype(BF16)


def dec_query_pos(t, part):
    q_id = t * TQ + lax.broadcasted_iota(jnp.int32, (1, TQ), 1)
    place = (q_id // DQTR) * DTOK + part * DQTR + q_id % DQTR
    return jnp.where(q_id < DQ, place, -1).astype(F32)


def dec_scores(kv_ref, ka_ref, pos_ref, c, rows, operands, q_at):
    q_t, d_t = operands
    s = jnp.dot(ka_ref[c, rows, :], q_t, preferred_element_type=F32)
    dprob = jnp.dot(kv_ref[c, rows, :], d_t, preferred_element_type=F32)
    k_at = pos_ref[rows, :]
    return jnp.where(jnp.concatenate([k_at, k_at], axis=1) <= q_at, s, NEG), dprob


def dec_first_kernel(place_ref, y_ref, kv_ref, ka_ref, kt_ref, pos_ref, m_ref, meta_ref,
                     qg_s, stat_s, wide_s, lens_s, sem):
    @pl.when(place_ref[0] == 3)
    def _():
        read_lens(y_ref, wide_s, lens_s, sem)

        def block(b, offset):
            length = lens_s[8 * b + 7, 0]
            meta_ref[b] = offset
            meta_ref[NB + b] = length
            chunk = y_ref[b].astype(F32)
            for c in range(3):
                keys = chunk[DIN_ROWS * c : DIN_ROWS * c + 64].astype(BF16)
                rows, row = place_block(kv_ref.at[c], ka_ref.at[c], keys, offset, length)
            pos_ref[rows, :] = (row + b * DTOK).astype(F32)
            return offset + ((length + 15) // 16) * 16

        end = lax.fori_loop(0, NB, block, jnp.int32(0))
        for c in range(3):
            rows = place_padding(kv_ref.at[c], ka_ref.at[c], end, TKD)
        pos_ref[rows, :] = jnp.zeros((TKD, LANES), F32)
        tiles = (end + TKD - 1) // TKD
        meta_ref[2 * NB] = tiles
        for b in range(NB):
            chunk = y_ref[b].astype(F32)
            for c in range(3):
                qg_s[c, pl.ds(DQTR * b, 16), :] = chunk[DIN_ROWS * c + DTOK : DIN_ROWS * (c + 1)]
        part = place_ref[1]
        stat_s[...] = jnp.zeros_like(stat_s)
        for c in range(3):
            qg_s[c, pl.ds(DQ, REST), :] = jnp.zeros((REST, LANES), F32)
            m_ref[c, pl.ds(0, 2 * TQ), :] = qg_s[c].astype(BF16)

            @pl.loop(0, tiles)
            def _(kt):
                kt_ref[c, kt] = turn(kv_ref[c, tile_rows(kt, TKD), :])

            operands = [query_operands(qg_s[c, pl.ds(t * TQ, TQ), :]) for t in range(2)]
            q_at = [dec_query_pos(t, part) for t in range(2)]

            def step(kt, carry):
                carry = list(carry)
                rows = tile_rows(kt, TKD)
                found = [dec_scores(kv_ref, ka_ref, pos_ref, c, rows, operands[t], q_at[t]) for t in range(2)]
                return tuple(score_sums(found[t], carry[t]) for t in range(2))

            found = lax.fori_loop(0, tiles, step, (no_moments(), no_moments()))
            for t in range(2):
                q_id = t * TQ + lax.broadcasted_iota(jnp.int32, (1, TQ), 1)
                for k, value in enumerate(merged(found[t])):
                    write_split(stat_s, 12 * k + 2 * t, jnp.where(q_id < DQ, value, NEG if k == 0 else 0.0))
            m_ref[c, pl.ds(2 * TQ, THERE_ROWS - 2 * TQ), :] = stat_s[...].astype(BF16)


def dec_last_kernel(place_ref, meta_ref, kv_ref, ka_ref, kt_ref, pos_ref, m_ref, b0_ref, b1_ref, b2_ref, enc_ref,
                    o_ref, acc_s, dq_s, out_s, sem):
    @pl.when(place_ref[0] == 3)
    def _():
        tiles = meta_ref[2 * NB]
        part = place_ref[1]
        for c, back_ref in enumerate((b0_ref, b1_ref, b2_ref)):
            qg = m_ref[c, pl.ds(0, 2 * TQ), :].astype(F32)
            back = back_ref[...].astype(F32)
            stats = back[2 * TQ :]
            cut = [qg[t * TQ : (t + 1) * TQ] for t in range(2)]
            operands = [query_operands(cut[t]) for t in range(2)]
            naturals = [natural_operands(cut[t]) for t in range(2)]
            q_at = [dec_query_pos(t, part) for t in range(2)]
            total = [read_split(stats, 2 * t) for t in range(2)]
            delta = [read_split(stats, 12 + 2 * t) for t in range(2)]

            def step(kt, dqs):
                rows = tile_rows(kt, TKD)
                found = [dec_scores(kv_ref, ka_ref, pos_ref, c, rows, operands[t], q_at[t]) for t in range(2)]
                parts = [grad_parts(*found[t], total[t], delta[t]) for t in range(2)]
                acc_s[rows, :] = key_grads(parts[0], naturals[0]) + key_grads(parts[1], naturals[1])
                keys = kt_ref[c, kt]
                return tuple(dqs[t] + jnp.dot(keys, parts[t][1], preferred_element_type=F32) for t in range(2))

            none = jnp.zeros((HD, TQ), F32)
            dqs = lax.fori_loop(0, tiles, step, (none, none))
            for t in range(2):
                rows = pl.ds(t * TQ, TQ)
                dq_s[rows, :] = both_halves(dqs[t]) + back[t * TQ : (t + 1) * TQ]
            row = lax.broadcasted_iota(jnp.int32, (DTOK, LANES), 0)
            low = lane_low((DTOK, LANES))
            for b in range(NB):
                grad = acc_s[pl.ds(pl.multiple_of(meta_ref[b], 16), DTOK), :]
                grad = jnp.where(row < meta_ref[NB + b], jnp.where(low, grad * 0.125, grad), 0.0)
                base = DQTR * b
                dq = jnp.where(lane_low((8, LANES)), dq_s[pl.ds(base, 8), :], dq_s[pl.ds(base + 7, 8), :])
                out_s[b, pl.ds(DOUT_ROWS * c, DOUT_ROWS), :] = jnp.concatenate([grad, dq], axis=0).astype(BF16)
        copy = pltpu.make_async_copy(out_s, o_ref, sem)
        copy.start()
        copy.wait()


SMEM = pl.BlockSpec(memory_space=pltpu.SMEM)
VMEM = pl.BlockSpec(memory_space=pltpu.VMEM)
ANY = pl.BlockSpec(memory_space=pl.ANY)
PARAMS = pltpu.CompilerParams(vmem_limit_bytes=VMEM_BYTES)


def shaped(shape, dtype):
    return jax.ShapeDtypeStruct(shape, dtype)


def lens_scratch():
    return [
        pltpu.VMEM((8 * NB, LANES), jnp.int32),
        pltpu.SMEM((8 * NB, LANES), jnp.int32),
        pltpu.SemaphoreType.DMA(()),
    ]


def score_scratch():
    return [pltpu.VMEM((NK_ENC, TQ), F32)] * 4


META = shaped((2 * NB + 8,), jnp.int32)


def dec_first(place, held):
    return pl.pallas_call(
        dec_first_kernel,
        out_shape=[
            shaped((3, NK_DEC + TKD, LANES), BF16),
            shaped((3, NK_DEC + TKD, LANES), BF16),
            shaped((3, NK_DEC // TKD, HD, TKD), BF16),
            shaped((NK_DEC + TKD, LANES), F32),
            shaped((3, THERE_ROWS, LANES), BF16),
            META,
        ],
        in_specs=[SMEM, VMEM],
        out_specs=[VMEM] * 5 + [SMEM],
        scratch_shapes=[
            pltpu.VMEM((3, 2 * TQ, LANES), F32),
            pltpu.VMEM((THERE_ROWS - 2 * TQ, LANES), F32),
        ] + lens_scratch(),
        compiler_params=PARAMS,
    )(place, held)


def enc_first(place, held):
    return pl.pallas_call(
        enc_first_kernel,
        out_shape=[
            shaped((NK_ENC + TK, LANES), BF16),
            shaped((NK_ENC + TK, LANES), BF16),
            shaped((NK_ENC // TK, HD, TK), BF16),
            shaped((NQ_ENC + 8, LANES), F32),
            shaped((NK_ENC, LANES), F32),
            shaped((FIRST_TILES * TQ, LANES), F32),
            META,
        ],
        in_specs=[SMEM, VMEM],
        out_specs=[VMEM] * 6 + [SMEM],
        scratch_shapes=score_scratch() + lens_scratch(),
        compiler_params=PARAMS,
    )(place, held)


def enc_dec(place, meta, keys, messages):
    return pl.pallas_call(
        enc_dec_kernel,
        out_shape=[
            shaped((NK_ENC, LANES), F32),
            shaped((REST, LANES), F32),
            shaped((BACK_ROWS, LANES), BF16),
        ],
        in_specs=[SMEM, SMEM] + [VMEM] * 7,
        out_specs=[VMEM] * 3,
        scratch_shapes=score_scratch() + [
            pltpu.VMEM((2 * TQ, LANES), F32),
            pltpu.VMEM((BACK_ROWS - 2 * TQ, LANES), F32),
        ],
        compiler_params=PARAMS,
    )(place, meta, *keys, *messages)


def enc_last(place, meta, keys, accs, dqs):
    return pl.pallas_call(
        enc_last_kernel,
        out_shape=shaped((NB, OUT_ROWS, LANES), BF16),
        in_specs=[SMEM, SMEM] + [VMEM] * 8,
        out_specs=VMEM,
        scratch_shapes=[
            pltpu.VMEM((NK_ENC, LANES), F32),
            pltpu.VMEM((NQ_ENC + 8, LANES), F32),
        ] + score_scratch(),
        compiler_params=PARAMS,
    )(place, meta, *keys, *accs, *dqs)


def dec_last(place, meta, keys, message, back, enc_out):
    return pl.pallas_call(
        dec_last_kernel,
        out_shape=shaped((NB, OUT_ROWS, LANES), BF16),
        in_specs=[SMEM, SMEM] + [VMEM] * 8 + [ANY],
        out_specs=ANY,
        scratch_shapes=[
            pltpu.VMEM((NK_DEC + TKD, LANES), F32),
            pltpu.VMEM((2 * TQ, LANES), F32),
            pltpu.VMEM((NB, OUT_ROWS, LANES), BF16),
            pltpu.SemaphoreType.DMA(()),
        ],
        input_output_aliases={10: 0},
        compiler_params=PARAMS,
    )(place, meta, *keys, message, *back, enc_out)


def on_device(queries, key_rows, value_rows, out_grad, enc_lengths, dec_lengths):
    group = lax.axis_index("grp").astype(jnp.int32)
    part = (lax.axis_index("blk") % 4).astype(jnp.int32)
    place = jnp.stack([group, part])
    chunks = pl.pallas_call(
        pack_kernel,
        out_shape=shaped((NB, IN_ROWS, LANES), BF16),
        in_specs=[SMEM, SMEM, SMEM, VMEM, VMEM, VMEM, VMEM],
        out_specs=VMEM,
        scratch_shapes=[pltpu.VMEM((8, TOK, LANES), F32), pltpu.VMEM((8, TOK, LANES), F32)],
        compiler_params=PARAMS,
    )(place, enc_lengths, dec_lengths, queries, key_rows, value_rows, out_grad)
    held = lax.all_to_all(chunks, "blk", 0, 0, tiled=True)

    def partner(c, blk):
        return (blk + 16) % NB if c < 2 else blk

    there = [[(3 * NB + s, c * NB + partner(c, s)) for s in range(NB)] for c in range(3)]
    *dec_keys, message, dec_meta = dec_first(place, held)
    got = [lax.ppermute(message[c], ("grp", "blk"), there[c]) for c in range(3)]
    *enc_keys, acc1, dq1, enc_meta = enc_first(place, held)
    acc2, dq2, answer = enc_dec(place, enc_meta, enc_keys, got)
    back = [lax.ppermute(answer, ("grp", "blk"), [(d, s) for s, d in there[c]]) for c in range(3)]
    enc_out = enc_last(place, enc_meta, enc_keys, (acc1, acc2), (dq1, dq2))
    final = dec_last(place, dec_meta, dec_keys, message, back, enc_out)
    final = lax.all_to_all(final, "blk", 0, 0, tiled=True)
    out = shaped(queries.shape, F32)
    return pl.pallas_call(
        unpack_kernel,
        out_shape=[out, out, out],
        in_specs=[SMEM, VMEM],
        out_specs=[VMEM, VMEM, VMEM],
        scratch_shapes=[pltpu.VMEM((TOK, LANES), F32)] * 3 + [pltpu.VMEM((DTOK, LANES), F32)],
        compiler_params=PARAMS,
    )(place, final)


def solution(mesh):
    rows = P("blk", "grp")
    return jax.shard_map(
        on_device,
        mesh=mesh,
        in_specs=(rows, rows, rows, rows, P("blk"), P("blk")),
        out_specs=(rows, rows, rows),
        check_vma=False,
    )
```

```python
import functools

import jax
import jax.numpy as jnp
from jax import lax
from jax.experimental import pallas as pl
from jax.experimental.pallas import tpu as pltpu
from jax.sharding import PartitionSpec as P

HD = 64
LANES = 128
NB = 32
TOK = 168
DTOK = 56
QTR = TOK // 4
DQTR = DTOK // 4
IN_ROWS = 216
DIN_ROWS = 72
OUT_ROWS = 192
DOUT_ROWS = 64
NQ_ENC = NB * QTR
DQ = NB * DQTR
TQ = 256
TK = 2048
SUB = 256
TKD = 768
NK_ENC = -(-(NB * 176) // TK) * TK
NK_DEC = -(-(NB * 64) // TKD) * TKD
REST = 2 * TQ - DQ
FIRST_TILES = 2
LAST_TILES = (NQ_ENC - REST) // TQ - FIRST_TILES
THERE_ROWS = 2 * TQ + 48
BACK_ROWS = 2 * TQ + 32
NEG = -1e30
F32 = jnp.float32
BF16 = jnp.bfloat16
MIB = 1024 * 1024


def flip(head):
    return (head + 4) % 8


def lane_low(shape):
    return lax.broadcasted_iota(jnp.int32, shape, len(shape) - 1) < HD


def pair_up(first, second):
    low = lane_low(first.shape)
    even = jnp.where(low, first, pltpu.roll(second, HD, 1))
    odd = jnp.where(low, pltpu.roll(first, HD, 1), second)
    return even, odd


def pack_kernel(group_ref, enc_ref, dec_ref, q_in, k_in, v_in, g_in, x_out,
                q_ref, k_ref, v_ref, g_ref, kv_s, qg_s, x_ref, in_sem, out_sem):
    is_dec = group_ref[0] == 3
    arrays = ((k_in, k_ref), (v_in, v_ref), (q_in, q_ref), (g_in, g_ref))
    fetches = [
        [
            pltpu.make_async_copy(src.at[:, pl.ds(pair * LANES, LANES)], dst.at[pair], in_sem.at[pair, i])
            for i, (src, dst) in enumerate(arrays)
        ]
        for pair in range(4)
    ]
    for some in fetches:
        for copy in some:
            copy.start()
    row = lax.broadcasted_iota(jnp.int32, (8, LANES), 0)
    enc_len, dec_len = enc_ref[0].astype(F32), dec_ref[0].astype(F32)
    tail = jnp.where(row == 6, enc_len, jnp.where(row == 7, dec_len, 0.0))

    def sent(pair):
        some = pl.ds(8 * pair, 8)
        return pltpu.make_async_copy(x_ref.at[some], x_out.at[some], out_sem.at[pair])

    for pair in range(4):
        for copy in fetches[pair]:
            copy.wait()
        even, odd = pair_up(k_ref[pair].astype(F32), v_ref[pair].astype(F32))
        kv_s[2 * pair], kv_s[2 * pair + 1] = even, odd
        even, odd = pair_up(q_ref[pair].astype(F32), g_ref[pair].astype(F32))
        qg_s[2 * pair], qg_s[2 * pair + 1] = even, odd

        @pl.when(jnp.logical_not(is_dec))
        def _():
            for head in (2 * pair, 2 * pair + 1):
                kv = kv_s[head]
                for part in range(4):
                    qg = qg_s[head, pl.ds(part * QTR, QTR), :]
                    x_ref[4 * head + part] = jnp.concatenate([kv, qg, tail[2:]], axis=0).astype(BF16)
            sent(pair).start()

    @pl.when(is_dec)
    def _():
        for head in range(8):
            for part in range(4):
                pieces = []
                for c in range(3):
                    src = flip(head) if c < 2 else head
                    pieces.append(kv_s[src, pl.ds(c, DTOK, stride=3), :])
                    pieces.append(qg_s[src, pl.ds(3 * part * DQTR + c, DQTR, stride=3), :])
                    pieces.append(tail[6:])
                x_ref[4 * head + part] = jnp.concatenate(pieces, axis=0).astype(BF16)
            if head % 2 == 1:
                sent(head // 2).start()

    for pair in range(4):
        sent(pair).wait()


def unpack_kernel(group_ref, w_ref, qo_ref, ko_ref, vo_ref, dq_s, dk_s, dv_s, tmp_s):
    is_dec = group_ref[0] == 3

    @pl.when(jnp.logical_not(is_dec))
    def _():
        for pair in range(4):
            cols = pl.ds(pair * LANES, LANES)
            sums = []
            for head in (2 * pair, 2 * pair + 1):
                total = None
                for part in range(4):
                    chunk = w_ref[4 * head + part].astype(F32)
                    total = chunk[:TOK] if total is None else total + chunk[:TOK]
                    dq = chunk[TOK:]
                    turned = pltpu.roll(dq, HD, 1)
                    first, second = (dq, turned) if head % 2 == 0 else (turned, dq)
                    base = part * QTR
                    if head % 2 == 0:
                        dq_s[pl.ds(base, 21), :] = first[:21]
                        dq_s[pl.ds(base + 21, 21), :] = second[:21]
                    else:
                        low = lane_low((21, LANES))
                        for start, value in ((base, first), (base + 21, second)):
                            old = dq_s[pl.ds(start, 21), :]
                            dq_s[pl.ds(start, 21), :] = jnp.where(low, old, value[:21])
                sums.append(total)
            low = lane_low((TOK, LANES))
            ko_ref[:, cols] = jnp.where(low, sums[0], pltpu.roll(sums[1], HD, 1))
            vo_ref[:, cols] = jnp.where(low, pltpu.roll(sums[0], HD, 1), sums[1])
            qo_ref[:, cols] = dq_s[...]

    @pl.when(is_dec)
    def _():
        for pair in range(4):
            cols = pl.ds(pair * LANES, LANES)
            for c in range(3):
                sums, dqs = [], []
                for head in (2 * pair, 2 * pair + 1):
                    place = flip(head) if c < 2 else head
                    total, pieces = None, []
                    for part in range(4):
                        chunk = w_ref[4 * place + part].astype(F32)[DOUT_ROWS * c : DOUT_ROWS * (c + 1)]
                        kv = chunk[:DTOK]
                        total = kv if total is None else total + kv
                        dq = chunk[DTOK:]
                        turned = pltpu.roll(dq, HD, 1)
                        pieces.append((dq, turned) if head % 2 == 0 else (turned, dq))
                    sums.append(total)
                    dqs.append(pieces)
                low = lane_low((DTOK, LANES))
                rows = pl.ds(c, DTOK, stride=3)
                dk_s[rows, :] = jnp.where(low, sums[0], pltpu.roll(sums[1], HD, 1))
                dv_s[rows, :] = jnp.where(low, pltpu.roll(sums[0], HD, 1), sums[1])
                low = lane_low((8, LANES))
                for part in range(4):
                    for half in range(2):
                        value = jnp.where(low, dqs[0][part][half], dqs[1][part][half])
                        tmp_s[pl.ds(part * DQTR + half * 7, 7), :] = value[:7]
                dq_s[rows, :] = tmp_s[...]
            ko_ref[:, cols] = dk_s[...]
            vo_ref[:, cols] = dv_s[...]
            qo_ref[:, cols] = dq_s[...]


def fold(tile, op):
    parts = [tile[8 * i : 8 * i + 8] for i in range(tile.shape[0] // 8)]
    while len(parts) > 1:
        parts = [op(parts[i], parts[i + 1]) if i + 1 < len(parts) else parts[i] for i in range(0, len(parts), 2)]
    return parts[0]


def spread(stat, rows):
    return jnp.concatenate([stat] * (rows // 8), axis=0)


def tile_rows(kt, size):
    return pl.ds(pl.multiple_of(kt * size, size), size)


def place_block(kv_ref, ka_ref, block, offset, length):
    size = block.shape[0]
    row = lax.broadcasted_iota(jnp.int32, (size, LANES), 0)
    lane = lax.broadcasted_iota(jnp.int32, (size, LANES), 1)
    rows = pl.ds(pl.multiple_of(offset, 16), size)
    kv_ref[rows, :] = block
    bias = jnp.where(row < length, 0.0, NEG)
    ka_ref[rows, :] = jnp.where(lane == HD, bias, block.astype(F32)).astype(BF16)


def place_padding(kv_ref, ka_ref, offset, size):
    lane = lax.broadcasted_iota(jnp.int32, (size, LANES), 1)
    rows = pl.ds(pl.multiple_of(offset, 16), size)
    kv_ref[rows, :] = jnp.zeros((size, LANES), BF16)
    ka_ref[rows, :] = jnp.where(lane == HD, NEG, 0.0).astype(BF16)


def turn(keys):
    return keys.astype(F32).T[:HD].astype(BF16)


def read_lens(y_ref, wide_s, lens_s, sem):
    lane = lax.broadcasted_iota(jnp.int32, (8, LANES), 1)
    found = jnp.zeros((8, LANES), F32)
    for b in range(NB):
        found = jnp.where(lane == b, y_ref[b].astype(F32)[IN_ROWS - 8 :], found)
    wide_s[...] = found.astype(jnp.int32)
    copy = pltpu.make_async_copy(wide_s, lens_s, sem)
    copy.start()
    copy.wait()


def query_operands(qg):
    turned = qg.T
    sub = lax.broadcasted_iota(jnp.int32, (LANES, TQ), 0)
    q_t = jnp.where(sub < HD, turned * 0.125, jnp.where(sub == HD, 1.0, 0.0)).astype(BF16)
    d_t = jnp.where(sub < HD, 0.0, turned).astype(BF16)
    return q_t, d_t


def natural_operands(qg):
    low = lane_low((TQ, LANES))
    return jnp.where(low, qg, 0.0).astype(BF16), jnp.where(low, 0.0, qg).astype(BF16)


def score_sums(found, running):
    s, dprob = found
    peak, norm, inner = running
    new_peak = jnp.maximum(peak, fold(s, jnp.maximum))
    prob = jnp.exp(s - spread(new_peak, s.shape[0]))
    shrink = jnp.exp(peak - new_peak)
    norm = norm * shrink + fold(prob, jnp.add)
    inner = inner * shrink + fold(prob * dprob, jnp.add)
    return new_peak, norm, inner


def merged(running):
    peak8, norm8, inner8 = running
    peak = jnp.max(peak8, axis=0, keepdims=True)
    shrink = jnp.exp(peak8 - peak)
    norm = jnp.sum(norm8 * shrink, axis=0, keepdims=True)
    inner = jnp.sum(inner8 * shrink, axis=0, keepdims=True)
    return peak, norm, inner


def no_moments():
    zero = jnp.zeros((8, TQ), F32)
    return jnp.full((8, TQ), NEG, F32), zero, zero


def grad_parts(s, dprob, total, delta):
    prob = jnp.exp(s - total)
    dscore = (prob * (dprob - delta)).astype(BF16)
    return prob.astype(BF16), dscore


def key_grads(parts, naturals):
    prob, dscore = parts
    q_nat, d_nat = naturals
    return jnp.dot(dscore, q_nat, preferred_element_type=F32) + jnp.dot(
        prob, d_nat, preferred_element_type=F32
    )


def both_halves(dq_t):
    dq_t = dq_t * 0.125
    return jnp.concatenate([dq_t, dq_t], axis=0).T


def write_split(ref, first_row, value):
    for term in range(3):
        low = value.astype(BF16).astype(F32)
        value = value - low
        for half in range(2):
            ref[pl.ds(first_row + 4 * term + half, 1), :] = low[:, half * LANES : (half + 1) * LANES]


def read_split(rows, first_row):
    total = None
    for term in (2, 1, 0):
        at = first_row + 4 * term
        piece = jnp.concatenate([rows[at : at + 1], rows[at + 1 : at + 2]], axis=1)
        total = piece if total is None else total + piece
    return total


def sweep(count, tiles, refs, query, start, emit, arrive, ready, leave):
    kv_ref, ka_ref, kt_ref, acc_ref, s_pair, dp_pair = refs

    def tile_step(kt, slot, now, then, dq_t, running):
        found = None
        for j in range(TK // SUB):
            rows = pl.ds(pl.multiple_of(kt * TK + j * SUB, SUB), SUB)
            fresh = None
            if then is not None:
                q_t, d_t = then
                fresh = (
                    jnp.dot(ka_ref[rows, :], q_t, preferred_element_type=F32),
                    jnp.dot(kv_ref[rows, :], d_t, preferred_element_type=F32),
                )
                s_pair[1 - slot][rows, :], dp_pair[1 - slot][rows, :] = fresh
            if now is not None:
                naturals, total, delta = now
                parts = grad_parts(s_pair[slot][rows, :], dp_pair[slot][rows, :], total, delta)
            if found is not None:
                running = score_sums(found, running)
            if now is not None:
                acc_ref[rows, :] += key_grads(parts, naturals)
                keys = kt_ref[kt, :, j * SUB : (j + 1) * SUB]
                dq_t = dq_t + jnp.dot(keys, parts[1], preferred_element_type=F32)
            found = fresh
        if found is not None:
            running = score_sums(found, running)
        return dq_t, running

    def run(slot, now, then, running):
        def step(kt, carry):
            if now is None:
                arrive(kt)
            carry = tile_step(kt, slot, now, then, *carry)
            if then is None:
                leave(kt)
            return carry

        return lax.fori_loop(0, tiles, step, (jnp.zeros((HD, TQ), F32), running))

    _, running = run(1, None, query_operands(query(0)), start(0))
    ready()
    for t in range(count):
        peak, norm, inner = merged(running)
        total, delta = peak + jnp.log(norm), inner / norm
        now = natural_operands(query(t)), total, delta
        if t == count - 1:
            dq_t, _ = run(t % 2, now, None, no_moments())
        else:
            dq_t, running = run(t % 2, now, query_operands(query(t + 1)), start(t + 1))
        emit(t, dq_t, total, delta)


def tile_copy(src_ref, dst_ref, sem, kt):
    rows = tile_rows(kt, TK)
    return pltpu.make_async_copy(src_ref.at[rows, :], dst_ref.at[rows, :], sem.at[kt])


def enc_first_kernel(group_ref, y_ref, kv_ref, ka_ref, kt_ref, qg_ref, acc_ref, dq_ref, meta_ref,
                     kv_s, ka_s, kt_s, qg_s, acc_s, dq_s, s0_s, s1_s, dp0_s, dp1_s,
                     acc_sem, sems, wide_s, lens_s, sem):
    @pl.when(group_ref[0] < 3)
    def _():
        read_lens(y_ref, wide_s, lens_s, sem)

        def block(b, offset):
            length = lens_s[6, b]
            meta_ref[b] = offset
            meta_ref[NB + b] = length
            place_block(kv_s, ka_s, y_ref[b, 0:176, :], offset, length)
            return offset + ((length + 15) // 16) * 16

        end = lax.fori_loop(0, NB, block, jnp.int32(0))
        place_padding(kv_s, ka_s, end, TK)
        tiles = (end + TK - 1) // TK
        meta_ref[2 * NB] = tiles
        for b in range(NB):
            qg_s[pl.ds(QTR * b, 48), :] = y_ref[b].astype(F32)[TOK:]

        def arrive(kt):
            kt_s[kt] = turn(kv_s[tile_rows(kt, TK), :])
            acc_s[tile_rows(kt, TK), :] = jnp.zeros((TK, LANES), F32)

        copies = [
            pltpu.make_async_copy(src, dst, sems.at[i])
            for i, (src, dst) in enumerate(
                ((kv_s, kv_ref), (ka_s, ka_ref), (qg_s, qg_ref), (kt_s, kt_ref), (dq_s, dq_ref)))
        ]
        for copy in copies[:3]:
            copy.start()

        def emit(t, dq_t, total, delta):
            dq_s[pl.ds(t * TQ, TQ), :] = both_halves(dq_t)

        sweep(FIRST_TILES, tiles, (kv_s, ka_s, kt_s, acc_s, (s0_s, s1_s), (dp0_s, dp1_s)),
              lambda t: qg_s[pl.ds(t * TQ, TQ), :], lambda t: no_moments(), emit,
              arrive, copies[3].start, lambda kt: tile_copy(acc_s, acc_ref, acc_sem, kt).start())
        copies[4].start()
        for copy in copies:
            copy.wait()

        @pl.loop(0, tiles)
        def _(kt):
            tile_copy(acc_s, acc_ref, acc_sem, kt).wait()


def fetch_keys(tiles, kv, ka, kt_all, acc, kt_sem):
    @pl.loop(0, tiles)
    def _(kt):
        tile_copy(*kv, kt).start()
        tile_copy(*ka, kt).start()

    kt_copy = pltpu.make_async_copy(*kt_all, kt_sem)
    kt_copy.start()

    @pl.loop(0, tiles)
    def _(kt):
        tile_copy(*acc, kt).start()

    def arrive(kt):
        tile_copy(*kv, kt).wait()
        tile_copy(*ka, kt).wait()

    def ready():
        kt_copy.wait()

        @pl.loop(0, tiles)
        def _(kt):
            tile_copy(*acc, kt).wait()

    return arrive, ready


def enc_dec_kernel(group_ref, meta_ref, kv_ref, ka_ref, kt_ref, qg_ref, acc1_ref, m0_ref, m1_ref, m2_ref,
                   acc_ref, dq_ref, back_ref, kv_s, ka_s, kt_s, acc_s, s0_s, s1_s, dp0_s, dp1_s,
                   own_s, got_s, stat_s, kv_sem, ka_sem, acc_sem, out_sem, sems):
    group = group_ref[0]

    @pl.when(group < 3)
    def _():
        for c, m_ref in enumerate((m0_ref, m1_ref, m2_ref)):
            @pl.when(group == c)
            def _():
                pltpu.make_async_copy(m_ref, got_s, sems.at[0]).start()

        rest = pltpu.make_async_copy(
            qg_ref.at[pl.ds(NQ_ENC - REST, REST), :], own_s.at[pl.ds(DQ, REST), :], sems.at[1])
        rest.start()
        tiles = meta_ref[2 * NB]
        arrive, ready = fetch_keys(tiles, (kv_ref, kv_s, kv_sem), (ka_ref, ka_s, ka_sem), (kt_ref, kt_s),
                                   (acc1_ref, acc_s, acc_sem), sems.at[2])
        pltpu.make_async_copy(m0_ref, got_s, sems.at[0]).wait()
        got = got_s[...].astype(F32)
        own_s[pl.ds(0, DQ), :] = got[:DQ]
        stats = got[2 * TQ :]
        rest.wait()

        def start(t):
            row = lax.broadcasted_iota(jnp.int32, (8, TQ), 0)
            peak, norm, inner = (read_split(stats, 12 * k + 2 * t) for k in range(3))
            return (jnp.where(row == 0, peak, NEG), jnp.where(row == 0, norm, 0.0),
                    jnp.where(row == 0, inner, 0.0))

        stat_s[...] = jnp.zeros_like(stat_s)

        def emit(t, dq_t, total, delta):
            dq = both_halves(dq_t)
            back_ref[pl.ds(t * TQ, TQ), :] = dq.astype(BF16)
            write_split(stat_s, 2 * t, total)
            write_split(stat_s, 12 + 2 * t, delta)
            if t == 1:
                dq_ref[...] = dq[TQ - REST :]

        sweep(2, tiles, (kv_s, ka_s, kt_s, acc_s, (s0_s, s1_s), (dp0_s, dp1_s)),
              lambda t: own_s[pl.ds(t * TQ, TQ), :], start, emit,
              arrive, ready, lambda kt: tile_copy(acc_s, acc_ref, out_sem, kt).start())
        back_ref[pl.ds(2 * TQ, BACK_ROWS - 2 * TQ), :] = stat_s[...].astype(BF16)

        @pl.loop(0, tiles)
        def _(kt):
            tile_copy(acc_s, acc_ref, out_sem, kt).wait()


def enc_last_kernel(group_ref, meta_ref, kv_ref, ka_ref, kt_ref, qg_ref, acc2_ref, dq1_ref, dq2_ref,
                    o_ref, same_ref, kv_s, ka_s, kt_s, acc_s, s0_s, s1_s, dp0_s, dp1_s,
                    qg_s, dq_s, out_s, kv_sem, ka_sem, acc_sem, out_sem, sems):
    @pl.when(group_ref[0] < 3)
    def _():
        tiles = meta_ref[2 * NB]
        own = pltpu.make_async_copy(
            qg_ref.at[pl.ds(FIRST_TILES * TQ, LAST_TILES * TQ), :], qg_s, sems.at[0])
        own.start()
        arrive, ready = fetch_keys(tiles, (kv_ref, kv_s, kv_sem), (ka_ref, ka_s, ka_sem), (kt_ref, kt_s),
                                   (acc2_ref, acc_s, acc_sem), sems.at[1])
        early = [
            pltpu.make_async_copy(dq1_ref, dq_s.at[pl.ds(0, FIRST_TILES * TQ), :], sems.at[2]),
            pltpu.make_async_copy(dq2_ref, dq_s.at[pl.ds(NQ_ENC - REST, REST), :], sems.at[3]),
        ]
        for copy in early:
            copy.start()
        dq_s[pl.ds(NQ_ENC, 8), :] = jnp.zeros((8, LANES), F32)
        own.wait()

        def emit(t, dq_t, total, delta):
            dq_s[pl.ds((FIRST_TILES + t) * TQ, TQ), :] = both_halves(dq_t)

        sweep(LAST_TILES, tiles, (kv_s, ka_s, kt_s, acc_s, (s0_s, s1_s), (dp0_s, dp1_s)),
              lambda t: qg_s[pl.ds(t * TQ, TQ), :], lambda t: no_moments(), emit,
              arrive, ready, lambda kt: None)
        for copy in early:
            copy.wait()
        row = lax.broadcasted_iota(jnp.int32, (TOK, LANES), 0)
        low = lane_low((TOK, LANES))
        copies = []
        for b in range(NB):
            grad = acc_s[pl.ds(pl.multiple_of(meta_ref[b], 16), TOK), :]
            grad = jnp.where(row < meta_ref[NB + b], jnp.where(low, grad * 0.125, grad), 0.0)
            base = QTR * b
            dq = jnp.where(lane_low((24, LANES)), dq_s[pl.ds(base, 24), :], dq_s[pl.ds(base + 21, 24), :])
            out_s[b] = jnp.concatenate([grad, dq], axis=0).astype(BF16)
            if b % 8 == 7:
                some = pl.ds(b - 7, 8)
                copies.append(pltpu.make_async_copy(out_s.at[some], o_ref.at[some], out_sem.at[b // 8]))
                copies[-1].start()
        for copy in copies:
            copy.wait()


def dec_query_pos(t, part):
    q_id = t * TQ + lax.broadcasted_iota(jnp.int32, (1, TQ), 1)
    place = (q_id // DQTR) * DTOK + part * DQTR + q_id % DQTR
    return jnp.where(q_id < DQ, place, -1).astype(F32)


def dec_scores(kv_ref, ka_ref, pos_ref, c, rows, operands, q_at):
    q_t, d_t = operands
    s = jnp.dot(ka_ref[c, rows, :], q_t, preferred_element_type=F32)
    dprob = jnp.dot(kv_ref[c, rows, :], d_t, preferred_element_type=F32)
    k_at = pos_ref[rows, :]
    return jnp.where(jnp.concatenate([k_at, k_at], axis=1) <= q_at, s, NEG), dprob


def put_pos(pos_ref, offset, b):
    row = lax.broadcasted_iota(jnp.int32, (64, LANES), 0)
    pos_ref[pl.ds(pl.multiple_of(offset, 16), 64), :] = (row + b * DTOK).astype(F32)


def dec_units(kt):
    return [
        (pl.ds(pl.multiple_of(kt * TKD + j * SUB, SUB), SUB), t) for j in range(TKD // SUB) for t in range(2)
    ]


def dec_first_kernel(group_ref, part_ref, held_ref, kv_out, ka_out, kt_out, m0_out, m1_out, m2_out, meta_ref,
                     y_ref, kv_ref, ka_ref, kt_ref, pos_ref, m_ref, qg_s, stat_s, sems, wide_s, lens_s, sem):
    @pl.when(group_ref[0] == 3)
    def _():
        fetch = pltpu.make_async_copy(held_ref, y_ref, sems.at[0])
        fetch.start()
        fetch.wait()
        read_lens(y_ref, wide_s, lens_s, sem)

        def block(b, offset):
            length = lens_s[7, b]
            meta_ref[b] = offset
            meta_ref[NB + b] = length
            chunk = y_ref[b].astype(F32)
            for c in range(3):
                keys = chunk[DIN_ROWS * c : DIN_ROWS * c + 64].astype(BF16)
                place_block(kv_ref.at[c], ka_ref.at[c], keys, offset, length)
            put_pos(pos_ref, offset, b)
            return offset + ((length + 15) // 16) * 16

        end = lax.fori_loop(0, NB, block, jnp.int32(0))
        for c in range(3):
            place_padding(kv_ref.at[c], ka_ref.at[c], end, TKD)
        tiles = (end + TKD - 1) // TKD
        meta_ref[2 * NB] = tiles
        for b in range(NB):
            chunk = y_ref[b].astype(F32)
            for c in range(3):
                qg_s[c, pl.ds(DQTR * b, 16), :] = chunk[DIN_ROWS * c + DTOK : DIN_ROWS * (c + 1)]
        part = part_ref[0]
        stat_s[...] = jnp.zeros_like(stat_s)
        for c in range(3):
            qg_s[c, pl.ds(DQ, REST), :] = jnp.zeros((REST, LANES), F32)
            m_ref[c, pl.ds(0, 2 * TQ), :] = qg_s[c].astype(BF16)

            @pl.loop(0, tiles)
            def _(kt):
                kt_ref[c, kt] = turn(kv_ref[c, tile_rows(kt, TKD), :])

        copies = [
            pltpu.make_async_copy(src, dst, sems.at[1 + i])
            for i, (src, dst) in enumerate(
                ((kv_ref, kv_out), (ka_ref, ka_out), (kt_ref, kt_out)))
        ]
        for copy in copies:
            copy.start()
        for c, out in enumerate((m0_out, m1_out, m2_out)):
            operands = [query_operands(qg_s[c, pl.ds(t * TQ, TQ), :]) for t in range(2)]
            q_at = [dec_query_pos(t, part) for t in range(2)]

            def step(kt, carry):
                carry = list(carry)
                units = dec_units(kt)
                ahead = lambda u: dec_scores(kv_ref, ka_ref, pos_ref, c, units[u][0], operands[units[u][1]], q_at[units[u][1]])
                found = ahead(0)
                for u, (rows, t) in enumerate(units):
                    fresh = ahead(u + 1) if u + 1 < len(units) else None
                    carry[t] = score_sums(found, carry[t])
                    found = fresh
                return tuple(carry)

            found = lax.fori_loop(0, tiles, step, (no_moments(), no_moments()))
            for t in range(2):
                q_id = t * TQ + lax.broadcasted_iota(jnp.int32, (1, TQ), 1)
                for k, value in enumerate(merged(found[t])):
                    write_split(stat_s, 12 * k + 2 * t, jnp.where(q_id < DQ, value, NEG if k == 0 else 0.0))
            m_ref[c, pl.ds(2 * TQ, THERE_ROWS - 2 * TQ), :] = stat_s[...].astype(BF16)
            copies.append(pltpu.make_async_copy(m_ref.at[c], out, sems.at[4 + c]))
            copies[-1].start()
        for copy in copies:
            copy.wait()


def dec_last_kernel(group_ref, part_ref, meta_ref, kv_in, ka_in, kt_in, m0_in, m1_in, m2_in, b0_in, b1_in, b2_in, enc_ref,
                    o_ref, kv_ref, ka_ref, kt_ref, pos_ref, m_ref, back_ref, acc_s, dq_s, out_s, sems, sem):
    @pl.when(group_ref[0] == 3)
    def _():
        tiles = meta_ref[2 * NB]
        part = part_ref[0]
        fetches = [
            [
                pltpu.make_async_copy(src, dst.at[c], sems.at[c, i])
                for i, (src, dst) in enumerate(
                    ((m_in, m_ref), (b_in, back_ref), (kv_in.at[c], kv_ref), (ka_in.at[c], ka_ref), (kt_in.at[c], kt_ref)))
            ]
            for c, (m_in, b_in) in enumerate(((m0_in, b0_in), (m1_in, b1_in), (m2_in, b2_in)))
        ]
        for some in fetches:
            for copy in some:
                copy.start()

        @pl.loop(0, NB)
        def _(b):
            put_pos(pos_ref, meta_ref[b], b)

        for c in range(3):
            for copy in fetches[c]:
                copy.wait()
            qg = m_ref[c, pl.ds(0, 2 * TQ), :].astype(F32)
            back = back_ref[c].astype(F32)
            stats = back[2 * TQ :]
            cut = [qg[t * TQ : (t + 1) * TQ] for t in range(2)]
            operands = [query_operands(cut[t]) for t in range(2)]
            naturals = [natural_operands(cut[t]) for t in range(2)]
            q_at = [dec_query_pos(t, part) for t in range(2)]
            total = [read_split(stats, 2 * t) for t in range(2)]
            delta = [read_split(stats, 12 + 2 * t) for t in range(2)]

            def step(kt, dqs):
                dqs = list(dqs)
                units = dec_units(kt)
                ahead = lambda u: dec_scores(kv_ref, ka_ref, pos_ref, c, units[u][0], operands[units[u][1]], q_at[units[u][1]])
                found = ahead(0)
                for u, (rows, t) in enumerate(units):
                    fresh = ahead(u + 1) if u + 1 < len(units) else None
                    parts = grad_parts(*found, total[t], delta[t])
                    grad = key_grads(parts, naturals[t])
                    acc_s[rows, :] = grad if t == 0 else acc_s[rows, :] + grad
                    keys = kt_ref[c, kt, :, u // 2 * SUB : (u // 2 + 1) * SUB]
                    dqs[t] = dqs[t] + jnp.dot(keys, parts[1], preferred_element_type=F32)
                    found = fresh
                return tuple(dqs)

            none = jnp.zeros((HD, TQ), F32)
            dqs = lax.fori_loop(0, tiles, step, (none, none))
            for t in range(2):
                rows = pl.ds(t * TQ, TQ)
                dq_s[rows, :] = both_halves(dqs[t]) + back[t * TQ : (t + 1) * TQ]
            row = lax.broadcasted_iota(jnp.int32, (DTOK, LANES), 0)
            low = lane_low((DTOK, LANES))
            for b in range(NB):
                grad = acc_s[pl.ds(pl.multiple_of(meta_ref[b], 16), DTOK), :]
                grad = jnp.where(row < meta_ref[NB + b], jnp.where(low, grad * 0.125, grad), 0.0)
                base = DQTR * b
                dq = jnp.where(lane_low((8, LANES)), dq_s[pl.ds(base, 8), :], dq_s[pl.ds(base + 7, 8), :])
                out_s[b, pl.ds(DOUT_ROWS * c, DOUT_ROWS), :] = jnp.concatenate([grad, dq], axis=0).astype(BF16)
        copy = pltpu.make_async_copy(out_s, o_ref, sem)
        copy.start()
        copy.wait()


SMEM = pl.BlockSpec(memory_space=pltpu.SMEM)
VMEM = pl.BlockSpec(memory_space=pltpu.VMEM)
ANY = pl.BlockSpec(memory_space=pl.ANY)


def limit(mib):
    return pltpu.CompilerParams(vmem_limit_bytes=mib * MIB)


def shaped(shape, dtype):
    return jax.ShapeDtypeStruct(shape, dtype)


def lens_scratch():
    return [
        pltpu.VMEM((8, LANES), jnp.int32),
        pltpu.SMEM((8, LANES), jnp.int32),
        pltpu.SemaphoreType.DMA(()),
    ]


def key_scratch():
    return [
        pltpu.VMEM((NK_ENC + TK, LANES), BF16),
        pltpu.VMEM((NK_ENC + TK, LANES), BF16),
        pltpu.VMEM((NK_ENC // TK, HD, TK), BF16),
    ]


def score_scratch():
    return [pltpu.VMEM((NK_ENC, LANES), F32)] + [pltpu.VMEM((NK_ENC, TQ), F32)] * 4


def dma(*shape):
    return pltpu.SemaphoreType.DMA(shape)


META = shaped((2 * NB + 8,), jnp.int32)
ENC_TILES = NK_ENC // TK


def dec_first(group, part, held):
    keys = [((3, NK_DEC + TKD, LANES), BF16), ((3, NK_DEC + TKD, LANES), BF16),
            ((3, NK_DEC // TKD, HD, TKD), BF16)]
    pos = ((NK_DEC + TKD, LANES), F32)
    return pl.pallas_call(
        dec_first_kernel,
        out_shape=[shaped(*k) for k in keys] + [shaped((THERE_ROWS, LANES), BF16)] * 3 + [META],
        in_specs=[SMEM, SMEM, ANY],
        out_specs=[ANY] * 6 + [SMEM],
        scratch_shapes=[pltpu.VMEM(held.shape, BF16)] + [pltpu.VMEM(*k) for k in keys + [pos]] + [
            pltpu.VMEM((3, THERE_ROWS, LANES), BF16),
            pltpu.VMEM((3, 2 * TQ, LANES), F32),
            pltpu.VMEM((THERE_ROWS - 2 * TQ, LANES), F32),
            dma(8),
        ] + lens_scratch(),
        compiler_params=limit(24),
    )(group, part, held)


def enc_first(group, held):
    return pl.pallas_call(
        enc_first_kernel,
        out_shape=[
            shaped((NK_ENC + TK, LANES), BF16),
            shaped((NK_ENC + TK, LANES), BF16),
            shaped((ENC_TILES, HD, TK), BF16),
            shaped((NQ_ENC + 8, LANES), F32),
            shaped((NK_ENC, LANES), F32),
            shaped((FIRST_TILES * TQ, LANES), F32),
            META,
        ],
        in_specs=[SMEM, VMEM],
        out_specs=[ANY] * 6 + [SMEM],
        scratch_shapes=key_scratch() + [
            pltpu.VMEM((NQ_ENC + 8, LANES), F32),
            score_scratch()[0],
            pltpu.VMEM((FIRST_TILES * TQ, LANES), F32),
        ] + score_scratch()[1:] + [dma(ENC_TILES), dma(5)] + lens_scratch(),
        compiler_params=limit(38),
    )(group, held)


def enc_dec(group, meta, keys, acc, messages):
    return pl.pallas_call(
        enc_dec_kernel,
        out_shape=[
            shaped((NK_ENC, LANES), F32),
            shaped((REST, LANES), F32),
            shaped((BACK_ROWS, LANES), BF16),
        ],
        in_specs=[SMEM, SMEM] + [ANY] * 8,
        out_specs=[ANY, VMEM, VMEM],
        scratch_shapes=key_scratch() + score_scratch() + [
            pltpu.VMEM((2 * TQ, LANES), F32),
            pltpu.VMEM((THERE_ROWS, LANES), BF16),
            pltpu.VMEM((BACK_ROWS - 2 * TQ, LANES), F32),
            dma(ENC_TILES), dma(ENC_TILES), dma(ENC_TILES), dma(ENC_TILES), dma(3),
        ],
        input_output_aliases={6: 0},
        compiler_params=limit(38),
    )(group, meta, *keys, acc, *messages)


def enc_last(group, meta, keys, acc, dqs):
    return pl.pallas_call(
        enc_last_kernel,
        out_shape=[shaped((NB, OUT_ROWS, LANES), BF16), shaped(acc.shape, F32)],
        in_specs=[SMEM, SMEM] + [ANY] * 7,
        out_specs=[ANY, ANY],
        scratch_shapes=key_scratch() + score_scratch() + [
            pltpu.VMEM((LAST_TILES * TQ, LANES), F32),
            pltpu.VMEM((NQ_ENC + 8, LANES), F32),
            pltpu.VMEM((NB, OUT_ROWS, LANES), BF16),
            dma(ENC_TILES), dma(ENC_TILES), dma(ENC_TILES), dma(4), dma(4),
        ],
        input_output_aliases={6: 1},
        compiler_params=limit(38),
    )(group, meta, *keys, acc, *dqs)[0]


def dec_last(group, part, meta, keys, messages, back, enc_out):
    return pl.pallas_call(
        dec_last_kernel,
        out_shape=shaped((NB, OUT_ROWS, LANES), BF16),
        in_specs=[SMEM, SMEM, SMEM] + [ANY] * 10,
        out_specs=ANY,
        scratch_shapes=[pltpu.VMEM(k.shape, k.dtype) for k in keys] + [
            pltpu.VMEM((NK_DEC + TKD, LANES), F32),
            pltpu.VMEM((3, THERE_ROWS, LANES), BF16),
            pltpu.VMEM((3, BACK_ROWS, LANES), BF16),
            pltpu.VMEM((NK_DEC + TKD, LANES), F32),
            pltpu.VMEM((2 * TQ, LANES), F32),
            pltpu.VMEM((NB, OUT_ROWS, LANES), BF16),
            dma(3, 5), dma(),
        ],
        input_output_aliases={12: 0},
        compiler_params=limit(24),
    )(group, part, meta, *keys, *messages, *back, enc_out)


def on_device(queries, key_rows, value_rows, out_grad, enc_lengths, dec_lengths):
    group = lax.axis_index("grp").astype(jnp.int32).reshape(1)
    part = (lax.axis_index("blk") % 4).astype(jnp.int32).reshape(1)
    chunks = pl.pallas_call(
        pack_kernel,
        out_shape=shaped((NB, IN_ROWS, LANES), BF16),
        in_specs=[SMEM, SMEM, SMEM, ANY, ANY, ANY, ANY],
        out_specs=ANY,
        scratch_shapes=[pltpu.VMEM((4, TOK, LANES), BF16)] * 4 + [pltpu.VMEM((8, TOK, LANES), F32)] * 2 + [
            pltpu.VMEM((NB, IN_ROWS, LANES), BF16), dma(4, 4), dma(4)],
        compiler_params=limit(62),
    )(group, enc_lengths, dec_lengths, queries, key_rows, value_rows, out_grad)
    held = lax.all_to_all(chunks, "blk", 0, 0, tiled=True)

    def partner(c, blk):
        return (blk + 16) % NB if c < 2 else blk

    there = [[(3 * NB + s, c * NB + partner(c, s)) for s in range(NB)] for c in range(3)]
    *dec_keys, m0, m1, m2, dec_meta = dec_first(group, part, held)
    messages = (m0, m1, m2)
    got = [lax.ppermute(messages[c], ("grp", "blk"), there[c]) for c in range(3)]
    *enc_keys, acc1, dq1, enc_meta = enc_first(group, held)
    acc2, dq2, answer = enc_dec(group, enc_meta, enc_keys, acc1, got)
    back = [lax.ppermute(answer, ("grp", "blk"), [(d, s) for s, d in there[c]]) for c in range(3)]
    enc_out = enc_last(group, enc_meta, enc_keys, acc2, (dq1, dq2))
    final = dec_last(group, part, dec_meta, dec_keys, messages, back, enc_out)
    final = lax.all_to_all(final, "blk", 0, 0, tiled=True)
    out = shaped(queries.shape, F32)
    return pl.pallas_call(
        unpack_kernel,
        out_shape=[out, out, out],
        in_specs=[SMEM, VMEM],
        out_specs=[VMEM, VMEM, VMEM],
        scratch_shapes=[pltpu.VMEM((TOK, LANES), F32)] * 3 + [pltpu.VMEM((DTOK, LANES), F32)],
        compiler_params=limit(10),
    )(group, final)


def solution(mesh):
    rows = P("blk", "grp")
    return jax.shard_map(
        on_device,
        mesh=mesh,
        in_specs=(rows, rows, rows, rows, P("blk"), P("blk")),
        out_specs=(rows, rows, rows),
        check_vma=False,
    )
```

```python
import functools

import jax
import jax.numpy as jnp
from jax import lax
from jax.experimental import pallas as pl
from jax.experimental.pallas import tpu as pltpu
from jax.sharding import PartitionSpec as P

HD = 64
LANES = 128
NB = 32
TOK = 168
DTOK = 56
QTR = TOK // 4
DQTR = DTOK // 4
IN_ROWS = 216
DIN_ROWS = 72
OUT_ROWS = 192
DOUT_ROWS = 64
NQ_ENC = NB * QTR
DQ = NB * DQTR
TQ = 256
TK = 2048
SUB = 256
TKD = 768
NK_ENC = -(-(NB * 176) // TK) * TK
NK_DEC = -(-(NB * 64) // TKD) * TKD
REST = 2 * TQ - DQ
FIRST_TILES = 3
LAST_TILES = (NQ_ENC - REST) // TQ - FIRST_TILES
THERE_ROWS = 2 * TQ + 48
BACK_ROWS = 2 * TQ + 32
NEG = -1e30
F32 = jnp.float32
BF16 = jnp.bfloat16
MIB = 1024 * 1024


def flip(head):
    return (head + 4) % 8


def lane_low(shape):
    return lax.broadcasted_iota(jnp.int32, shape, len(shape) - 1) < HD


def pair_up(first, second):
    low = lane_low(first.shape)
    even = jnp.where(low, first, pltpu.roll(second, HD, 1))
    odd = jnp.where(low, pltpu.roll(first, HD, 1), second)
    return even, odd


def pack_kernel(group_ref, part_ref, enc_ref, dec_ref, q_in, k_in, v_in, g_in, x_out,
                q_ref, k_ref, v_ref, g_ref, kv_s, qg_s, x_ref, in_sem, out_sem):
    is_dec = group_ref[0] == 3
    arrays = ((k_in, k_ref), (v_in, v_ref), (q_in, q_ref), (g_in, g_ref))
    fetches = [
        [
            pltpu.make_async_copy(src.at[:, pl.ds(pair * LANES, LANES)], dst.at[pair], in_sem.at[pair, i])
            for i, (src, dst) in enumerate(arrays)
        ]
        for pair in range(4)
    ]
    for some in fetches:
        for copy in some:
            copy.start()
    row = lax.broadcasted_iota(jnp.int32, (8, LANES), 0)
    enc_len, dec_len = enc_ref[0].astype(F32), dec_ref[0].astype(F32)
    tail = jnp.where(row == 6, enc_len, jnp.where(row == 7, dec_len, 0.0))

    def sent(pair):
        some = pl.ds(8 * pair, 8)
        return pltpu.make_async_copy(x_ref.at[some], x_out.at[some], out_sem.at[pair])

    for pair in range(4):
        for copy in fetches[pair]:
            copy.wait()
        even, odd = pair_up(k_ref[pair].astype(F32), v_ref[pair].astype(F32))
        kv_s[2 * pair], kv_s[2 * pair + 1] = even, odd
        even, odd = pair_up(q_ref[pair].astype(F32), g_ref[pair].astype(F32))
        qg_s[2 * pair], qg_s[2 * pair + 1] = even, odd

        @pl.when(jnp.logical_not(is_dec))
        def _():
            for head in (2 * pair, 2 * pair + 1):
                kv = kv_s[head]
                for part in range(4):
                    qg = qg_s[head, pl.ds(part * QTR, QTR), :]
                    x_ref[4 * head + part] = jnp.concatenate([kv, qg, tail[2:]], axis=0).astype(BF16)
            sent(pair).start()

    @pl.when(is_dec)
    def _():
        for head in range(8):
            for part in range(4):
                pieces = []
                for c in range(3):
                    src = flip(head) if c < 2 else head
                    pieces.append(kv_s[src, pl.ds(c, DTOK, stride=3), :])
                    pieces.append(qg_s[src, pl.ds(3 * part * DQTR + c, DQTR, stride=3), :])
                    pieces.append(tail[6:])
                x_ref[4 * head + part] = jnp.concatenate(pieces, axis=0).astype(BF16)
            if head % 2 == 1:
                sent(head // 2).start()

    for pair in range(4):
        sent(pair).wait()


def unpack_kernel(group_ref, w_ref, qo_ref, ko_ref, vo_ref, dq_s, dk_s, dv_s, tmp_s):
    is_dec = group_ref[0] == 3

    @pl.when(jnp.logical_not(is_dec))
    def _():
        for pair in range(4):
            cols = pl.ds(pair * LANES, LANES)
            sums = []
            for head in (2 * pair, 2 * pair + 1):
                total = None
                for part in range(4):
                    chunk = w_ref[4 * head + part].astype(F32)
                    total = chunk[:TOK] if total is None else total + chunk[:TOK]
                    dq = chunk[TOK:]
                    turned = pltpu.roll(dq, HD, 1)
                    first, second = (dq, turned) if head % 2 == 0 else (turned, dq)
                    base = part * QTR
                    if head % 2 == 0:
                        dq_s[pl.ds(base, 21), :] = first[:21]
                        dq_s[pl.ds(base + 21, 21), :] = second[:21]
                    else:
                        low = lane_low((21, LANES))
                        for start, value in ((base, first), (base + 21, second)):
                            old = dq_s[pl.ds(start, 21), :]
                            dq_s[pl.ds(start, 21), :] = jnp.where(low, old, value[:21])
                sums.append(total)
            low = lane_low((TOK, LANES))
            ko_ref[:, cols] = jnp.where(low, sums[0], pltpu.roll(sums[1], HD, 1))
            vo_ref[:, cols] = jnp.where(low, pltpu.roll(sums[0], HD, 1), sums[1])
            qo_ref[:, cols] = dq_s[...]

    @pl.when(is_dec)
    def _():
        for pair in range(4):
            cols = pl.ds(pair * LANES, LANES)
            for c in range(3):
                sums, dqs = [], []
                for head in (2 * pair, 2 * pair + 1):
                    place = flip(head) if c < 2 else head
                    total, pieces = None, []
                    for part in range(4):
                        chunk = w_ref[4 * place + part].astype(F32)[DOUT_ROWS * c : DOUT_ROWS * (c + 1)]
                        kv = chunk[:DTOK]
                        total = kv if total is None else total + kv
                        dq = chunk[DTOK:]
                        turned = pltpu.roll(dq, HD, 1)
                        pieces.append((dq, turned) if head % 2 == 0 else (turned, dq))
                    sums.append(total)
                    dqs.append(pieces)
                low = lane_low((DTOK, LANES))
                rows = pl.ds(c, DTOK, stride=3)
                dk_s[rows, :] = jnp.where(low, sums[0], pltpu.roll(sums[1], HD, 1))
                dv_s[rows, :] = jnp.where(low, pltpu.roll(sums[0], HD, 1), sums[1])
                low = lane_low((8, LANES))
                for part in range(4):
                    for half in range(2):
                        value = jnp.where(low, dqs[0][part][half], dqs[1][part][half])
                        tmp_s[pl.ds(part * DQTR + half * 7, 7), :] = value[:7]
                dq_s[rows, :] = tmp_s[...]
            ko_ref[:, cols] = dk_s[...]
            vo_ref[:, cols] = dv_s[...]
            qo_ref[:, cols] = dq_s[...]


def fold(tile, op):
    parts = [tile[8 * i : 8 * i + 8] for i in range(tile.shape[0] // 8)]
    while len(parts) > 1:
        parts = [op(parts[i], parts[i + 1]) if i + 1 < len(parts) else parts[i] for i in range(0, len(parts), 2)]
    return parts[0]


def spread(stat, rows):
    return jnp.concatenate([stat] * (rows // 8), axis=0)


def tile_rows(kt, size):
    return pl.ds(pl.multiple_of(kt * size, size), size)


def place_block(kv_ref, ka_ref, block, offset, length):
    size = block.shape[0]
    row = lax.broadcasted_iota(jnp.int32, (size, LANES), 0)
    lane = lax.broadcasted_iota(jnp.int32, (size, LANES), 1)
    rows = pl.ds(pl.multiple_of(offset, 16), size)
    kv_ref[rows, :] = block
    bias = jnp.where(row < length, 0.0, NEG)
    ka_ref[rows, :] = jnp.where(lane == HD, bias, block.astype(F32)).astype(BF16)


def place_padding(kv_ref, ka_ref, offset, size):
    lane = lax.broadcasted_iota(jnp.int32, (size, LANES), 1)
    rows = pl.ds(pl.multiple_of(offset, 16), size)
    kv_ref[rows, :] = jnp.zeros((size, LANES), BF16)
    ka_ref[rows, :] = jnp.where(lane == HD, NEG, 0.0).astype(BF16)


def turn(keys):
    return keys.astype(F32).T[:HD].astype(BF16)


def read_lens(y_ref, wide_s, lens_s, sem):
    lane = lax.broadcasted_iota(jnp.int32, (8, LANES), 1)
    found = jnp.zeros((8, LANES), F32)
    for b in range(NB):
        found = jnp.where(lane == b, y_ref[b].astype(F32)[IN_ROWS - 8 :], found)
    wide_s[...] = found.astype(jnp.int32)
    copy = pltpu.make_async_copy(wide_s, lens_s, sem)
    copy.start()
    copy.wait()


def query_operands(qg):
    turned = qg.T
    sub = lax.broadcasted_iota(jnp.int32, (LANES, TQ), 0)
    q_t = jnp.where(sub < HD, turned * 0.125, jnp.where(sub == HD, 1.0, 0.0)).astype(BF16)
    d_t = jnp.where(sub < HD, 0.0, turned).astype(BF16)
    return q_t, d_t


def natural_operands(qg):
    low = lane_low((TQ, LANES))
    return jnp.where(low, qg, 0.0).astype(BF16), jnp.where(low, 0.0, qg).astype(BF16)


def score_sums(found, running):
    s, dprob = found
    peak, norm, inner = running
    new_peak = jnp.maximum(peak, fold(s, jnp.maximum))
    prob = jnp.exp(s - spread(new_peak, s.shape[0]))
    shrink = jnp.exp(peak - new_peak)
    norm = norm * shrink + fold(prob, jnp.add)
    inner = inner * shrink + fold(prob * dprob, jnp.add)
    return new_peak, norm, inner


def merged(running):
    peak8, norm8, inner8 = running
    peak = jnp.max(peak8, axis=0, keepdims=True)
    shrink = jnp.exp(peak8 - peak)
    norm = jnp.sum(norm8 * shrink, axis=0, keepdims=True)
    inner = jnp.sum(inner8 * shrink, axis=0, keepdims=True)
    return peak, norm, inner


def no_moments():
    zero = jnp.zeros((8, TQ), F32)
    return jnp.full((8, TQ), NEG, F32), zero, zero


def grad_parts(s, dprob, total, delta):
    prob = jnp.exp(s - total)
    dscore = (prob * (dprob - delta)).astype(BF16)
    return prob.astype(BF16), dscore


def key_grads(parts, naturals):
    prob, dscore = parts
    q_nat, d_nat = naturals
    return jnp.dot(dscore, q_nat, preferred_element_type=F32) + jnp.dot(
        prob, d_nat, preferred_element_type=F32
    )


def both_halves(dq_t):
    dq_t = dq_t * 0.125
    return jnp.concatenate([dq_t, dq_t], axis=0).T


def write_split(ref, first_row, value):
    for term in range(3):
        low = value.astype(BF16).astype(F32)
        value = value - low
        for half in range(2):
            ref[pl.ds(first_row + 4 * term + half, 1), :] = low[:, half * LANES : (half + 1) * LANES]


def read_split(rows, first_row):
    total = None
    for term in (2, 1, 0):
        at = first_row + 4 * term
        piece = jnp.concatenate([rows[at : at + 1], rows[at + 1 : at + 2]], axis=1)
        total = piece if total is None else total + piece
    return total


def sweep(count, tiles, refs, query, start, emit, arrive, ready, leave):
    kv_ref, ka_ref, kt_ref, acc_ref, s_pair, dp_pair = refs

    def tile_step(kt, slot, now, then, dq_t, running):
        found = None
        for j in range(TK // SUB):
            rows = pl.ds(pl.multiple_of(kt * TK + j * SUB, SUB), SUB)
            fresh = None
            if then is not None:
                q_t, d_t = then
                fresh = (
                    jnp.dot(ka_ref[rows, :], q_t, preferred_element_type=F32),
                    jnp.dot(kv_ref[rows, :], d_t, preferred_element_type=F32),
                )
                s_pair[1 - slot][rows, :], dp_pair[1 - slot][rows, :] = fresh
            if now is not None:
                naturals, total, delta = now
                parts = grad_parts(s_pair[slot][rows, :], dp_pair[slot][rows, :], total, delta)
            if found is not None:
                running = score_sums(found, running)
            if now is not None:
                acc_ref[rows, :] += key_grads(parts, naturals)
                keys = kt_ref[kt, :, j * SUB : (j + 1) * SUB]
                dq_t = dq_t + jnp.dot(keys, parts[1], preferred_element_type=F32)
            found = fresh
        if found is not None:
            running = score_sums(found, running)
        return dq_t, running

    def run(slot, now, then, running):
        def step(kt, carry):
            if now is None:
                arrive(kt)
            carry = tile_step(kt, slot, now, then, *carry)
            if then is None:
                leave(kt)
            return carry

        return lax.fori_loop(0, tiles, step, (jnp.zeros((HD, TQ), F32), running))

    _, running = run(1, None, query_operands(query(0)), start(0))
    ready()
    for t in range(count):
        peak, norm, inner = merged(running)
        total, delta = peak + jnp.log(norm), inner / norm
        now = natural_operands(query(t)), total, delta
        if t == count - 1:
            dq_t, _ = run(t % 2, now, None, no_moments())
        else:
            dq_t, running = run(t % 2, now, query_operands(query(t + 1)), start(t + 1))
        emit(t, dq_t, total, delta)


def tile_copy(src_ref, dst_ref, sem, kt):
    rows = tile_rows(kt, TK)
    return pltpu.make_async_copy(src_ref.at[rows, :], dst_ref.at[rows, :], sem.at[kt])


def enc_first_kernel(group_ref, y_ref, kv_ref, ka_ref, kt_ref, qg_ref, acc_ref, dq_ref, meta_ref,
                     kv_s, ka_s, kt_s, qg_s, acc_s, dq_s, s0_s, s1_s, dp0_s, dp1_s,
                     acc_sem, sems, wide_s, lens_s, sem):
    @pl.when(group_ref[0] < 3)
    def _():
        read_lens(y_ref, wide_s, lens_s, sem)

        def block(b, offset):
            length = lens_s[6, b]
            meta_ref[b] = offset
            meta_ref[NB + b] = length
            place_block(kv_s, ka_s, y_ref[b, 0:176, :], offset, length)
            return offset + ((length + 15) // 16) * 16

        end = lax.fori_loop(0, NB, block, jnp.int32(0))
        place_padding(kv_s, ka_s, end, TK)
        tiles = (end + TK - 1) // TK
        meta_ref[2 * NB] = tiles
        for b in range(NB):
            qg_s[pl.ds(QTR * b, 48), :] = y_ref[b].astype(F32)[TOK:]

        def arrive(kt):
            kt_s[kt] = turn(kv_s[tile_rows(kt, TK), :])
            acc_s[tile_rows(kt, TK), :] = jnp.zeros((TK, LANES), F32)

        copies = [
            pltpu.make_async_copy(src, dst, sems.at[i])
            for i, (src, dst) in enumerate(
                ((kv_s, kv_ref), (ka_s, ka_ref), (qg_s, qg_ref), (kt_s, kt_ref), (dq_s, dq_ref)))
        ]
        for copy in copies[:3]:
            copy.start()

        def emit(t, dq_t, total, delta):
            dq_s[pl.ds(t * TQ, TQ), :] = both_halves(dq_t)

        sweep(FIRST_TILES, tiles, (kv_s, ka_s, kt_s, acc_s, (s0_s, s1_s), (dp0_s, dp1_s)),
              lambda t: qg_s[pl.ds(t * TQ, TQ), :], lambda t: no_moments(), emit,
              arrive, copies[3].start, lambda kt: tile_copy(acc_s, acc_ref, acc_sem, kt).start())
        copies[4].start()
        for copy in copies:
            copy.wait()

        @pl.loop(0, tiles)
        def _(kt):
            tile_copy(acc_s, acc_ref, acc_sem, kt).wait()


def fetch_keys(tiles, kv, ka, kt_all, acc, kt_sem):
    @pl.loop(0, tiles)
    def _(kt):
        tile_copy(*kv, kt).start()
        tile_copy(*ka, kt).start()

    kt_copy = pltpu.make_async_copy(*kt_all, kt_sem)
    kt_copy.start()

    @pl.loop(0, tiles)
    def _(kt):
        tile_copy(*acc, kt).start()

    def arrive(kt):
        tile_copy(*kv, kt).wait()
        tile_copy(*ka, kt).wait()

    def ready():
        kt_copy.wait()

        @pl.loop(0, tiles)
        def _(kt):
            tile_copy(*acc, kt).wait()

    return arrive, ready


def enc_dec_kernel(group_ref, meta_ref, kv_ref, ka_ref, kt_ref, qg_ref, acc1_ref, m0_ref, m1_ref, m2_ref,
                   acc_ref, dq_ref, back_ref, kv_s, ka_s, kt_s, acc_s, s0_s, s1_s, dp0_s, dp1_s,
                   own_s, got_s, stat_s, kv_sem, ka_sem, acc_sem, out_sem, sems):
    group = group_ref[0]

    @pl.when(group < 3)
    def _():
        for c, m_ref in enumerate((m0_ref, m1_ref, m2_ref)):
            @pl.when(group == c)
            def _():
                pltpu.make_async_copy(m_ref, got_s, sems.at[0]).start()

        rest = pltpu.make_async_copy(
            qg_ref.at[pl.ds(NQ_ENC - REST, REST), :], own_s.at[pl.ds(DQ, REST), :], sems.at[1])
        rest.start()
        tiles = meta_ref[2 * NB]
        arrive, ready = fetch_keys(tiles, (kv_ref, kv_s, kv_sem), (ka_ref, ka_s, ka_sem), (kt_ref, kt_s),
                                   (acc1_ref, acc_s, acc_sem), sems.at[2])
        pltpu.make_async_copy(m0_ref, got_s, sems.at[0]).wait()
        got = got_s[...].astype(F32)
        own_s[pl.ds(0, DQ), :] = got[:DQ]
        stats = got[2 * TQ :]
        rest.wait()

        def start(t):
            row = lax.broadcasted_iota(jnp.int32, (8, TQ), 0)
            peak, norm, inner = (read_split(stats, 12 * k + 2 * t) for k in range(3))
            return (jnp.where(row == 0, peak, NEG), jnp.where(row == 0, norm, 0.0),
                    jnp.where(row == 0, inner, 0.0))

        stat_s[...] = jnp.zeros_like(stat_s)

        def emit(t, dq_t, total, delta):
            dq = both_halves(dq_t)
            back_ref[pl.ds(t * TQ, TQ), :] = dq.astype(BF16)
            write_split(stat_s, 2 * t, total)
            write_split(stat_s, 12 + 2 * t, delta)
            if t == 1:
                dq_ref[...] = dq[TQ - REST :]

        sweep(2, tiles, (kv_s, ka_s, kt_s, acc_s, (s0_s, s1_s), (dp0_s, dp1_s)),
              lambda t: own_s[pl.ds(t * TQ, TQ), :], start, emit,
              arrive, ready, lambda kt: tile_copy(acc_s, acc_ref, out_sem, kt).start())
        back_ref[pl.ds(2 * TQ, BACK_ROWS - 2 * TQ), :] = stat_s[...].astype(BF16)

        @pl.loop(0, tiles)
        def _(kt):
            tile_copy(acc_s, acc_ref, out_sem, kt).wait()


def enc_last_kernel(group_ref, meta_ref, kv_ref, ka_ref, kt_ref, qg_ref, acc2_ref, dq1_ref, dq2_ref,
                    o_ref, same_ref, kv_s, ka_s, kt_s, acc_s, s0_s, s1_s, dp0_s, dp1_s,
                    qg_s, dq_s, out_s, kv_sem, ka_sem, acc_sem, out_sem, sems):
    @pl.when(group_ref[0] < 3)
    def _():
        tiles = meta_ref[2 * NB]
        own = pltpu.make_async_copy(
            qg_ref.at[pl.ds(FIRST_TILES * TQ, LAST_TILES * TQ), :], qg_s, sems.at[0])
        own.start()
        arrive, ready = fetch_keys(tiles, (kv_ref, kv_s, kv_sem), (ka_ref, ka_s, ka_sem), (kt_ref, kt_s),
                                   (acc2_ref, acc_s, acc_sem), sems.at[1])
        early = [
            pltpu.make_async_copy(dq1_ref, dq_s.at[pl.ds(0, FIRST_TILES * TQ), :], sems.at[2]),
            pltpu.make_async_copy(dq2_ref, dq_s.at[pl.ds(NQ_ENC - REST, REST), :], sems.at[3]),
        ]
        for copy in early:
            copy.start()
        dq_s[pl.ds(NQ_ENC, 8), :] = jnp.zeros((8, LANES), F32)
        own.wait()

        def emit(t, dq_t, total, delta):
            dq_s[pl.ds((FIRST_TILES + t) * TQ, TQ), :] = both_halves(dq_t)

        sweep(LAST_TILES, tiles, (kv_s, ka_s, kt_s, acc_s, (s0_s, s1_s), (dp0_s, dp1_s)),
              lambda t: qg_s[pl.ds(t * TQ, TQ), :], lambda t: no_moments(), emit,
              arrive, ready, lambda kt: None)
        for copy in early:
            copy.wait()
        row = lax.broadcasted_iota(jnp.int32, (TOK, LANES), 0)
        low = lane_low((TOK, LANES))
        copies = []
        for b in range(NB):
            grad = acc_s[pl.ds(pl.multiple_of(meta_ref[b], 16), TOK), :]
            grad = jnp.where(row < meta_ref[NB + b], jnp.where(low, grad * 0.125, grad), 0.0)
            base = QTR * b
            dq = jnp.where(lane_low((24, LANES)), dq_s[pl.ds(base, 24), :], dq_s[pl.ds(base + 21, 24), :])
            out_s[b] = jnp.concatenate([grad, dq], axis=0).astype(BF16)
            if b % 8 == 7:
                some = pl.ds(b - 7, 8)
                copies.append(pltpu.make_async_copy(out_s.at[some], o_ref.at[some], out_sem.at[b // 8]))
                copies[-1].start()
        for copy in copies:
            copy.wait()


def dec_query_pos(t, part):
    q_id = t * TQ + lax.broadcasted_iota(jnp.int32, (1, TQ), 1)
    place = (q_id // DQTR) * DTOK + part * DQTR + q_id % DQTR
    return jnp.where(q_id < DQ, place, -1).astype(F32)


def dec_scores(kv_ref, ka_ref, pos_ref, c, rows, operands, q_at):
    q_t, d_t = operands
    s = jnp.dot(ka_ref[c, rows, :], q_t, preferred_element_type=F32)
    dprob = jnp.dot(kv_ref[c, rows, :], d_t, preferred_element_type=F32)
    k_at = pos_ref[rows, :]
    return jnp.where(jnp.concatenate([k_at, k_at], axis=1) <= q_at, s, NEG), dprob


def put_pos(pos_ref, offset, b):
    row = lax.broadcasted_iota(jnp.int32, (64, LANES), 0)
    pos_ref[pl.ds(pl.multiple_of(offset, 16), 64), :] = (row + b * DTOK).astype(F32)


def dec_units(kt):
    return [
        (pl.ds(pl.multiple_of(kt * TKD + j * SUB, SUB), SUB), t) for j in range(TKD // SUB) for t in range(2)
    ]


def dec_first_kernel(group_ref, part_ref, held_ref, kv_out, ka_out, kt_out, m0_out, m1_out, m2_out, meta_ref,
                     y_ref, kv_ref, ka_ref, kt_ref, pos_ref, m_ref, qg_s, stat_s, sems, wide_s, lens_s, sem):
    @pl.when(group_ref[0] == 3)
    def _():
        fetch = pltpu.make_async_copy(held_ref, y_ref, sems.at[0])
        fetch.start()
        fetch.wait()
        read_lens(y_ref, wide_s, lens_s, sem)

        def block(b, offset):
            length = lens_s[7, b]
            meta_ref[b] = offset
            meta_ref[NB + b] = length
            chunk = y_ref[b].astype(F32)
            for c in range(3):
                keys = chunk[DIN_ROWS * c : DIN_ROWS * c + 64].astype(BF16)
                place_block(kv_ref.at[c], ka_ref.at[c], keys, offset, length)
            put_pos(pos_ref, offset, b)
            return offset + ((length + 15) // 16) * 16

        end = lax.fori_loop(0, NB, block, jnp.int32(0))
        for c in range(3):
            place_padding(kv_ref.at[c], ka_ref.at[c], end, TKD)
        tiles = (end + TKD - 1) // TKD
        meta_ref[2 * NB] = tiles
        for b in range(NB):
            chunk = y_ref[b].astype(F32)
            for c in range(3):
                qg_s[c, pl.ds(DQTR * b, 16), :] = chunk[DIN_ROWS * c + DTOK : DIN_ROWS * (c + 1)]
        part = part_ref[0]
        stat_s[...] = jnp.zeros_like(stat_s)
        for c in range(3):
            qg_s[c, pl.ds(DQ, REST), :] = jnp.zeros((REST, LANES), F32)
            m_ref[c, pl.ds(0, 2 * TQ), :] = qg_s[c].astype(BF16)

            @pl.loop(0, tiles)
            def _(kt):
                kt_ref[c, kt] = turn(kv_ref[c, tile_rows(kt, TKD), :])

        copies = [
            pltpu.make_async_copy(src, dst, sems.at[1 + i])
            for i, (src, dst) in enumerate(
                ((kv_ref, kv_out), (ka_ref, ka_out), (kt_ref, kt_out)))
        ]
        for copy in copies:
            copy.start()
        for c, out in enumerate((m0_out, m1_out, m2_out)):
            operands = [query_operands(qg_s[c, pl.ds(t * TQ, TQ), :]) for t in range(2)]
            q_at = [dec_query_pos(t, part) for t in range(2)]

            def step(kt, carry):
                carry = list(carry)
                units = dec_units(kt)
                ahead = lambda u: dec_scores(kv_ref, ka_ref, pos_ref, c, units[u][0], operands[units[u][1]], q_at[units[u][1]])
                found = ahead(0)
                for u, (rows, t) in enumerate(units):
                    fresh = ahead(u + 1) if u + 1 < len(units) else None
                    carry[t] = score_sums(found, carry[t])
                    found = fresh
                return tuple(carry)

            found = lax.fori_loop(0, tiles, step, (no_moments(), no_moments()))
            for t in range(2):
                q_id = t * TQ + lax.broadcasted_iota(jnp.int32, (1, TQ), 1)
                for k, value in enumerate(merged(found[t])):
                    write_split(stat_s, 12 * k + 2 * t, jnp.where(q_id < DQ, value, NEG if k == 0 else 0.0))
            m_ref[c, pl.ds(2 * TQ, THERE_ROWS - 2 * TQ), :] = stat_s[...].astype(BF16)
            copies.append(pltpu.make_async_copy(m_ref.at[c], out, sems.at[4 + c]))
            copies[-1].start()
        for copy in copies:
            copy.wait()


def dec_last_kernel(group_ref, part_ref, meta_ref, kv_in, ka_in, kt_in, m0_in, m1_in, m2_in, b0_in, b1_in, b2_in, enc_ref,
                    o_ref, kv_ref, ka_ref, kt_ref, pos_ref, m_ref, back_ref, acc_s, dq_s, out_s, sems, sem):
    @pl.when(group_ref[0] == 3)
    def _():
        tiles = meta_ref[2 * NB]
        part = part_ref[0]
        fetches = [
            [
                pltpu.make_async_copy(src, dst.at[c], sems.at[c, i])
                for i, (src, dst) in enumerate(
                    ((m_in, m_ref), (b_in, back_ref), (kv_in.at[c], kv_ref), (ka_in.at[c], ka_ref), (kt_in.at[c], kt_ref)))
            ]
            for c, (m_in, b_in) in enumerate(((m0_in, b0_in), (m1_in, b1_in), (m2_in, b2_in)))
        ]
        for some in fetches:
            for copy in some:
                copy.start()

        @pl.loop(0, NB)
        def _(b):
            put_pos(pos_ref, meta_ref[b], b)

        for c in range(3):
            for copy in fetches[c]:
                copy.wait()
            qg = m_ref[c, pl.ds(0, 2 * TQ), :].astype(F32)
            back = back_ref[c].astype(F32)
            stats = back[2 * TQ :]
            cut = [qg[t * TQ : (t + 1) * TQ] for t in range(2)]
            operands = [query_operands(cut[t]) for t in range(2)]
            naturals = [natural_operands(cut[t]) for t in range(2)]
            q_at = [dec_query_pos(t, part) for t in range(2)]
            total = [read_split(stats, 2 * t) for t in range(2)]
            delta = [read_split(stats, 12 + 2 * t) for t in range(2)]

            def step(kt, dqs):
                dqs = list(dqs)
                units = dec_units(kt)
                ahead = lambda u: dec_scores(kv_ref, ka_ref, pos_ref, c, units[u][0], operands[units[u][1]], q_at[units[u][1]])
                found = ahead(0)
                for u, (rows, t) in enumerate(units):
                    fresh = ahead(u + 1) if u + 1 < len(units) else None
                    parts = grad_parts(*found, total[t], delta[t])
                    grad = key_grads(parts, naturals[t])
                    acc_s[rows, :] = grad if t == 0 else acc_s[rows, :] + grad
                    keys = kt_ref[c, kt, :, u // 2 * SUB : (u // 2 + 1) * SUB]
                    dqs[t] = dqs[t] + jnp.dot(keys, parts[1], preferred_element_type=F32)
                    found = fresh
                return tuple(dqs)

            none = jnp.zeros((HD, TQ), F32)
            dqs = lax.fori_loop(0, tiles, step, (none, none))
            for t in range(2):
                rows = pl.ds(t * TQ, TQ)
                dq_s[rows, :] = both_halves(dqs[t]) + back[t * TQ : (t + 1) * TQ]
            row = lax.broadcasted_iota(jnp.int32, (DTOK, LANES), 0)
            low = lane_low((DTOK, LANES))
            for b in range(NB):
                grad = acc_s[pl.ds(pl.multiple_of(meta_ref[b], 16), DTOK), :]
                grad = jnp.where(row < meta_ref[NB + b], jnp.where(low, grad * 0.125, grad), 0.0)
                base = DQTR * b
                dq = jnp.where(lane_low((8, LANES)), dq_s[pl.ds(base, 8), :], dq_s[pl.ds(base + 7, 8), :])
                out_s[b, pl.ds(DOUT_ROWS * c, DOUT_ROWS), :] = jnp.concatenate([grad, dq], axis=0).astype(BF16)
        copy = pltpu.make_async_copy(out_s, o_ref, sem)
        copy.start()
        copy.wait()


SMEM = pl.BlockSpec(memory_space=pltpu.SMEM)
VMEM = pl.BlockSpec(memory_space=pltpu.VMEM)
ANY = pl.BlockSpec(memory_space=pl.ANY)


def limit(mib):
    return pltpu.CompilerParams(vmem_limit_bytes=mib * MIB)


def shaped(shape, dtype):
    return jax.ShapeDtypeStruct(shape, dtype)


def lens_scratch():
    return [
        pltpu.VMEM((8, LANES), jnp.int32),
        pltpu.SMEM((8, LANES), jnp.int32),
        pltpu.SemaphoreType.DMA(()),
    ]


def key_scratch():
    return [
        pltpu.VMEM((NK_ENC + TK, LANES), BF16),
        pltpu.VMEM((NK_ENC + TK, LANES), BF16),
        pltpu.VMEM((NK_ENC // TK, HD, TK), BF16),
    ]


def score_scratch():
    return [pltpu.VMEM((NK_ENC, LANES), F32)] + [pltpu.VMEM((NK_ENC, TQ), F32)] * 4


def dma(*shape):
    return pltpu.SemaphoreType.DMA(shape)


META = shaped((2 * NB + 8,), jnp.int32)
ENC_TILES = NK_ENC // TK


def dec_first(group, part, held):
    keys = [((3, NK_DEC + TKD, LANES), BF16), ((3, NK_DEC + TKD, LANES), BF16),
            ((3, NK_DEC // TKD, HD, TKD), BF16)]
    pos = ((NK_DEC + TKD, LANES), F32)
    return pl.pallas_call(
        dec_first_kernel,
        out_shape=[shaped(*k) for k in keys] + [shaped((THERE_ROWS, LANES), BF16)] * 3 + [META],
        in_specs=[SMEM, SMEM, ANY],
        out_specs=[ANY] * 6 + [SMEM],
        scratch_shapes=[pltpu.VMEM(held.shape, BF16)] + [pltpu.VMEM(*k) for k in keys + [pos]] + [
            pltpu.VMEM((3, THERE_ROWS, LANES), BF16),
            pltpu.VMEM((3, 2 * TQ, LANES), F32),
            pltpu.VMEM((THERE_ROWS - 2 * TQ, LANES), F32),
            dma(8),
        ] + lens_scratch(),
        compiler_params=limit(24),
    )(group, part, held)


def enc_first(group, held):
    return pl.pallas_call(
        enc_first_kernel,
        out_shape=[
            shaped((NK_ENC + TK, LANES), BF16),
            shaped((NK_ENC + TK, LANES), BF16),
            shaped((ENC_TILES, HD, TK), BF16),
            shaped((NQ_ENC + 8, LANES), F32),
            shaped((NK_ENC, LANES), F32),
            shaped((FIRST_TILES * TQ, LANES), F32),
            META,
        ],
        in_specs=[SMEM, VMEM],
        out_specs=[ANY] * 6 + [SMEM],
        scratch_shapes=key_scratch() + [
            pltpu.VMEM((NQ_ENC + 8, LANES), F32),
            score_scratch()[0],
            pltpu.VMEM((FIRST_TILES * TQ, LANES), F32),
        ] + score_scratch()[1:] + [dma(ENC_TILES), dma(5)] + lens_scratch(),
        compiler_params=limit(38),
    )(group, held)


def enc_dec(group, meta, keys, acc, messages):
    return pl.pallas_call(
        enc_dec_kernel,
        out_shape=[
            shaped((NK_ENC, LANES), F32),
            shaped((REST, LANES), F32),
            shaped((BACK_ROWS, LANES), BF16),
        ],
        in_specs=[SMEM, SMEM] + [ANY] * 8,
        out_specs=[ANY, VMEM, VMEM],
        scratch_shapes=key_scratch() + score_scratch() + [
            pltpu.VMEM((2 * TQ, LANES), F32),
            pltpu.VMEM((THERE_ROWS, LANES), BF16),
            pltpu.VMEM((BACK_ROWS - 2 * TQ, LANES), F32),
            dma(ENC_TILES), dma(ENC_TILES), dma(ENC_TILES), dma(ENC_TILES), dma(3),
        ],
        input_output_aliases={6: 0},
        compiler_params=limit(38),
    )(group, meta, *keys, acc, *messages)


def enc_last(group, meta, keys, acc, dqs):
    return pl.pallas_call(
        enc_last_kernel,
        out_shape=[shaped((NB, OUT_ROWS, LANES), BF16), shaped(acc.shape, F32)],
        in_specs=[SMEM, SMEM] + [ANY] * 7,
        out_specs=[ANY, ANY],
        scratch_shapes=key_scratch() + score_scratch() + [
            pltpu.VMEM((LAST_TILES * TQ, LANES), F32),
            pltpu.VMEM((NQ_ENC + 8, LANES), F32),
            pltpu.VMEM((NB, OUT_ROWS, LANES), BF16),
            dma(ENC_TILES), dma(ENC_TILES), dma(ENC_TILES), dma(4), dma(4),
        ],
        input_output_aliases={6: 1},
        compiler_params=limit(38),
    )(group, meta, *keys, acc, *dqs)[0]


def dec_last(group, part, meta, keys, messages, back, enc_out):
    return pl.pallas_call(
        dec_last_kernel,
        out_shape=shaped((NB, OUT_ROWS, LANES), BF16),
        in_specs=[SMEM, SMEM, SMEM] + [ANY] * 10,
        out_specs=ANY,
        scratch_shapes=[pltpu.VMEM(k.shape, k.dtype) for k in keys] + [
            pltpu.VMEM((NK_DEC + TKD, LANES), F32),
            pltpu.VMEM((3, THERE_ROWS, LANES), BF16),
            pltpu.VMEM((3, BACK_ROWS, LANES), BF16),
            pltpu.VMEM((NK_DEC + TKD, LANES), F32),
            pltpu.VMEM((2 * TQ, LANES), F32),
            pltpu.VMEM((NB, OUT_ROWS, LANES), BF16),
            dma(3, 5), dma(),
        ],
        input_output_aliases={12: 0},
        compiler_params=limit(24),
    )(group, part, meta, *keys, *messages, *back, enc_out)


def on_device(queries, key_rows, value_rows, out_grad, enc_lengths, dec_lengths):
    group = lax.axis_index("grp").astype(jnp.int32).reshape(1)
    part = (lax.axis_index("blk") % 4).astype(jnp.int32).reshape(1)
    chunks = pl.pallas_call(
        pack_kernel,
        out_shape=shaped((NB, IN_ROWS, LANES), BF16),
        in_specs=[SMEM, SMEM, SMEM, SMEM, ANY, ANY, ANY, ANY],
        out_specs=ANY,
        scratch_shapes=[pltpu.VMEM((4, TOK, LANES), BF16)] * 4 + [pltpu.VMEM((8, TOK, LANES), F32)] * 2 + [
            pltpu.VMEM((NB, IN_ROWS, LANES), BF16), dma(4, 4), dma(4)],
        compiler_params=limit(62),
    )(group, part, enc_lengths, dec_lengths, queries, key_rows, value_rows, out_grad)
    held = lax.all_to_all(chunks, "blk", 0, 0, tiled=True)

    def partner(c, blk):
        return (blk + 16) % NB if c < 2 else blk

    there = [[(3 * NB + s, c * NB + partner(c, s)) for s in range(NB)] for c in range(3)]
    *dec_keys, m0, m1, m2, dec_meta = dec_first(group, part, held)
    messages = (m0, m1, m2)
    got = [lax.ppermute(messages[c], ("grp", "blk"), there[c]) for c in range(3)]
    *enc_keys, acc1, dq1, enc_meta = enc_first(group, held)
    acc2, dq2, answer = enc_dec(group, enc_meta, enc_keys, acc1, got)
    back = [lax.ppermute(answer, ("grp", "blk"), [(d, s) for s, d in there[c]]) for c in range(3)]
    enc_out = enc_last(group, enc_meta, enc_keys, acc2, (dq1, dq2))
    final = dec_last(group, part, dec_meta, dec_keys, messages, back, enc_out)
    final = lax.all_to_all(final, "blk", 0, 0, tiled=True)
    out = shaped(queries.shape, F32)
    return pl.pallas_call(
        unpack_kernel,
        out_shape=[out, out, out],
        in_specs=[SMEM, VMEM],
        out_specs=[VMEM, VMEM, VMEM],
        scratch_shapes=[pltpu.VMEM((TOK, LANES), F32)] * 3 + [pltpu.VMEM((DTOK, LANES), F32)],
        compiler_params=limit(10),
    )(group, final)


def solution(mesh):
    rows = P("blk", "grp")
    return jax.shard_map(
        on_device,
        mesh=mesh,
        in_specs=(rows, rows, rows, rows, P("blk"), P("blk")),
        out_specs=(rows, rows, rows),
        check_vma=False,
    )
```

```python
import functools

import jax
import jax.numpy as jnp
from jax import lax
from jax.experimental import pallas as pl
from jax.experimental.pallas import tpu as pltpu
from jax.sharding import PartitionSpec as P

HD = 64
LANES = 128
NB = 32
TOK = 168
DTOK = 56
QTR = TOK // 4
DQTR = DTOK // 4
IN_ROWS = 216
DIN_ROWS = 72
OUT_ROWS = 192
DOUT_ROWS = 64
NQ_ENC = NB * QTR
DQ = NB * DQTR
TQ = 256
TK = 2048
SUB = 256
TKD = 768
NK_ENC = -(-(NB * 176) // TK) * TK
NK_DEC = -(-(NB * 64) // TKD) * TKD
REST = 2 * TQ - DQ
FIRST_TILES = 2
LAST_TILES = (NQ_ENC - REST) // TQ - FIRST_TILES
THERE_ROWS = 2 * TQ + 48
BACK_ROWS = 2 * TQ + 32
NEG = -1e30
F32 = jnp.float32
BF16 = jnp.bfloat16
MIB = 1024 * 1024


def flip(head):
    return (head + 4) % 8


def lane_low(shape):
    return lax.broadcasted_iota(jnp.int32, shape, len(shape) - 1) < HD


def pair_up(first, second):
    low = lane_low(first.shape)
    even = jnp.where(low, first, pltpu.roll(second, HD, 1))
    odd = jnp.where(low, pltpu.roll(first, HD, 1), second)
    return even, odd


def pack_kernel(group_ref, part_ref, enc_ref, dec_ref, q_in, k_in, v_in, g_in, x_out,
                q_ref, k_ref, v_ref, g_ref, kv_s, qg_s, x_ref, in_sem, out_sem):
    is_dec = group_ref[0] == 3
    arrays = ((k_in, k_ref), (v_in, v_ref), (q_in, q_ref), (g_in, g_ref))
    fetches = [
        [
            pltpu.make_async_copy(src.at[:, pl.ds(pair * LANES, LANES)], dst.at[pair], in_sem.at[pair, i])
            for i, (src, dst) in enumerate(arrays)
        ]
        for pair in range(4)
    ]
    for some in fetches:
        for copy in some:
            copy.start()
    row = lax.broadcasted_iota(jnp.int32, (8, LANES), 0)
    enc_len, dec_len = enc_ref[0].astype(F32), dec_ref[0].astype(F32)
    tail = jnp.where(row == 6, enc_len, jnp.where(row == 7, dec_len, 0.0))

    def sent(pair):
        some = pl.ds(8 * pair, 8)
        return pltpu.make_async_copy(x_ref.at[some], x_out.at[some], out_sem.at[pair])

    for pair in range(4):
        for copy in fetches[pair]:
            copy.wait()
        even, odd = pair_up(k_ref[pair].astype(F32), v_ref[pair].astype(F32))
        kv_s[2 * pair], kv_s[2 * pair + 1] = even, odd
        even, odd = pair_up(q_ref[pair].astype(F32), g_ref[pair].astype(F32))
        qg_s[2 * pair], qg_s[2 * pair + 1] = even, odd

        @pl.when(jnp.logical_not(is_dec))
        def _():
            for head in (2 * pair, 2 * pair + 1):
                kv = kv_s[head]
                for part in range(4):
                    qg = qg_s[head, pl.ds(part * QTR, QTR), :]
                    x_ref[4 * head + part] = jnp.concatenate([kv, qg, tail[2:]], axis=0).astype(BF16)
            sent(pair).start()

    @pl.when(is_dec)
    def _():
        for head in range(8):
            for part in range(4):
                pieces = []
                for c in range(3):
                    src = flip(head) if c < 2 else head
                    pieces.append(kv_s[src, pl.ds(c, DTOK, stride=3), :])
                    pieces.append(qg_s[src, pl.ds(3 * part * DQTR + c, DQTR, stride=3), :])
                    pieces.append(tail[6:])
                x_ref[4 * head + part] = jnp.concatenate(pieces, axis=0).astype(BF16)
            if head % 2 == 1:
                sent(head // 2).start()

    for pair in range(4):
        sent(pair).wait()


def unpack_kernel(group_ref, w_ref, qo_ref, ko_ref, vo_ref, dq_s, dk_s, dv_s, tmp_s):
    is_dec = group_ref[0] == 3

    @pl.when(jnp.logical_not(is_dec))
    def _():
        for pair in range(4):
            cols = pl.ds(pair * LANES, LANES)
            sums = []
            for head in (2 * pair, 2 * pair + 1):
                total = None
                for part in range(4):
                    chunk = w_ref[4 * head + part].astype(F32)
                    total = chunk[:TOK] if total is None else total + chunk[:TOK]
                    dq = chunk[TOK:]
                    turned = pltpu.roll(dq, HD, 1)
                    first, second = (dq, turned) if head % 2 == 0 else (turned, dq)
                    base = part * QTR
                    if head % 2 == 0:
                        dq_s[pl.ds(base, 21), :] = first[:21]
                        dq_s[pl.ds(base + 21, 21), :] = second[:21]
                    else:
                        low = lane_low((21, LANES))
                        for start, value in ((base, first), (base + 21, second)):
                            old = dq_s[pl.ds(start, 21), :]
                            dq_s[pl.ds(start, 21), :] = jnp.where(low, old, value[:21])
                sums.append(total)
            low = lane_low((TOK, LANES))
            ko_ref[:, cols] = jnp.where(low, sums[0], pltpu.roll(sums[1], HD, 1))
            vo_ref[:, cols] = jnp.where(low, pltpu.roll(sums[0], HD, 1), sums[1])
            qo_ref[:, cols] = dq_s[...]

    @pl.when(is_dec)
    def _():
        for pair in range(4):
            cols = pl.ds(pair * LANES, LANES)
            for c in range(3):
                sums, dqs = [], []
                for head in (2 * pair, 2 * pair + 1):
                    place = flip(head) if c < 2 else head
                    total, pieces = None, []
                    for part in range(4):
                        chunk = w_ref[4 * place + part].astype(F32)[DOUT_ROWS * c : DOUT_ROWS * (c + 1)]
                        kv = chunk[:DTOK]
                        total = kv if total is None else total + kv
                        dq = chunk[DTOK:]
                        turned = pltpu.roll(dq, HD, 1)
                        pieces.append((dq, turned) if head % 2 == 0 else (turned, dq))
                    sums.append(total)
                    dqs.append(pieces)
                low = lane_low((DTOK, LANES))
                rows = pl.ds(c, DTOK, stride=3)
                dk_s[rows, :] = jnp.where(low, sums[0], pltpu.roll(sums[1], HD, 1))
                dv_s[rows, :] = jnp.where(low, pltpu.roll(sums[0], HD, 1), sums[1])
                low = lane_low((8, LANES))
                for part in range(4):
                    for half in range(2):
                        value = jnp.where(low, dqs[0][part][half], dqs[1][part][half])
                        tmp_s[pl.ds(part * DQTR + half * 7, 7), :] = value[:7]
                dq_s[rows, :] = tmp_s[...]
            ko_ref[:, cols] = dk_s[...]
            vo_ref[:, cols] = dv_s[...]
            qo_ref[:, cols] = dq_s[...]


def fold(tile, op):
    parts = [tile[8 * i : 8 * i + 8] for i in range(tile.shape[0] // 8)]
    while len(parts) > 1:
        parts = [op(parts[i], parts[i + 1]) if i + 1 < len(parts) else parts[i] for i in range(0, len(parts), 2)]
    return parts[0]


def spread(stat, rows):
    return jnp.concatenate([stat] * (rows // 8), axis=0)


def tile_rows(kt, size):
    return pl.ds(pl.multiple_of(kt * size, size), size)


def place_block(kv_ref, ka_ref, block, offset, length):
    size = block.shape[0]
    row = lax.broadcasted_iota(jnp.int32, (size, LANES), 0)
    lane = lax.broadcasted_iota(jnp.int32, (size, LANES), 1)
    rows = pl.ds(pl.multiple_of(offset, 16), size)
    kv_ref[rows, :] = block
    bias = jnp.where(row < length, 0.0, NEG)
    ka_ref[rows, :] = jnp.where(lane == HD, bias, block.astype(F32)).astype(BF16)


def place_padding(kv_ref, ka_ref, offset, size):
    lane = lax.broadcasted_iota(jnp.int32, (size, LANES), 1)
    rows = pl.ds(pl.multiple_of(offset, 16), size)
    kv_ref[rows, :] = jnp.zeros((size, LANES), BF16)
    ka_ref[rows, :] = jnp.where(lane == HD, NEG, 0.0).astype(BF16)


def turn(keys):
    return keys.astype(F32).T[:HD].astype(BF16)


def read_lens(y_ref, wide_s, lens_s, sem):
    lane = lax.broadcasted_iota(jnp.int32, (8, LANES), 1)
    found = jnp.zeros((8, LANES), F32)
    for b in range(NB):
        found = jnp.where(lane == b, y_ref[b].astype(F32)[IN_ROWS - 8 :], found)
    wide_s[...] = found.astype(jnp.int32)
    copy = pltpu.make_async_copy(wide_s, lens_s, sem)
    copy.start()
    copy.wait()


def query_operands(qg):
    turned = qg.T
    sub = lax.broadcasted_iota(jnp.int32, (LANES, TQ), 0)
    q_t = jnp.where(sub < HD, turned * 0.125, jnp.where(sub == HD, 1.0, 0.0)).astype(BF16)
    d_t = jnp.where(sub < HD, 0.0, turned).astype(BF16)
    return q_t, d_t


def natural_operands(qg):
    low = lane_low((TQ, LANES))
    return jnp.where(low, qg, 0.0).astype(BF16), jnp.where(low, 0.0, qg).astype(BF16)


def score_sums(found, running):
    s, dprob = found
    peak, norm, inner = running
    new_peak = jnp.maximum(peak, fold(s, jnp.maximum))
    prob = jnp.exp(s - spread(new_peak, s.shape[0]))
    shrink = jnp.exp(peak - new_peak)
    norm = norm * shrink + fold(prob, jnp.add)
    inner = inner * shrink + fold(prob * dprob, jnp.add)
    return new_peak, norm, inner


def merged(running):
    peak8, norm8, inner8 = running
    peak = jnp.max(peak8, axis=0, keepdims=True)
    shrink = jnp.exp(peak8 - peak)
    norm = jnp.sum(norm8 * shrink, axis=0, keepdims=True)
    inner = jnp.sum(inner8 * shrink, axis=0, keepdims=True)
    return peak, norm, inner


def no_moments():
    zero = jnp.zeros((8, TQ), F32)
    return jnp.full((8, TQ), NEG, F32), zero, zero


def grad_parts(s, dprob, total, delta):
    prob = jnp.exp(s - total)
    dscore = (prob * (dprob - delta)).astype(BF16)
    return prob.astype(BF16), dscore


def key_grads(parts, naturals):
    prob, dscore = parts
    q_nat, d_nat = naturals
    return jnp.dot(dscore, q_nat, preferred_element_type=F32) + jnp.dot(
        prob, d_nat, preferred_element_type=F32
    )


def both_halves(dq_t):
    dq_t = dq_t * 0.125
    return jnp.concatenate([dq_t, dq_t], axis=0).T


def write_split(ref, first_row, value):
    for term in range(3):
        low = value.astype(BF16).astype(F32)
        value = value - low
        for half in range(2):
            ref[pl.ds(first_row + 4 * term + half, 1), :] = low[:, half * LANES : (half + 1) * LANES]


def read_split(rows, first_row):
    total = None
    for term in (2, 1, 0):
        at = first_row + 4 * term
        piece = jnp.concatenate([rows[at : at + 1], rows[at + 1 : at + 2]], axis=1)
        total = piece if total is None else total + piece
    return total


def sweep(count, tiles, refs, query, start, emit, arrive, ready, leave):
    kv_ref, ka_ref, kt_ref, acc_ref, s_pair, dp_pair = refs

    def tile_step(kt, slot, now, then, dq_t, running):
        found = None
        for j in range(TK // SUB):
            rows = pl.ds(pl.multiple_of(kt * TK + j * SUB, SUB), SUB)
            fresh = None
            if then is not None:
                q_t, d_t = then
                fresh = (
                    jnp.dot(ka_ref[rows, :], q_t, preferred_element_type=F32),
                    jnp.dot(kv_ref[rows, :], d_t, preferred_element_type=F32),
                )
                s_pair[1 - slot][rows, :], dp_pair[1 - slot][rows, :] = fresh
            if now is not None:
                naturals, total, delta = now
                parts = grad_parts(s_pair[slot][rows, :], dp_pair[slot][rows, :], total, delta)
            if found is not None:
                running = score_sums(found, running)
            if now is not None:
                acc_ref[rows, :] += key_grads(parts, naturals)
                keys = kt_ref[kt, :, j * SUB : (j + 1) * SUB]
                dq_t = dq_t + jnp.dot(keys, parts[1], preferred_element_type=F32)
            found = fresh
        if found is not None:
            running = score_sums(found, running)
        return dq_t, running

    def run(slot, now, then, running):
        def step(kt, carry):
            if now is None:
                arrive(kt)
            carry = tile_step(kt, slot, now, then, *carry)
            if then is None:
                leave(kt)
            return carry

        return lax.fori_loop(0, tiles, step, (jnp.zeros((HD, TQ), F32), running))

    _, running = run(1, None, query_operands(query(0)), start(0))
    ready()
    for t in range(count):
        peak, norm, inner = merged(running)
        total, delta = peak + jnp.log(norm), inner / norm
        now = natural_operands(query(t)), total, delta
        if t == count - 1:
            dq_t, _ = run(t % 2, now, None, no_moments())
        else:
            dq_t, running = run(t % 2, now, query_operands(query(t + 1)), start(t + 1))
        emit(t, dq_t, total, delta)


def tile_copy(src_ref, dst_ref, sem, kt):
    rows = tile_rows(kt, TK)
    return pltpu.make_async_copy(src_ref.at[rows, :], dst_ref.at[rows, :], sem.at[kt])


def enc_first_kernel(group_ref, y_ref, kv_ref, ka_ref, kt_ref, qg_ref, acc_ref, dq_ref, meta_ref,
                     kv_s, ka_s, kt_s, qg_s, acc_s, dq_s, s0_s, s1_s, dp0_s, dp1_s,
                     acc_sem, sems, wide_s, lens_s, sem):
    @pl.when(group_ref[0] < 3)
    def _():
        read_lens(y_ref, wide_s, lens_s, sem)

        def block(b, offset):
            length = lens_s[6, b]
            meta_ref[b] = offset
            meta_ref[NB + b] = length
            place_block(kv_s, ka_s, y_ref[b, 0:176, :], offset, length)
            return offset + ((length + 15) // 16) * 16

        end = lax.fori_loop(0, NB, block, jnp.int32(0))
        place_padding(kv_s, ka_s, end, TK)
        tiles = (end + TK - 1) // TK
        meta_ref[2 * NB] = tiles
        for b in range(NB):
            qg_s[pl.ds(QTR * b, 48), :] = y_ref[b].astype(F32)[TOK:]

        def arrive(kt):
            kt_s[kt] = turn(kv_s[tile_rows(kt, TK), :])
            acc_s[tile_rows(kt, TK), :] = jnp.zeros((TK, LANES), F32)

        copies = [
            pltpu.make_async_copy(src, dst, sems.at[i])
            for i, (src, dst) in enumerate(
                ((kv_s, kv_ref), (ka_s, ka_ref), (qg_s, qg_ref), (kt_s, kt_ref), (dq_s, dq_ref)))
        ]
        for copy in copies[:3]:
            copy.start()

        def emit(t, dq_t, total, delta):
            dq_s[pl.ds(t * TQ, TQ), :] = both_halves(dq_t)

        sweep(FIRST_TILES, tiles, (kv_s, ka_s, kt_s, acc_s, (s0_s, s1_s), (dp0_s, dp1_s)),
              lambda t: qg_s[pl.ds(t * TQ, TQ), :], lambda t: no_moments(), emit,
              arrive, copies[3].start, lambda kt: tile_copy(acc_s, acc_ref, acc_sem, kt).start())
        copies[4].start()
        for copy in copies:
            copy.wait()

        @pl.loop(0, tiles)
        def _(kt):
            tile_copy(acc_s, acc_ref, acc_sem, kt).wait()


def fetch_keys(tiles, kv, ka, kt_all, acc, kt_sem):
    @pl.loop(0, tiles)
    def _(kt):
        tile_copy(*kv, kt).start()
        tile_copy(*ka, kt).start()

    kt_copy = pltpu.make_async_copy(*kt_all, kt_sem)
    kt_copy.start()

    @pl.loop(0, tiles)
    def _(kt):
        tile_copy(*acc, kt).start()

    def arrive(kt):
        tile_copy(*kv, kt).wait()
        tile_copy(*ka, kt).wait()

    def ready():
        kt_copy.wait()

        @pl.loop(0, tiles)
        def _(kt):
            tile_copy(*acc, kt).wait()

    return arrive, ready


def enc_dec_kernel(group_ref, meta_ref, kv_ref, ka_ref, kt_ref, qg_ref, acc1_ref, m0_ref, m1_ref, m2_ref,
                   acc_ref, dq_ref, back_ref, kv_s, ka_s, kt_s, acc_s, s0_s, s1_s, dp0_s, dp1_s,
                   own_s, got_s, stat_s, kv_sem, ka_sem, acc_sem, out_sem, sems):
    group = group_ref[0]

    @pl.when(group < 3)
    def _():
        for c, m_ref in enumerate((m0_ref, m1_ref, m2_ref)):
            @pl.when(group == c)
            def _():
                pltpu.make_async_copy(m_ref, got_s, sems.at[0]).start()

        rest = pltpu.make_async_copy(
            qg_ref.at[pl.ds(NQ_ENC - REST, REST), :], own_s.at[pl.ds(DQ, REST), :], sems.at[1])
        rest.start()
        tiles = meta_ref[2 * NB]
        arrive, ready = fetch_keys(tiles, (kv_ref, kv_s, kv_sem), (ka_ref, ka_s, ka_sem), (kt_ref, kt_s),
                                   (acc1_ref, acc_s, acc_sem), sems.at[2])
        pltpu.make_async_copy(m0_ref, got_s, sems.at[0]).wait()
        got = got_s[...].astype(F32)
        own_s[pl.ds(0, DQ), :] = got[:DQ]
        stats = got[2 * TQ :]
        rest.wait()

        def start(t):
            row = lax.broadcasted_iota(jnp.int32, (8, TQ), 0)
            peak, norm, inner = (read_split(stats, 12 * k + 2 * t) for k in range(3))
            return (jnp.where(row == 0, peak, NEG), jnp.where(row == 0, norm, 0.0),
                    jnp.where(row == 0, inner, 0.0))

        stat_s[...] = jnp.zeros_like(stat_s)

        def emit(t, dq_t, total, delta):
            dq = both_halves(dq_t)
            back_ref[pl.ds(t * TQ, TQ), :] = dq.astype(BF16)
            write_split(stat_s, 2 * t, total)
            write_split(stat_s, 12 + 2 * t, delta)
            if t == 1:
                dq_ref[...] = dq[TQ - REST :]

        sweep(2, tiles, (kv_s, ka_s, kt_s, acc_s, (s0_s, s1_s), (dp0_s, dp1_s)),
              lambda t: own_s[pl.ds(t * TQ, TQ), :], start, emit,
              arrive, ready, lambda kt: tile_copy(acc_s, acc_ref, out_sem, kt).start())
        back_ref[pl.ds(2 * TQ, BACK_ROWS - 2 * TQ), :] = stat_s[...].astype(BF16)

        @pl.loop(0, tiles)
        def _(kt):
            tile_copy(acc_s, acc_ref, out_sem, kt).wait()


def enc_last_kernel(group_ref, meta_ref, kv_ref, ka_ref, kt_ref, qg_ref, acc2_ref, dq1_ref, dq2_ref,
                    o_ref, same_ref, kv_s, ka_s, kt_s, acc_s, s0_s, s1_s, dp0_s, dp1_s,
                    qg_s, dq_s, out_s, kv_sem, ka_sem, acc_sem, out_sem, sems):
    @pl.when(group_ref[0] < 3)
    def _():
        tiles = meta_ref[2 * NB]
        own = pltpu.make_async_copy(
            qg_ref.at[pl.ds(FIRST_TILES * TQ, LAST_TILES * TQ), :], qg_s, sems.at[0])
        own.start()
        arrive, ready = fetch_keys(tiles, (kv_ref, kv_s, kv_sem), (ka_ref, ka_s, ka_sem), (kt_ref, kt_s),
                                   (acc2_ref, acc_s, acc_sem), sems.at[1])
        early = [
            pltpu.make_async_copy(dq1_ref, dq_s.at[pl.ds(0, FIRST_TILES * TQ), :], sems.at[2]),
            pltpu.make_async_copy(dq2_ref, dq_s.at[pl.ds(NQ_ENC - REST, REST), :], sems.at[3]),
        ]
        for copy in early:
            copy.start()
        dq_s[pl.ds(NQ_ENC, 8), :] = jnp.zeros((8, LANES), F32)
        own.wait()

        def emit(t, dq_t, total, delta):
            dq_s[pl.ds((FIRST_TILES + t) * TQ, TQ), :] = both_halves(dq_t)

        sweep(LAST_TILES, tiles, (kv_s, ka_s, kt_s, acc_s, (s0_s, s1_s), (dp0_s, dp1_s)),
              lambda t: qg_s[pl.ds(t * TQ, TQ), :], lambda t: no_moments(), emit,
              arrive, ready, lambda kt: None)
        for copy in early:
            copy.wait()
        row = lax.broadcasted_iota(jnp.int32, (TOK, LANES), 0)
        low = lane_low((TOK, LANES))
        copies = []
        for b in range(NB):
            grad = acc_s[pl.ds(pl.multiple_of(meta_ref[b], 16), TOK), :]
            grad = jnp.where(row < meta_ref[NB + b], jnp.where(low, grad * 0.125, grad), 0.0)
            base = QTR * b
            dq = jnp.where(lane_low((24, LANES)), dq_s[pl.ds(base, 24), :], dq_s[pl.ds(base + 21, 24), :])
            out_s[b] = jnp.concatenate([grad, dq], axis=0).astype(BF16)
            if b % 8 == 7:
                some = pl.ds(b - 7, 8)
                copies.append(pltpu.make_async_copy(out_s.at[some], o_ref.at[some], out_sem.at[b // 8]))
                copies[-1].start()
        for copy in copies:
            copy.wait()


def dec_query_pos(t, part):
    q_id = t * TQ + lax.broadcasted_iota(jnp.int32, (1, TQ), 1)
    place = (q_id // DQTR) * DTOK + part * DQTR + q_id % DQTR
    return jnp.where(q_id < DQ, place, -1).astype(F32)


def dec_scores(kv_ref, ka_ref, pos_ref, c, rows, operands, q_at):
    q_t, d_t = operands
    s = jnp.dot(ka_ref[c, rows, :], q_t, preferred_element_type=F32)
    dprob = jnp.dot(kv_ref[c, rows, :], d_t, preferred_element_type=F32)
    k_at = pos_ref[rows, :]
    return jnp.where(jnp.concatenate([k_at, k_at], axis=1) <= q_at, s, NEG), dprob


def put_pos(pos_ref, offset, b):
    row = lax.broadcasted_iota(jnp.int32, (64, LANES), 0)
    pos_ref[pl.ds(pl.multiple_of(offset, 16), 64), :] = (row + b * DTOK).astype(F32)


def dec_units(kt):
    return [
        (pl.ds(pl.multiple_of(kt * TKD + j * SUB, SUB), SUB), t) for j in range(TKD // SUB) for t in range(2)
    ]


def dec_first_kernel(group_ref, part_ref, held_ref, kv_out, ka_out, m0_out, m1_out, m2_out, meta_ref,
                     y_ref, kv_ref, ka_ref, pos_ref, m_ref, qg_s, stat_s, sems, wide_s, lens_s, sem):
    @pl.when(group_ref[0] == 3)
    def _():
        fetch = pltpu.make_async_copy(held_ref, y_ref, sems.at[0])
        fetch.start()
        fetch.wait()
        read_lens(y_ref, wide_s, lens_s, sem)

        end = jnp.int32(0)
        for b in range(NB):
            length = lens_s[7, b]
            meta_ref[b] = end
            meta_ref[NB + b] = length
            chunk = y_ref[b].astype(F32)
            for c in range(3):
                keys = chunk[DIN_ROWS * c : DIN_ROWS * c + 64].astype(BF16)
                place_block(kv_ref.at[c], ka_ref.at[c], keys, end, length)
                qg_s[c, pl.ds(DQTR * b, 16), :] = chunk[DIN_ROWS * c + DTOK : DIN_ROWS * (c + 1)]
            put_pos(pos_ref, end, b)
            end = end + ((length + 15) // 16) * 16
        for c in range(3):
            place_padding(kv_ref.at[c], ka_ref.at[c], end, TKD)
        tiles = (end + TKD - 1) // TKD
        meta_ref[2 * NB] = tiles
        part = part_ref[0]
        stat_s[...] = jnp.zeros_like(stat_s)
        for c in range(3):
            qg_s[c, pl.ds(DQ, REST), :] = jnp.zeros((REST, LANES), F32)
            m_ref[c, pl.ds(0, 2 * TQ), :] = qg_s[c].astype(BF16)

        copies = [
            pltpu.make_async_copy(src, dst, sems.at[1 + i])
            for i, (src, dst) in enumerate(((kv_ref, kv_out), (ka_ref, ka_out)))
        ]
        for copy in copies:
            copy.start()
        for c, out in enumerate((m0_out, m1_out, m2_out)):
            operands = [query_operands(qg_s[c, pl.ds(t * TQ, TQ), :]) for t in range(2)]
            q_at = [dec_query_pos(t, part) for t in range(2)]

            def step(kt, carry):
                carry = list(carry)
                units = dec_units(kt)
                ahead = lambda u: dec_scores(kv_ref, ka_ref, pos_ref, c, units[u][0], operands[units[u][1]], q_at[units[u][1]])
                found = ahead(0)
                for u, (rows, t) in enumerate(units):
                    fresh = ahead(u + 1) if u + 1 < len(units) else None
                    carry[t] = score_sums(found, carry[t])
                    found = fresh
                return tuple(carry)

            found = lax.fori_loop(0, tiles, step, (no_moments(), no_moments()))
            for t in range(2):
                q_id = t * TQ + lax.broadcasted_iota(jnp.int32, (1, TQ), 1)
                for k, value in enumerate(merged(found[t])):
                    write_split(stat_s, 12 * k + 2 * t, jnp.where(q_id < DQ, value, NEG if k == 0 else 0.0))
            m_ref[c, pl.ds(2 * TQ, THERE_ROWS - 2 * TQ), :] = stat_s[...].astype(BF16)
            copies.append(pltpu.make_async_copy(m_ref.at[c], out, sems.at[4 + c]))
            copies[-1].start()
        for copy in copies:
            copy.wait()


def dec_last_kernel(group_ref, part_ref, meta_ref, kv_ref, ka_ref, m0_in, m1_in, m2_in, b0_in, b1_in, b2_in, enc_ref,
                    o_ref, pos_ref, m_ref, back_ref, acc_s, dq_s, out_s, sems, out_sem):
    @pl.when(group_ref[0] == 3)
    def _():
        tiles = meta_ref[2 * NB]
        part = part_ref[0]
        fetches = [
            [
                pltpu.make_async_copy(src, dst.at[c], sems.at[c, i])
                for i, (src, dst) in enumerate(((m_in, m_ref), (b_in, back_ref)))
            ]
            for c, (m_in, b_in) in enumerate(((m0_in, b0_in), (m1_in, b1_in), (m2_in, b2_in)))
        ]
        for some in fetches:
            for copy in some:
                copy.start()

        @pl.loop(0, NB)
        def _(b):
            put_pos(pos_ref, meta_ref[b], b)

        for c in range(3):
            for copy in fetches[c]:
                copy.wait()
            qg = m_ref[c, pl.ds(0, 2 * TQ), :].astype(F32)
            back = back_ref[c].astype(F32)
            stats = back[2 * TQ :]
            cut = [qg[t * TQ : (t + 1) * TQ] for t in range(2)]
            operands = [query_operands(cut[t]) for t in range(2)]
            naturals = [natural_operands(cut[t]) for t in range(2)]
            q_at = [dec_query_pos(t, part) for t in range(2)]
            total = [read_split(stats, 2 * t) for t in range(2)]
            delta = [read_split(stats, 12 + 2 * t) for t in range(2)]

            def step(kt, dqs):
                dqs = list(dqs)
                units = dec_units(kt)
                ahead = lambda u: dec_scores(kv_ref, ka_ref, pos_ref, c, units[u][0], operands[units[u][1]], q_at[units[u][1]])
                found = ahead(0)
                for u, (rows, t) in enumerate(units):
                    fresh = ahead(u + 1) if u + 1 < len(units) else None
                    parts = grad_parts(*found, total[t], delta[t])
                    grad = key_grads(parts, naturals[t])
                    acc_s[rows, :] = grad if t == 0 else acc_s[rows, :] + grad
                    if t == 0:
                        keys = turn(kv_ref[c, rows, :])
                    dqs[t] = dqs[t] + jnp.dot(keys, parts[1], preferred_element_type=F32)
                    found = fresh
                return tuple(dqs)

            none = jnp.zeros((HD, TQ), F32)
            dqs = lax.fori_loop(0, tiles, step, (none, none))
            for t in range(2):
                rows = pl.ds(t * TQ, TQ)
                dq_s[rows, :] = both_halves(dqs[t]) + back[t * TQ : (t + 1) * TQ]
            row = lax.broadcasted_iota(jnp.int32, (DTOK, LANES), 0)
            low = lane_low((DTOK, LANES))
            for b in range(NB):
                grad = acc_s[pl.ds(pl.multiple_of(meta_ref[b], 16), DTOK), :]
                grad = jnp.where(row < meta_ref[NB + b], jnp.where(low, grad * 0.125, grad), 0.0)
                base = DQTR * b
                dq = jnp.where(lane_low((8, LANES)), dq_s[pl.ds(base, 8), :], dq_s[pl.ds(base + 7, 8), :])
                out_s[b, pl.ds(DOUT_ROWS * c, DOUT_ROWS), :] = jnp.concatenate([grad, dq], axis=0).astype(BF16)
                if c == 2 and b % 8 == 7:
                    some = pl.ds(b - 7, 8)
                    pltpu.make_async_copy(out_s.at[some], o_ref.at[some], out_sem.at[b // 8]).start()
        for i in range(NB // 8):
            some = pl.ds(8 * i, 8)
            pltpu.make_async_copy(out_s.at[some], o_ref.at[some], out_sem.at[i]).wait()


SMEM = pl.BlockSpec(memory_space=pltpu.SMEM)
VMEM = pl.BlockSpec(memory_space=pltpu.VMEM)
ANY = pl.BlockSpec(memory_space=pl.ANY)


def limit(mib):
    return pltpu.CompilerParams(vmem_limit_bytes=mib * MIB)


def shaped(shape, dtype):
    return jax.ShapeDtypeStruct(shape, dtype)


def lens_scratch():
    return [
        pltpu.VMEM((8, LANES), jnp.int32),
        pltpu.SMEM((8, LANES), jnp.int32),
        pltpu.SemaphoreType.DMA(()),
    ]


def key_scratch():
    return [
        pltpu.VMEM((NK_ENC + TK, LANES), BF16),
        pltpu.VMEM((NK_ENC + TK, LANES), BF16),
        pltpu.VMEM((NK_ENC // TK, HD, TK), BF16),
    ]


def score_scratch():
    return [pltpu.VMEM((NK_ENC, LANES), F32)] + [pltpu.VMEM((NK_ENC, TQ), F32)] * 4


def dma(*shape):
    return pltpu.SemaphoreType.DMA(shape)


META = shaped((2 * NB + 8,), jnp.int32)
ENC_TILES = NK_ENC // TK


def dec_first(group, part, held):
    keys = [((3, NK_DEC + TKD, LANES), BF16), ((3, NK_DEC + TKD, LANES), BF16)]
    pos = ((NK_DEC + TKD, LANES), F32)
    return pl.pallas_call(
        dec_first_kernel,
        out_shape=[shaped(*k) for k in keys] + [shaped((THERE_ROWS, LANES), BF16)] * 3 + [META],
        in_specs=[SMEM, SMEM, ANY],
        out_specs=[ANY] * 5 + [SMEM],
        scratch_shapes=[pltpu.VMEM(held.shape, BF16)] + [pltpu.VMEM(*k) for k in keys + [pos]] + [
            pltpu.VMEM((3, THERE_ROWS, LANES), BF16),
            pltpu.VMEM((3, 2 * TQ, LANES), F32),
            pltpu.VMEM((THERE_ROWS - 2 * TQ, LANES), F32),
            dma(8),
        ] + lens_scratch(),
        compiler_params=limit(24),
    )(group, part, held)


def enc_first(group, held):
    return pl.pallas_call(
        enc_first_kernel,
        out_shape=[
            shaped((NK_ENC + TK, LANES), BF16),
            shaped((NK_ENC + TK, LANES), BF16),
            shaped((ENC_TILES, HD, TK), BF16),
            shaped((NQ_ENC + 8, LANES), F32),
            shaped((NK_ENC, LANES), F32),
            shaped((FIRST_TILES * TQ, LANES), F32),
            META,
        ],
        in_specs=[SMEM, VMEM],
        out_specs=[ANY] * 6 + [SMEM],
        scratch_shapes=key_scratch() + [
            pltpu.VMEM((NQ_ENC + 8, LANES), F32),
            score_scratch()[0],
            pltpu.VMEM((FIRST_TILES * TQ, LANES), F32),
        ] + score_scratch()[1:] + [dma(ENC_TILES), dma(5)] + lens_scratch(),
        compiler_params=limit(38),
    )(group, held)


def enc_dec(group, meta, keys, acc, messages):
    return pl.pallas_call(
        enc_dec_kernel,
        out_shape=[
            shaped((NK_ENC, LANES), F32),
            shaped((REST, LANES), F32),
            shaped((BACK_ROWS, LANES), BF16),
        ],
        in_specs=[SMEM, SMEM] + [ANY] * 8,
        out_specs=[ANY, VMEM, VMEM],
        scratch_shapes=key_scratch() + score_scratch() + [
            pltpu.VMEM((2 * TQ, LANES), F32),
            pltpu.VMEM((THERE_ROWS, LANES), BF16),
            pltpu.VMEM((BACK_ROWS - 2 * TQ, LANES), F32),
            dma(ENC_TILES), dma(ENC_TILES), dma(ENC_TILES), dma(ENC_TILES), dma(3),
        ],
        input_output_aliases={6: 0},
        compiler_params=limit(38),
    )(group, meta, *keys, acc, *messages)


def enc_last(group, meta, keys, acc, dqs):
    return pl.pallas_call(
        enc_last_kernel,
        out_shape=[shaped((NB, OUT_ROWS, LANES), BF16), shaped(acc.shape, F32)],
        in_specs=[SMEM, SMEM] + [ANY] * 7,
        out_specs=[ANY, ANY],
        scratch_shapes=key_scratch() + score_scratch() + [
            pltpu.VMEM((LAST_TILES * TQ, LANES), F32),
            pltpu.VMEM((NQ_ENC + 8, LANES), F32),
            pltpu.VMEM((NB, OUT_ROWS, LANES), BF16),
            dma(ENC_TILES), dma(ENC_TILES), dma(ENC_TILES), dma(4), dma(4),
        ],
        input_output_aliases={6: 1},
        compiler_params=limit(38),
    )(group, meta, *keys, acc, *dqs)[0]


def dec_last(group, part, meta, keys, messages, back, enc_out):
    return pl.pallas_call(
        dec_last_kernel,
        out_shape=shaped((NB, OUT_ROWS, LANES), BF16),
        in_specs=[SMEM, SMEM, SMEM] + [VMEM] * 2 + [ANY] * 7,
        out_specs=ANY,
        scratch_shapes=[
            pltpu.VMEM((NK_DEC + TKD, LANES), F32),
            pltpu.VMEM((3, THERE_ROWS, LANES), BF16),
            pltpu.VMEM((3, BACK_ROWS, LANES), BF16),
            pltpu.VMEM((NK_DEC + TKD, LANES), F32),
            pltpu.VMEM((2 * TQ, LANES), F32),
            pltpu.VMEM((NB, OUT_ROWS, LANES), BF16),
            dma(3, 2), dma(4),
        ],
        input_output_aliases={11: 0},
        compiler_params=limit(24),
    )(group, part, meta, *keys, *messages, *back, enc_out)


def on_device(queries, key_rows, value_rows, out_grad, enc_lengths, dec_lengths):
    group = lax.axis_index("grp").astype(jnp.int32).reshape(1)
    part = (lax.axis_index("blk") % 4).astype(jnp.int32).reshape(1)
    chunks = pl.pallas_call(
        pack_kernel,
        out_shape=shaped((NB, IN_ROWS, LANES), BF16),
        in_specs=[SMEM, SMEM, SMEM, SMEM, ANY, ANY, ANY, ANY],
        out_specs=ANY,
        scratch_shapes=[pltpu.VMEM((4, TOK, LANES), BF16)] * 4 + [pltpu.VMEM((8, TOK, LANES), F32)] * 2 + [
            pltpu.VMEM((NB, IN_ROWS, LANES), BF16), dma(4, 4), dma(4)],
        compiler_params=limit(62),
    )(group, part, enc_lengths, dec_lengths, queries, key_rows, value_rows, out_grad)
    held = lax.all_to_all(chunks, "blk", 0, 0, tiled=True)

    def partner(c, blk):
        return (blk + 16) % NB if c < 2 else blk

    there = [[(3 * NB + s, c * NB + partner(c, s)) for s in range(NB)] for c in range(3)]
    *dec_keys, m0, m1, m2, dec_meta = dec_first(group, part, held)
    messages = (m0, m1, m2)
    got = [lax.ppermute(messages[c], ("grp", "blk"), there[c]) for c in range(3)]
    *enc_keys, acc1, dq1, enc_meta = enc_first(group, held)
    acc2, dq2, answer = enc_dec(group, enc_meta, enc_keys, acc1, got)
    back = [lax.ppermute(answer, ("grp", "blk"), [(d, s) for s, d in there[c]]) for c in (2, 1, 0)][::-1]
    enc_out = enc_last(group, enc_meta, enc_keys, acc2, (dq1, dq2))
    final = dec_last(group, part, dec_meta, dec_keys, messages, back, enc_out)
    final = lax.all_to_all(final, "blk", 0, 0, tiled=True)
    out = shaped(queries.shape, F32)
    return pl.pallas_call(
        unpack_kernel,
        out_shape=[out, out, out],
        in_specs=[SMEM, VMEM],
        out_specs=[VMEM, VMEM, VMEM],
        scratch_shapes=[pltpu.VMEM((TOK, LANES), F32)] * 3 + [pltpu.VMEM((DTOK, LANES), F32)],
        compiler_params=limit(10),
    )(group, final)


def solution(mesh):
    rows = P("blk", "grp")
    return jax.shard_map(
        on_device,
        mesh=mesh,
        in_specs=(rows, rows, rows, rows, P("blk"), P("blk")),
        out_specs=(rows, rows, rows),
        check_vma=False,
    )
```

```python
import functools

import jax
import jax.numpy as jnp
from jax import lax
from jax.experimental import pallas as pl
from jax.experimental.pallas import tpu as pltpu
from jax.sharding import PartitionSpec as P

HD = 64
LANES = 128
NB = 32
TOK = 168
DTOK = 56
QTR = TOK // 4
DQTR = DTOK // 4
IN_ROWS = 216
DIN_ROWS = 72
OUT_ROWS = 192
DOUT_ROWS = 64
NQ_ENC = NB * QTR
DQ = NB * DQTR
TQ = 256
TK = 2048
SUB = 256
TKD = 768
NK_ENC = -(-(NB * 176) // TK) * TK
NK_DEC = -(-(NB * 64) // TKD) * TKD
REST = 2 * TQ - DQ
FIRST_TILES = 3
LAST_TILES = (NQ_ENC - REST) // TQ - FIRST_TILES
THERE_ROWS = 2 * TQ + 48
BACK_ROWS = 2 * TQ + 32
NEG = -1e30
F32 = jnp.float32
BF16 = jnp.bfloat16
MIB = 1024 * 1024


def flip(head):
    return (head + 4) % 8


def lane_low(shape):
    return lax.broadcasted_iota(jnp.int32, shape, len(shape) - 1) < HD


def pair_up(first, second):
    low = lane_low(first.shape)
    even = jnp.where(low, first, pltpu.roll(second, HD, 1))
    odd = jnp.where(low, pltpu.roll(first, HD, 1), second)
    return even, odd


def pack_kernel(group_ref, part_ref, enc_ref, dec_ref, q_in, k_in, v_in, g_in, x_out,
                q_ref, k_ref, v_ref, g_ref, kv_s, qg_s, x_ref, in_sem, out_sem):
    is_dec = group_ref[0] == 3
    arrays = ((k_in, k_ref), (v_in, v_ref), (q_in, q_ref), (g_in, g_ref))
    fetches = [
        [
            pltpu.make_async_copy(src.at[:, pl.ds(pair * LANES, LANES)], dst.at[pair], in_sem.at[pair, i])
            for i, (src, dst) in enumerate(arrays)
        ]
        for pair in range(4)
    ]
    for some in fetches:
        for copy in some:
            copy.start()
    row = lax.broadcasted_iota(jnp.int32, (8, LANES), 0)
    enc_len, dec_len = enc_ref[0].astype(F32), dec_ref[0].astype(F32)
    tail = jnp.where(row == 6, enc_len, jnp.where(row == 7, dec_len, 0.0))

    def sent(pair):
        some = pl.ds(8 * pair, 8)
        return pltpu.make_async_copy(x_ref.at[some], x_out.at[some], out_sem.at[pair])

    for pair in range(4):
        for copy in fetches[pair]:
            copy.wait()
        even, odd = pair_up(k_ref[pair].astype(F32), v_ref[pair].astype(F32))
        kv_s[2 * pair], kv_s[2 * pair + 1] = even, odd
        even, odd = pair_up(q_ref[pair].astype(F32), g_ref[pair].astype(F32))
        qg_s[2 * pair], qg_s[2 * pair + 1] = even, odd

        @pl.when(jnp.logical_not(is_dec))
        def _():
            for head in (2 * pair, 2 * pair + 1):
                kv = kv_s[head]
                for part in range(4):
                    qg = qg_s[head, pl.ds(part * QTR, QTR), :]
                    x_ref[4 * head + part] = jnp.concatenate([kv, qg, tail[2:]], axis=0).astype(BF16)
            sent(pair).start()

    @pl.when(is_dec)
    def _():
        for head in range(8):
            for part in range(4):
                pieces = []
                for c in range(3):
                    src = flip(head) if c < 2 else head
                    pieces.append(kv_s[src, pl.ds(c, DTOK, stride=3), :])
                    pieces.append(qg_s[src, pl.ds(3 * part * DQTR + c, DQTR, stride=3), :])
                    pieces.append(tail[6:])
                x_ref[4 * head + part] = jnp.concatenate(pieces, axis=0).astype(BF16)
            if head % 2 == 1:
                sent(head // 2).start()

    for pair in range(4):
        sent(pair).wait()


def unpack_kernel(group_ref, w_ref, qo_ref, ko_ref, vo_ref, dq_s, dk_s, dv_s, tmp_s):
    is_dec = group_ref[0] == 3

    @pl.when(jnp.logical_not(is_dec))
    def _():
        for pair in range(4):
            cols = pl.ds(pair * LANES, LANES)
            sums = []
            for head in (2 * pair, 2 * pair + 1):
                total = None
                for part in range(4):
                    chunk = w_ref[4 * head + part].astype(F32)
                    total = chunk[:TOK] if total is None else total + chunk[:TOK]
                    dq = chunk[TOK:]
                    turned = pltpu.roll(dq, HD, 1)
                    first, second = (dq, turned) if head % 2 == 0 else (turned, dq)
                    base = part * QTR
                    if head % 2 == 0:
                        dq_s[pl.ds(base, 21), :] = first[:21]
                        dq_s[pl.ds(base + 21, 21), :] = second[:21]
                    else:
                        low = lane_low((21, LANES))
                        for start, value in ((base, first), (base + 21, second)):
                            old = dq_s[pl.ds(start, 21), :]
                            dq_s[pl.ds(start, 21), :] = jnp.where(low, old, value[:21])
                sums.append(total)
            low = lane_low((TOK, LANES))
            ko_ref[:, cols] = jnp.where(low, sums[0], pltpu.roll(sums[1], HD, 1))
            vo_ref[:, cols] = jnp.where(low, pltpu.roll(sums[0], HD, 1), sums[1])
            qo_ref[:, cols] = dq_s[...]

    @pl.when(is_dec)
    def _():
        for pair in range(4):
            cols = pl.ds(pair * LANES, LANES)
            for c in range(3):
                sums, dqs = [], []
                for head in (2 * pair, 2 * pair + 1):
                    place = flip(head) if c < 2 else head
                    total, pieces = None, []
                    for part in range(4):
                        chunk = w_ref[4 * place + part].astype(F32)[DOUT_ROWS * c : DOUT_ROWS * (c + 1)]
                        kv = chunk[:DTOK]
                        total = kv if total is None else total + kv
                        dq = chunk[DTOK:]
                        turned = pltpu.roll(dq, HD, 1)
                        pieces.append((dq, turned) if head % 2 == 0 else (turned, dq))
                    sums.append(total)
                    dqs.append(pieces)
                low = lane_low((DTOK, LANES))
                rows = pl.ds(c, DTOK, stride=3)
                dk_s[rows, :] = jnp.where(low, sums[0], pltpu.roll(sums[1], HD, 1))
                dv_s[rows, :] = jnp.where(low, pltpu.roll(sums[0], HD, 1), sums[1])
                low = lane_low((8, LANES))
                for part in range(4):
                    for half in range(2):
                        value = jnp.where(low, dqs[0][part][half], dqs[1][part][half])
                        tmp_s[pl.ds(part * DQTR + half * 7, 7), :] = value[:7]
                dq_s[rows, :] = tmp_s[...]
            ko_ref[:, cols] = dk_s[...]
            vo_ref[:, cols] = dv_s[...]
            qo_ref[:, cols] = dq_s[...]


def fold(tile, op):
    parts = [tile[8 * i : 8 * i + 8] for i in range(tile.shape[0] // 8)]
    while len(parts) > 1:
        parts = [op(parts[i], parts[i + 1]) if i + 1 < len(parts) else parts[i] for i in range(0, len(parts), 2)]
    return parts[0]


def spread(stat, rows):
    return jnp.concatenate([stat] * (rows // 8), axis=0)


def tile_rows(kt, size):
    return pl.ds(pl.multiple_of(kt * size, size), size)


def place_block(kv_ref, ka_ref, block, offset, length):
    size = block.shape[0]
    row = lax.broadcasted_iota(jnp.int32, (size, LANES), 0)
    lane = lax.broadcasted_iota(jnp.int32, (size, LANES), 1)
    rows = pl.ds(pl.multiple_of(offset, 16), size)
    kv_ref[rows, :] = block
    bias = jnp.where(row < length, 0.0, NEG)
    ka_ref[rows, :] = jnp.where(lane == HD, bias, block.astype(F32)).astype(BF16)


def place_padding(kv_ref, ka_ref, offset, size):
    lane = lax.broadcasted_iota(jnp.int32, (size, LANES), 1)
    rows = pl.ds(pl.multiple_of(offset, 16), size)
    kv_ref[rows, :] = jnp.zeros((size, LANES), BF16)
    ka_ref[rows, :] = jnp.where(lane == HD, NEG, 0.0).astype(BF16)


def turn(keys):
    return keys.astype(F32).T[:HD].astype(BF16)


def read_lens(y_ref, wide_s, lens_s, sem):
    lane = lax.broadcasted_iota(jnp.int32, (8, LANES), 1)
    found = jnp.zeros((8, LANES), F32)
    for b in range(NB):
        found = jnp.where(lane == b, y_ref[b].astype(F32)[IN_ROWS - 8 :], found)
    wide_s[...] = found.astype(jnp.int32)
    copy = pltpu.make_async_copy(wide_s, lens_s, sem)
    copy.start()
    copy.wait()


def query_operands(qg):
    turned = qg.T
    sub = lax.broadcasted_iota(jnp.int32, (LANES, TQ), 0)
    q_t = jnp.where(sub < HD, turned * 0.125, jnp.where(sub == HD, 1.0, 0.0)).astype(BF16)
    d_t = jnp.where(sub < HD, 0.0, turned).astype(BF16)
    return q_t, d_t


def natural_operands(qg):
    low = lane_low((TQ, LANES))
    return jnp.where(low, qg, 0.0).astype(BF16), jnp.where(low, 0.0, qg).astype(BF16)


def score_sums(found, running):
    s, dprob = found
    peak, norm, inner = running
    new_peak = jnp.maximum(peak, fold(s, jnp.maximum))
    prob = jnp.exp(s - spread(new_peak, s.shape[0]))
    shrink = jnp.exp(peak - new_peak)
    norm = norm * shrink + fold(prob, jnp.add)
    inner = inner * shrink + fold(prob * dprob, jnp.add)
    return new_peak, norm, inner


def merged(running):
    peak8, norm8, inner8 = running
    peak = jnp.max(peak8, axis=0, keepdims=True)
    shrink = jnp.exp(peak8 - peak)
    norm = jnp.sum(norm8 * shrink, axis=0, keepdims=True)
    inner = jnp.sum(inner8 * shrink, axis=0, keepdims=True)
    return peak, norm, inner


def no_moments():
    zero = jnp.zeros((8, TQ), F32)
    return jnp.full((8, TQ), NEG, F32), zero, zero


def grad_parts(s, dprob, total, delta):
    prob = jnp.exp(s - total)
    dscore = (prob * (dprob - delta)).astype(BF16)
    return prob.astype(BF16), dscore


def key_grads(parts, naturals):
    prob, dscore = parts
    q_nat, d_nat = naturals
    return jnp.dot(dscore, q_nat, preferred_element_type=F32) + jnp.dot(
        prob, d_nat, preferred_element_type=F32
    )


def both_halves(dq_t):
    dq_t = dq_t * 0.125
    return jnp.concatenate([dq_t, dq_t], axis=0).T


def write_split(ref, first_row, value):
    for term in range(3):
        low = value.astype(BF16).astype(F32)
        value = value - low
        for half in range(2):
            ref[pl.ds(first_row + 4 * term + half, 1), :] = low[:, half * LANES : (half + 1) * LANES]


def read_split(rows, first_row):
    total = None
    for term in (2, 1, 0):
        at = first_row + 4 * term
        piece = jnp.concatenate([rows[at : at + 1], rows[at + 1 : at + 2]], axis=1)
        total = piece if total is None else total + piece
    return total


def sweep(count, tiles, refs, query, start, emit, arrive, ready, leave):
    kv_ref, ka_ref, kt_ref, acc_ref, s_pair, dp_pair = refs

    def tile_step(kt, slot, now, then, dq_t, running):
        found = None
        for j in range(TK // SUB):
            rows = pl.ds(pl.multiple_of(kt * TK + j * SUB, SUB), SUB)
            fresh = None
            if then is not None:
                q_t, d_t = then
                fresh = (
                    jnp.dot(ka_ref[rows, :], q_t, preferred_element_type=F32),
                    jnp.dot(kv_ref[rows, :], d_t, preferred_element_type=F32),
                )
                s_pair[1 - slot][rows, :], dp_pair[1 - slot][rows, :] = fresh
            if now is not None:
                naturals, total, delta = now
                parts = grad_parts(s_pair[slot][rows, :], dp_pair[slot][rows, :], total, delta)
            if found is not None:
                running = score_sums(found, running)
            if now is not None:
                acc_ref[rows, :] += key_grads(parts, naturals)
                keys = kt_ref[kt, :, j * SUB : (j + 1) * SUB]
                dq_t = dq_t + jnp.dot(keys, parts[1], preferred_element_type=F32)
            found = fresh
        if found is not None:
            running = score_sums(found, running)
        return dq_t, running

    def run(slot, now, then, running):
        def step(kt, carry):
            if now is None:
                arrive(kt)
            carry = tile_step(kt, slot, now, then, *carry)
            if then is None:
                leave(kt)
            return carry

        return lax.fori_loop(0, tiles, step, (jnp.zeros((HD, TQ), F32), running))

    _, running = run(1, None, query_operands(query(0)), start(0))
    ready()
    for t in range(count):
        peak, norm, inner = merged(running)
        total, delta = peak + jnp.log(norm), inner / norm
        now = natural_operands(query(t)), total, delta
        if t == count - 1:
            dq_t, _ = run(t % 2, now, None, no_moments())
        else:
            dq_t, running = run(t % 2, now, query_operands(query(t + 1)), start(t + 1))
        emit(t, dq_t, total, delta)


def tile_copy(src_ref, dst_ref, sem, kt):
    rows = tile_rows(kt, TK)
    return pltpu.make_async_copy(src_ref.at[rows, :], dst_ref.at[rows, :], sem.at[kt])


def enc_first_kernel(group_ref, y_ref, kv_ref, ka_ref, kt_ref, qg_ref, acc_ref, dq_ref, meta_ref,
                     kv_s, ka_s, kt_s, qg_s, acc_s, dq_s, s0_s, s1_s, dp0_s, dp1_s,
                     acc_sem, sems, wide_s, lens_s, sem):
    @pl.when(group_ref[0] < 3)
    def _():
        read_lens(y_ref, wide_s, lens_s, sem)

        def block(b, offset):
            length = lens_s[6, b]
            meta_ref[b] = offset
            meta_ref[NB + b] = length
            place_block(kv_s, ka_s, y_ref[b, 0:176, :], offset, length)
            return offset + ((length + 15) // 16) * 16

        end = lax.fori_loop(0, NB, block, jnp.int32(0))
        place_padding(kv_s, ka_s, end, TK)
        tiles = (end + TK - 1) // TK
        meta_ref[2 * NB] = tiles
        for b in range(NB):
            qg_s[pl.ds(QTR * b, 48), :] = y_ref[b].astype(F32)[TOK:]

        def arrive(kt):
            kt_s[kt] = turn(kv_s[tile_rows(kt, TK), :])
            acc_s[tile_rows(kt, TK), :] = jnp.zeros((TK, LANES), F32)

        copies = [
            pltpu.make_async_copy(src, dst, sems.at[i])
            for i, (src, dst) in enumerate(
                ((kv_s, kv_ref), (ka_s, ka_ref), (qg_s, qg_ref), (kt_s, kt_ref), (dq_s, dq_ref)))
        ]
        for copy in copies[:3]:
            copy.start()

        def emit(t, dq_t, total, delta):
            dq_s[pl.ds(t * TQ, TQ), :] = both_halves(dq_t)

        sweep(FIRST_TILES, tiles, (kv_s, ka_s, kt_s, acc_s, (s0_s, s1_s), (dp0_s, dp1_s)),
              lambda t: qg_s[pl.ds(t * TQ, TQ), :], lambda t: no_moments(), emit,
              arrive, copies[3].start, lambda kt: tile_copy(acc_s, acc_ref, acc_sem, kt).start())
        copies[4].start()
        for copy in copies:
            copy.wait()

        @pl.loop(0, tiles)
        def _(kt):
            tile_copy(acc_s, acc_ref, acc_sem, kt).wait()


def fetch_keys(tiles, kv, ka, kt_all, acc, kt_sem):
    @pl.loop(0, tiles)
    def _(kt):
        tile_copy(*kv, kt).start()
        tile_copy(*ka, kt).start()

    kt_copy = pltpu.make_async_copy(*kt_all, kt_sem)
    kt_copy.start()

    @pl.loop(0, tiles)
    def _(kt):
        tile_copy(*acc, kt).start()

    def arrive(kt):
        tile_copy(*kv, kt).wait()
        tile_copy(*ka, kt).wait()

    def ready():
        kt_copy.wait()

        @pl.loop(0, tiles)
        def _(kt):
            tile_copy(*acc, kt).wait()

    return arrive, ready


def enc_dec_kernel(group_ref, meta_ref, kv_ref, ka_ref, kt_ref, qg_ref, acc1_ref, m0_ref, m1_ref, m2_ref,
                   acc_ref, dq_ref, back_ref, kv_s, ka_s, kt_s, acc_s, s0_s, s1_s, dp0_s, dp1_s,
                   own_s, got_s, stat_s, kv_sem, ka_sem, acc_sem, out_sem, sems):
    group = group_ref[0]

    @pl.when(group < 3)
    def _():
        for c, m_ref in enumerate((m0_ref, m1_ref, m2_ref)):
            @pl.when(group == c)
            def _():
                pltpu.make_async_copy(m_ref, got_s, sems.at[0]).start()

        rest = pltpu.make_async_copy(
            qg_ref.at[pl.ds(NQ_ENC - REST, REST), :], own_s.at[pl.ds(DQ, REST), :], sems.at[1])
        rest.start()
        tiles = meta_ref[2 * NB]
        arrive, ready = fetch_keys(tiles, (kv_ref, kv_s, kv_sem), (ka_ref, ka_s, ka_sem), (kt_ref, kt_s),
                                   (acc1_ref, acc_s, acc_sem), sems.at[2])
        pltpu.make_async_copy(m0_ref, got_s, sems.at[0]).wait()
        got = got_s[...].astype(F32)
        own_s[pl.ds(0, DQ), :] = got[:DQ]
        stats = got[2 * TQ :]
        rest.wait()

        def start(t):
            row = lax.broadcasted_iota(jnp.int32, (8, TQ), 0)
            peak, norm, inner = (read_split(stats, 12 * k + 2 * t) for k in range(3))
            return (jnp.where(row == 0, peak, NEG), jnp.where(row == 0, norm, 0.0),
                    jnp.where(row == 0, inner, 0.0))

        stat_s[...] = jnp.zeros_like(stat_s)

        def emit(t, dq_t, total, delta):
            dq = both_halves(dq_t)
            back_ref[pl.ds(t * TQ, TQ), :] = dq.astype(BF16)
            write_split(stat_s, 2 * t, total)
            write_split(stat_s, 12 + 2 * t, delta)
            if t == 1:
                dq_ref[...] = dq[TQ - REST :]

        sweep(2, tiles, (kv_s, ka_s, kt_s, acc_s, (s0_s, s1_s), (dp0_s, dp1_s)),
              lambda t: own_s[pl.ds(t * TQ, TQ), :], start, emit,
              arrive, ready, lambda kt: tile_copy(acc_s, acc_ref, out_sem, kt).start())
        back_ref[pl.ds(2 * TQ, BACK_ROWS - 2 * TQ), :] = stat_s[...].astype(BF16)

        @pl.loop(0, tiles)
        def _(kt):
            tile_copy(acc_s, acc_ref, out_sem, kt).wait()


def enc_last_kernel(group_ref, meta_ref, kv_ref, ka_ref, kt_ref, qg_ref, acc2_ref, dq1_ref, dq2_ref,
                    o_ref, same_ref, kv_s, ka_s, kt_s, acc_s, s0_s, s1_s, dp0_s, dp1_s,
                    qg_s, dq_s, out_s, kv_sem, ka_sem, acc_sem, out_sem, sems):
    @pl.when(group_ref[0] < 3)
    def _():
        tiles = meta_ref[2 * NB]
        own = pltpu.make_async_copy(
            qg_ref.at[pl.ds(FIRST_TILES * TQ, LAST_TILES * TQ), :], qg_s, sems.at[0])
        own.start()
        arrive, ready = fetch_keys(tiles, (kv_ref, kv_s, kv_sem), (ka_ref, ka_s, ka_sem), (kt_ref, kt_s),
                                   (acc2_ref, acc_s, acc_sem), sems.at[1])
        early = [
            pltpu.make_async_copy(dq1_ref, dq_s.at[pl.ds(0, FIRST_TILES * TQ), :], sems.at[2]),
            pltpu.make_async_copy(dq2_ref, dq_s.at[pl.ds(NQ_ENC - REST, REST), :], sems.at[3]),
        ]
        for copy in early:
            copy.start()
        dq_s[pl.ds(NQ_ENC, 8), :] = jnp.zeros((8, LANES), F32)
        own.wait()

        def emit(t, dq_t, total, delta):
            dq_s[pl.ds((FIRST_TILES + t) * TQ, TQ), :] = both_halves(dq_t)

        sweep(LAST_TILES, tiles, (kv_s, ka_s, kt_s, acc_s, (s0_s, s1_s), (dp0_s, dp1_s)),
              lambda t: qg_s[pl.ds(t * TQ, TQ), :], lambda t: no_moments(), emit,
              arrive, ready, lambda kt: None)
        for copy in early:
            copy.wait()
        row = lax.broadcasted_iota(jnp.int32, (TOK, LANES), 0)
        low = lane_low((TOK, LANES))
        copies = []
        for b in range(NB):
            grad = acc_s[pl.ds(pl.multiple_of(meta_ref[b], 16), TOK), :]
            grad = jnp.where(row < meta_ref[NB + b], jnp.where(low, grad * 0.125, grad), 0.0)
            base = QTR * b
            dq = jnp.where(lane_low((24, LANES)), dq_s[pl.ds(base, 24), :], dq_s[pl.ds(base + 21, 24), :])
            out_s[b] = jnp.concatenate([grad, dq], axis=0).astype(BF16)
            if b % 8 == 7:
                some = pl.ds(b - 7, 8)
                copies.append(pltpu.make_async_copy(out_s.at[some], o_ref.at[some], out_sem.at[b // 8]))
                copies[-1].start()
        for copy in copies:
            copy.wait()


def dec_query_pos(t, part):
    q_id = t * TQ + lax.broadcasted_iota(jnp.int32, (1, TQ), 1)
    place = (q_id // DQTR) * DTOK + part * DQTR + q_id % DQTR
    return jnp.where(q_id < DQ, place, -1).astype(F32)


def dec_scores(kv_ref, ka_ref, pos_ref, c, rows, operands, q_at):
    q_t, d_t = operands
    s = jnp.dot(ka_ref[c, rows, :], q_t, preferred_element_type=F32)
    dprob = jnp.dot(kv_ref[c, rows, :], d_t, preferred_element_type=F32)
    k_at = pos_ref[rows, :]
    return jnp.where(jnp.concatenate([k_at, k_at], axis=1) <= q_at, s, NEG), dprob


def put_pos(pos_ref, offset, b):
    row = lax.broadcasted_iota(jnp.int32, (64, LANES), 0)
    pos_ref[pl.ds(pl.multiple_of(offset, 16), 64), :] = (row + b * DTOK).astype(F32)


def dec_units(kt):
    return [
        (pl.ds(pl.multiple_of(kt * TKD + j * SUB, SUB), SUB), t) for j in range(TKD // SUB) for t in range(2)
    ]


def dec_first_kernel(group_ref, part_ref, held_ref, kv_out, ka_out, m0_out, m1_out, m2_out, meta_ref,
                     y_ref, kv_ref, ka_ref, pos_ref, m_ref, qg_s, stat_s, sems, wide_s, lens_s, sem):
    @pl.when(group_ref[0] == 3)
    def _():
        fetch = pltpu.make_async_copy(held_ref, y_ref, sems.at[0])
        fetch.start()
        fetch.wait()
        read_lens(y_ref, wide_s, lens_s, sem)

        end = jnp.int32(0)
        for b in range(NB):
            length = lens_s[7, b]
            meta_ref[b] = end
            meta_ref[NB + b] = length
            chunk = y_ref[b].astype(F32)
            for c in range(3):
                keys = chunk[DIN_ROWS * c : DIN_ROWS * c + 64].astype(BF16)
                place_block(kv_ref.at[c], ka_ref.at[c], keys, end, length)
                qg_s[c, pl.ds(DQTR * b, 16), :] = chunk[DIN_ROWS * c + DTOK : DIN_ROWS * (c + 1)]
            put_pos(pos_ref, end, b)
            end = end + ((length + 15) // 16) * 16
        for c in range(3):
            place_padding(kv_ref.at[c], ka_ref.at[c], end, TKD)
        tiles = (end + TKD - 1) // TKD
        meta_ref[2 * NB] = tiles
        part = part_ref[0]
        stat_s[...] = jnp.zeros_like(stat_s)
        for c in range(3):
            qg_s[c, pl.ds(DQ, REST), :] = jnp.zeros((REST, LANES), F32)
            m_ref[c, pl.ds(0, 2 * TQ), :] = qg_s[c].astype(BF16)

        copies = [
            pltpu.make_async_copy(src, dst, sems.at[1 + i])
            for i, (src, dst) in enumerate(((kv_ref, kv_out), (ka_ref, ka_out)))
        ]
        for copy in copies:
            copy.start()
        for c, out in enumerate((m0_out, m1_out, m2_out)):
            operands = [query_operands(qg_s[c, pl.ds(t * TQ, TQ), :]) for t in range(2)]
            q_at = [dec_query_pos(t, part) for t in range(2)]

            def step(kt, carry):
                carry = list(carry)
                units = dec_units(kt)
                ahead = lambda u: dec_scores(kv_ref, ka_ref, pos_ref, c, units[u][0], operands[units[u][1]], q_at[units[u][1]])
                found = ahead(0)
                for u, (rows, t) in enumerate(units):
                    fresh = ahead(u + 1) if u + 1 < len(units) else None
                    carry[t] = score_sums(found, carry[t])
                    found = fresh
                return tuple(carry)

            found = lax.fori_loop(0, tiles, step, (no_moments(), no_moments()))
            for t in range(2):
                q_id = t * TQ + lax.broadcasted_iota(jnp.int32, (1, TQ), 1)
                for k, value in enumerate(merged(found[t])):
                    write_split(stat_s, 12 * k + 2 * t, jnp.where(q_id < DQ, value, NEG if k == 0 else 0.0))
            m_ref[c, pl.ds(2 * TQ, THERE_ROWS - 2 * TQ), :] = stat_s[...].astype(BF16)
            copies.append(pltpu.make_async_copy(m_ref.at[c], out, sems.at[4 + c]))
            copies[-1].start()
        for copy in copies:
            copy.wait()


def dec_last_kernel(group_ref, part_ref, meta_ref, kv_ref, ka_ref, m0_in, m1_in, m2_in, b0_in, b1_in, b2_in, enc_ref,
                    o_ref, pos_ref, m_ref, back_ref, acc_s, dq_s, out_s, sems, out_sem):
    @pl.when(group_ref[0] == 3)
    def _():
        tiles = meta_ref[2 * NB]
        part = part_ref[0]
        fetches = [
            [
                pltpu.make_async_copy(src, dst.at[c], sems.at[c, i])
                for i, (src, dst) in enumerate(((m_in, m_ref), (b_in, back_ref)))
            ]
            for c, (m_in, b_in) in enumerate(((m0_in, b0_in), (m1_in, b1_in), (m2_in, b2_in)))
        ]
        for some in fetches:
            for copy in some:
                copy.start()

        @pl.loop(0, NB)
        def _(b):
            put_pos(pos_ref, meta_ref[b], b)

        for c in range(3):
            for copy in fetches[c]:
                copy.wait()
            qg = m_ref[c, pl.ds(0, 2 * TQ), :].astype(F32)
            back = back_ref[c].astype(F32)
            stats = back[2 * TQ :]
            cut = [qg[t * TQ : (t + 1) * TQ] for t in range(2)]
            operands = [query_operands(cut[t]) for t in range(2)]
            naturals = [natural_operands(cut[t]) for t in range(2)]
            q_at = [dec_query_pos(t, part) for t in range(2)]
            total = [read_split(stats, 2 * t) for t in range(2)]
            delta = [read_split(stats, 12 + 2 * t) for t in range(2)]

            def step(kt, dqs):
                dqs = list(dqs)
                units = dec_units(kt)
                ahead = lambda u: dec_scores(kv_ref, ka_ref, pos_ref, c, units[u][0], operands[units[u][1]], q_at[units[u][1]])
                found = ahead(0)
                for u, (rows, t) in enumerate(units):
                    fresh = ahead(u + 1) if u + 1 < len(units) else None
                    parts = grad_parts(*found, total[t], delta[t])
                    grad = key_grads(parts, naturals[t])
                    acc_s[rows, :] = grad if t == 0 else acc_s[rows, :] + grad
                    if t == 0:
                        keys = turn(kv_ref[c, rows, :])
                    dqs[t] = dqs[t] + jnp.dot(keys, parts[1], preferred_element_type=F32)
                    found = fresh
                return tuple(dqs)

            none = jnp.zeros((HD, TQ), F32)
            dqs = lax.fori_loop(0, tiles, step, (none, none))
            for t in range(2):
                rows = pl.ds(t * TQ, TQ)
                dq_s[rows, :] = both_halves(dqs[t]) + back[t * TQ : (t + 1) * TQ]
            row = lax.broadcasted_iota(jnp.int32, (DTOK, LANES), 0)
            low = lane_low((DTOK, LANES))
            for b in range(NB):
                grad = acc_s[pl.ds(pl.multiple_of(meta_ref[b], 16), DTOK), :]
                grad = jnp.where(row < meta_ref[NB + b], jnp.where(low, grad * 0.125, grad), 0.0)
                base = DQTR * b
                dq = jnp.where(lane_low((8, LANES)), dq_s[pl.ds(base, 8), :], dq_s[pl.ds(base + 7, 8), :])
                out_s[b, pl.ds(DOUT_ROWS * c, DOUT_ROWS), :] = jnp.concatenate([grad, dq], axis=0).astype(BF16)
                if c == 2 and b % 8 == 7:
                    some = pl.ds(b - 7, 8)
                    pltpu.make_async_copy(out_s.at[some], o_ref.at[some], out_sem.at[b // 8]).start()
        for i in range(NB // 8):
            some = pl.ds(8 * i, 8)
            pltpu.make_async_copy(out_s.at[some], o_ref.at[some], out_sem.at[i]).wait()


SMEM = pl.BlockSpec(memory_space=pltpu.SMEM)
VMEM = pl.BlockSpec(memory_space=pltpu.VMEM)
ANY = pl.BlockSpec(memory_space=pl.ANY)


def limit(mib):
    return pltpu.CompilerParams(vmem_limit_bytes=mib * MIB)


def shaped(shape, dtype):
    return jax.ShapeDtypeStruct(shape, dtype)


def lens_scratch():
    return [
        pltpu.VMEM((8, LANES), jnp.int32),
        pltpu.SMEM((8, LANES), jnp.int32),
        pltpu.SemaphoreType.DMA(()),
    ]


def key_scratch():
    return [
        pltpu.VMEM((NK_ENC + TK, LANES), BF16),
        pltpu.VMEM((NK_ENC + TK, LANES), BF16),
        pltpu.VMEM((NK_ENC // TK, HD, TK), BF16),
    ]


def score_scratch():
    return [pltpu.VMEM((NK_ENC, LANES), F32)] + [pltpu.VMEM((NK_ENC, TQ), F32)] * 4


def dma(*shape):
    return pltpu.SemaphoreType.DMA(shape)


META = shaped((2 * NB + 8,), jnp.int32)
ENC_TILES = NK_ENC // TK


def dec_first(group, part, held):
    keys = [((3, NK_DEC + TKD, LANES), BF16), ((3, NK_DEC + TKD, LANES), BF16)]
    pos = ((NK_DEC + TKD, LANES), F32)
    return pl.pallas_call(
        dec_first_kernel,
        out_shape=[shaped(*k) for k in keys] + [shaped((THERE_ROWS, LANES), BF16)] * 3 + [META],
        in_specs=[SMEM, SMEM, ANY],
        out_specs=[ANY] * 5 + [SMEM],
        scratch_shapes=[pltpu.VMEM(held.shape, BF16)] + [pltpu.VMEM(*k) for k in keys + [pos]] + [
            pltpu.VMEM((3, THERE_ROWS, LANES), BF16),
            pltpu.VMEM((3, 2 * TQ, LANES), F32),
            pltpu.VMEM((THERE_ROWS - 2 * TQ, LANES), F32),
            dma(8),
        ] + lens_scratch(),
        compiler_params=limit(24),
    )(group, part, held)


def enc_first(group, held):
    return pl.pallas_call(
        enc_first_kernel,
        out_shape=[
            shaped((NK_ENC + TK, LANES), BF16),
            shaped((NK_ENC + TK, LANES), BF16),
            shaped((ENC_TILES, HD, TK), BF16),
            shaped((NQ_ENC + 8, LANES), F32),
            shaped((NK_ENC, LANES), F32),
            shaped((FIRST_TILES * TQ, LANES), F32),
            META,
        ],
        in_specs=[SMEM, VMEM],
        out_specs=[ANY] * 6 + [SMEM],
        scratch_shapes=key_scratch() + [
            pltpu.VMEM((NQ_ENC + 8, LANES), F32),
            score_scratch()[0],
            pltpu.VMEM((FIRST_TILES * TQ, LANES), F32),
        ] + score_scratch()[1:] + [dma(ENC_TILES), dma(5)] + lens_scratch(),
        compiler_params=limit(38),
    )(group, held)


def enc_dec(group, meta, keys, acc, messages):
    return pl.pallas_call(
        enc_dec_kernel,
        out_shape=[
            shaped((NK_ENC, LANES), F32),
            shaped((REST, LANES), F32),
            shaped((BACK_ROWS, LANES), BF16),
        ],
        in_specs=[SMEM, SMEM] + [ANY] * 8,
        out_specs=[ANY, VMEM, VMEM],
        scratch_shapes=key_scratch() + score_scratch() + [
            pltpu.VMEM((2 * TQ, LANES), F32),
            pltpu.VMEM((THERE_ROWS, LANES), BF16),
            pltpu.VMEM((BACK_ROWS - 2 * TQ, LANES), F32),
            dma(ENC_TILES), dma(ENC_TILES), dma(ENC_TILES), dma(ENC_TILES), dma(3),
        ],
        input_output_aliases={6: 0},
        compiler_params=limit(38),
    )(group, meta, *keys, acc, *messages)


def enc_last(group, meta, keys, acc, dqs):
    return pl.pallas_call(
        enc_last_kernel,
        out_shape=[shaped((NB, OUT_ROWS, LANES), BF16), shaped(acc.shape, F32)],
        in_specs=[SMEM, SMEM] + [ANY] * 7,
        out_specs=[ANY, ANY],
        scratch_shapes=key_scratch() + score_scratch() + [
            pltpu.VMEM((LAST_TILES * TQ, LANES), F32),
            pltpu.VMEM((NQ_ENC + 8, LANES), F32),
            pltpu.VMEM((NB, OUT_ROWS, LANES), BF16),
            dma(ENC_TILES), dma(ENC_TILES), dma(ENC_TILES), dma(4), dma(4),
        ],
        input_output_aliases={6: 1},
        compiler_params=limit(38),
    )(group, meta, *keys, acc, *dqs)[0]


def dec_last(group, part, meta, keys, messages, back, enc_out):
    return pl.pallas_call(
        dec_last_kernel,
        out_shape=shaped((NB, OUT_ROWS, LANES), BF16),
        in_specs=[SMEM, SMEM, SMEM] + [VMEM] * 2 + [ANY] * 7,
        out_specs=ANY,
        scratch_shapes=[
            pltpu.VMEM((NK_DEC + TKD, LANES), F32),
            pltpu.VMEM((3, THERE_ROWS, LANES), BF16),
            pltpu.VMEM((3, BACK_ROWS, LANES), BF16),
            pltpu.VMEM((NK_DEC + TKD, LANES), F32),
            pltpu.VMEM((2 * TQ, LANES), F32),
            pltpu.VMEM((NB, OUT_ROWS, LANES), BF16),
            dma(3, 2), dma(4),
        ],
        input_output_aliases={11: 0},
        compiler_params=limit(24),
    )(group, part, meta, *keys, *messages, *back, enc_out)


def on_device(queries, key_rows, value_rows, out_grad, enc_lengths, dec_lengths):
    group = lax.axis_index("grp").astype(jnp.int32).reshape(1)
    part = (lax.axis_index("blk") % 4).astype(jnp.int32).reshape(1)
    chunks = pl.pallas_call(
        pack_kernel,
        out_shape=shaped((NB, IN_ROWS, LANES), BF16),
        in_specs=[SMEM, SMEM, SMEM, SMEM, ANY, ANY, ANY, ANY],
        out_specs=ANY,
        scratch_shapes=[pltpu.VMEM((4, TOK, LANES), BF16)] * 4 + [pltpu.VMEM((8, TOK, LANES), F32)] * 2 + [
            pltpu.VMEM((NB, IN_ROWS, LANES), BF16), dma(4, 4), dma(4)],
        compiler_params=limit(62),
    )(group, part, enc_lengths, dec_lengths, queries, key_rows, value_rows, out_grad)
    held = lax.all_to_all(chunks, "blk", 0, 0, tiled=True)

    def partner(c, blk):
        return (blk + 16) % NB if c < 2 else blk

    there = [[(3 * NB + s, c * NB + partner(c, s)) for s in range(NB)] for c in range(3)]
    *dec_keys, m0, m1, m2, dec_meta = dec_first(group, part, held)
    messages = (m0, m1, m2)
    got = [lax.ppermute(messages[c], ("grp", "blk"), there[c]) for c in range(3)]
    *enc_keys, acc1, dq1, enc_meta = enc_first(group, held)
    acc2, dq2, answer = enc_dec(group, enc_meta, enc_keys, acc1, got)
    back = [lax.ppermute(answer, ("grp", "blk"), [(d, s) for s, d in there[c]]) for c in (2, 1, 0)][::-1]
    enc_out = enc_last(group, enc_meta, enc_keys, acc2, (dq1, dq2))
    final = dec_last(group, part, dec_meta, dec_keys, messages, back, enc_out)
    final = lax.all_to_all(final, "blk", 0, 0, tiled=True)
    out = shaped(queries.shape, F32)
    return pl.pallas_call(
        unpack_kernel,
        out_shape=[out, out, out],
        in_specs=[SMEM, VMEM],
        out_specs=[VMEM, VMEM, VMEM],
        scratch_shapes=[pltpu.VMEM((TOK, LANES), F32)] * 3 + [pltpu.VMEM((DTOK, LANES), F32)],
        compiler_params=limit(10),
    )(group, final)


def solution(mesh):
    rows = P("blk", "grp")
    return jax.shard_map(
        on_device,
        mesh=mesh,
        in_specs=(rows, rows, rows, rows, P("blk"), P("blk")),
        out_specs=(rows, rows, rows),
        check_vma=False,
    )
```
